512 devices in a mesh: section: 128 (over z, y, core), rep: 4 (over x).
Axes of the slice: x: 4, y: 8, z: 8, core: 2. Of those that a mesh axis runs over, the one named last changes fastest.
Arguments:
- node_feats: bfloat16 [32768, 256], P(('section', 'rep')), may hold values from -6 to 6
- weight: bfloat16 [256, 256], replicated, may hold values from -0.375 to 0.375
- node_scale: bfloat16 [32768], P(('section', 'rep')), may hold values from 0.19921875 to 1
- tile_mask: int32 [256, 256], P('section'), may hold values from 0 to 1, as said below
- cotangent: bfloat16 [32768, 256], P(('section', 'rep')), may hold values from -6 to 6
Outputs:
- layer_out: bfloat16 [32768, 256], P(('section', 'rep'))
- grad_feats: bfloat16 [32768, 256], P(('section', 'rep'))
- grad_weight: float32 [256, 256], replicated
The draws below stay inside these ranges and needn't reach their ends.
Inputs may be any that keep to these rules, and one draw needn't show every extreme that they name: tile_mask is symmetric, 0 or 1, with ones on its diagonal and next to it.
All inputs are finite; a program needn't handle non-finite values.
Results may differ from the reference program's by a relative error of at most 0.0067.
Values may be sent and summed in bfloat16 or wider, within the bound.
A program may use at most 64 MiB of HBM per device.

```python
import math
import jax
import jax.numpy as jnp
from jax import lax

F = 256
TILE = 128
NT = 256
NODES = 32768


def draw_tile_mask(key, part):
    key = jax.random.fold_in(key, 7)
    key_row, key_pair, key_hub = jax.random.split(key, 3)
    row_weight = jax.random.randint(key_row, (NT,), 1, 5)
    raw_pairs = jax.random.randint(key_pair, (NT, NT), 0, 64)
    indices = jnp.arange(NT, dtype=jnp.int32)
    upper = indices[:, None] < indices[None, :]
    symmetric = jnp.where(upper, raw_pairs, raw_pairs.T)
    linked = symmetric < row_weight[:, None] * row_weight[None, :]
    banded = jnp.abs(indices[:, None] - indices[None, :]) <= 1
    hub_tile = jax.random.randint(key_hub, (), 0, NT)
    hub_links = (indices[:, None] == hub_tile) | (indices[None, :] == hub_tile)
    return (linked | banded | hub_links).astype(jnp.int32)


def levels(own_key, shape, shards, least, top_value):
    def one(position, parts):
        heights = jax.random.uniform(jax.random.fold_in(jax.random.fold_in(own_key, 6), position), (parts,), jnp.float32, least / len(shards), top_value / len(shards))
        return jnp.repeat(jnp.exp(heights), shape[position] // parts).reshape((-1,) + (1,) * (len(shape) - position - 1))

    gain = one(*shards[0])
    for cut in shards[1:]:
        gain = gain * one(*cut)
    return gain


def centred(rng, dims, spread, most, shards=(), held_as=jnp.bfloat16):
    gain = levels(rng, dims, shards, -0.22, 0.18) if shards else 1.0
    result = jax.random.normal(rng, dims, jnp.float32) * spread * gain
    return jnp.minimum(jnp.maximum(result, -most), most).astype(held_as)


def setup_inputs(seed: int = 0) -> dict:
    streams_of = jax.random.split(jax.random.key(seed), 6)
    node_feats = centred(streams_of[0], (NODES, F), 1.0, 6.0, ((0, 512),))
    weight = centred(streams_of[1], (F, F), F ** -0.5, 0.375)
    node_scale = jnp.clip(jnp.exp(math.log(1.0) - 1.6133518 * jax.random.uniform(streams_of[2], (NODES,), jnp.float32) ** levels(streams_of[2], (NODES,), ((0, 512),), -0.2, 0.2)), 0.19921875, 1.0).astype(jnp.bfloat16)
    tile_mask = draw_tile_mask(jax.random.fold_in(streams_of[5], 71), 0)
    cotangent = centred(streams_of[4], (NODES, F), 1.0, 6.0, ((0, 512),))
    return {"node_feats": node_feats, "weight": weight, "node_scale": node_scale, "tile_mask": tile_mask, "cotangent": cotangent}


def edge_values(row_ids, col_ids):
    product = row_ids[:, None] * col_ids[None, :] % 65521
    hashed = (product * 20011 + (row_ids[:, None] + col_ids[None, :]) * 7919) % 65521
    return hashed.astype(jnp.float32) * (2.0 / 65521.0) - 1.0

def reference(node_feats, weight, node_scale, tile_mask, cotangent):
    coef = 4.0 / math.sqrt(TILE * NT)
    scale = node_scale.astype(jnp.float32)
    projected = (scale[:, None] * jnp.dot(node_feats, weight, preferred_element_type=jnp.float32)).astype(jnp.bfloat16)
    proj_tiles = projected.reshape(NT, TILE, F)
    offsets = jnp.arange(TILE, dtype=jnp.int32)

    def tile_values(row_tile, col_tile):
        row_ids = row_tile * TILE + offsets
        col_ids = col_tile * TILE + offsets
        return (edge_values(row_ids, col_ids) * coef).astype(jnp.bfloat16)

    def row_step(unused, row_tile):

        def col_step(total, col_tile):

            def add_tile(inner):
                return inner + jnp.dot(tile_values(row_tile, col_tile), proj_tiles[col_tile], preferred_element_type=jnp.float32)
            return (lax.cond(tile_mask[row_tile, col_tile] > 0, add_tile, lambda inner: inner, total), None)
        total, unused_out = lax.scan(col_step, jnp.zeros((TILE, F), jnp.float32), jnp.arange(NT, dtype=jnp.int32))
        return (unused, total)
    unused_carry, agg_tiles = lax.scan(row_step, jnp.float32(0.0), jnp.arange(NT, dtype=jnp.int32))
    presum = scale[:, None] * agg_tiles.reshape(NODES, F)
    layer_out = jax.nn.silu(presum).astype(jnp.bfloat16)
    sigma = jax.nn.sigmoid(presum)
    deriv = sigma * (1.0 + presum * (1.0 - sigma))
    error = (scale[:, None] * cotangent.astype(jnp.float32) * deriv).astype(jnp.bfloat16)
    err_tiles = error.reshape(NT, TILE, F)

    def back_row(total, row_tile):

        def back_col(inner_total, col_tile):

            def add_tile(inner):
                term = jnp.dot(tile_values(row_tile, col_tile).T, err_tiles[row_tile], preferred_element_type=jnp.float32)
                return inner.at[col_tile].add(term)
            return (lax.cond(tile_mask[row_tile, col_tile] > 0, add_tile, lambda inner: inner, inner_total), None)
        total, unused_out = lax.scan(back_col, total, jnp.arange(NT, dtype=jnp.int32))
        return (total, None)
    back_tiles, unused_rows = lax.scan(back_row, jnp.zeros((NT, TILE, F), jnp.float32), jnp.arange(NT, dtype=jnp.int32))
    vgrad = (scale[:, None] * back_tiles.reshape(NODES, F)).astype(jnp.bfloat16)
    grad_weight = jnp.dot(node_feats.T, vgrad, preferred_element_type=jnp.float32)
    grad_feats = jnp.dot(vgrad, weight.T, preferred_element_type=jnp.float32).astype(jnp.bfloat16)
    return (layer_out, grad_feats, grad_weight)
```

```python
import functools
import math

import jax
import jax.numpy as jnp
from jax import lax
from jax.experimental import pallas as pl
from jax.experimental.pallas import tpu as pltpu
from jax.sharding import PartitionSpec as P


MESH = pl.DeviceIdType.MESH
NZ, NY, NX = 8, 8, 4
ROWS = 64
HALF = 128
MODULUS = 65521
OFFSET = (0, 1, 7, 2, 6, 3, 5, 4)
SLOT = {off: k for k, off in enumerate(OFFSET)}
GROUPS = ((0, 1), (1, 3), (3, 5), (5, 8))
COPIES = 160
BF16 = jnp.bfloat16
F32 = jnp.float32


def fold(v):
    return (v & 0xFFFF) + 15 * (v >> 16)


def reduce_once(v):
    return jnp.where(v >= MODULUS, v - MODULUS, v)


def add_mod(q, step):
    total = q + step
    return jnp.where(total >= float(MODULUS), total - float(MODULUS), total)


def kernel(
    coef,
    feats, weight, scale_row, mask, cot,
    layer_out, grad_feats, grad_weight,
    adj, cm, gath, masks, csend, crecv, acc, ysend, yrecv,
    part, a1s, a1r, half, a2s, a2r, a3r, a4r, wbuf, scale_col,
    send_sems, recv_sems,
):
    sec = lax.axis_index("section")
    x = lax.axis_index("rep")
    c = sec % 2
    y = (sec // 2) % NY
    z = sec // (2 * NY)
    x_one = x + 1 - 2 * (x % 2)
    x_two = 3 - x
    x_opp = (x + 2) % NX

    def device(zz, yy, cc, xx):
        return ((zz * NY + yy) * 2 + cc, xx)

    sibling = device(z, y, 1 - c, x)
    east, west = device(z, y, c, x_one), device(z, y, c, x_two)

    def z_peer(e):
        return device((z + e) % NZ, y, c, x)

    def y_peer(e):
        return device(z, (y + e) % NY, c, x)

    def x_peer(e):
        return device(z, y, c, (x + e) % NX)

    barrier = pltpu.get_barrier_semaphore()
    peers = [z_peer(e) for e in range(1, NZ)] + [y_peer(e) for e in range(1, NY)]
    peers += [x_peer(e) for e in range(1, NX)] + [sibling]
    for peer in peers:
        pl.semaphore_signal(barrier, inc=1, device_id=peer, device_id_type=MESH)

    started = []

    def copy(src, dst, target):
        number = len(started)
        one = pltpu.make_async_remote_copy(
            src_ref=src, dst_ref=dst, send_sem=send_sems.at[number],
            recv_sem=recv_sems.at[number], device_id=target, device_id_type=MESH,
        )
        one.start()
        started.append(one)
        return one

    row = scale_row[...].astype(F32)
    pick = lax.broadcasted_iota(jnp.int32, (ROWS, ROWS), 0) == lax.broadcasted_iota(
        jnp.int32, (ROWS, ROWS), 1
    )
    column = jnp.sum(jnp.where(pick, jnp.broadcast_to(row, (ROWS, ROWS)), 0.0), axis=1, keepdims=True)
    scale_col[...] = jnp.broadcast_to(column, (ROWS, HALF))
    for f in range(2):
        lanes = slice(f * HALF, (f + 1) * HALF)
        gath[0, f, 0, 0] = (scale_col[...] * feats[:, lanes].astype(F32)).astype(BF16)
    masks[0] = jnp.zeros((8, HALF), F32)
    masks[0, 0:2, :] = mask[:, 0:HALF].astype(F32)
    masks[0, 2:4, :] = mask[:, HALF:].astype(F32)

    pl.semaphore_wait(barrier, len(peers))

    def start_pass(p):
        state = {}
        for f in range(2):
            own = gath.at[p, f, 0, 0]
            zs = {}
            for k in range(1, NZ):
                e = (NZ - OFFSET[k]) % NZ
                zs[k] = copy(own, gath.at[p, f, 0, k], z_peer(e))
            state[f] = {"z": zs, "one": {}, "two": {}, "opp": {}}
            forward(p, f, 0, state)
        return state

    def forward(p, f, g, state):
        lo, hi = GROUPS[g]
        for k in range(lo, hi):
            if k:
                state[f]["z"][k].wait_recv()
        run = pl.ds(lo, hi - lo)
        state[f]["one"][g] = copy(gath.at[p, f, 0, run], gath.at[p, f, 1, run], east)
        state[f]["two"][g] = copy(gath.at[p, f, 0, run], gath.at[p, f, 2, run], west)

    def relay(p, f, g, state):
        lo, hi = GROUPS[g]
        run = pl.ds(lo, hi - lo)
        if f == 0:
            state[f]["two"][g].wait_recv()
            state[f]["opp"][g] = copy(gath.at[p, f, 2, run], gath.at[p, f, 3, run], east)
        else:
            state[f]["one"][g].wait_recv()
            state[f]["opp"][g] = copy(gath.at[p, f, 1, run], gath.at[p, f, 3, run], west)

    def finish_gather(f, state):
        for g in range(len(GROUPS)):
            state[f]["one" if f == 0 else "two"][g].wait_recv()
            state[f]["opp"][g].wait_recv()

    def product(p, f, side):
        right = gath[p, f].reshape(NX * NZ * ROWS, HALF)

        def block(n, _):
            at = pl.multiple_of(n * 256, 256)
            value = jnp.dot(
                adj[pl.ds(side * 512 + at, 256), :], right, preferred_element_type=F32
            )
            if side == 0:
                csend[p, f, pl.ds(at, 256), :] = value.astype(BF16)
            else:
                acc[pl.ds(at, 256), :] = value
            return 0

        lax.fori_loop(0, 2, block, 0)

    def sums_first(p, f, state):
        product(p, f, 0)
        state[f]["core"] = copy(csend.at[p, f], crecv.at[p, f], sibling)

    def sums_second(p, f, state):
        product(p, f, 1)
        state[f]["core"].wait_recv()
        total = acc[...] + crecv[p, f].astype(F32)
        acc[...] = total
        ysend[p, f] = total.astype(BF16)
        state[f]["y"] = {}
        for e in (1, 7, 2, 6, 3, 5, 4):
            at = pl.multiple_of(((y + e) % NY) * ROWS, ROWS)
            state[f]["y"][e] = copy(
                ysend.at[p, f, pl.ds(at, ROWS)], yrecv.at[p, f, e], y_peer(e)
            )
        state[f]["own"] = acc[pl.ds(pl.multiple_of(y * ROWS, ROWS), ROWS), :]

    def sums_last(p, f, state):
        total = state[f]["own"]
        for e in range(1, NY):
            state[f]["y"][e].wait_recv()
            total = total + yrecv[p, f, e].astype(F32)
        return total

    col_j = lax.broadcasted_iota(jnp.int32, (16, 512), 1)
    row_i = lax.broadcasted_iota(jnp.int32, (16, 512), 0)
    col_slot = col_j >> 6
    col_off = jnp.where((col_slot & 1) == 1, (col_slot + 1) >> 1, (8 - (col_slot >> 1)) & 7)
    col_base = ((((z + col_off) & 7) * NY + y) * 2 + c) * 256 + (col_j & 63)

    def side_core(side):
        return 1 - c if side == 0 else c

    def mask_columns():
        which = lax.broadcasted_iota(jnp.int32, (16, HALF), 0)
        lane = lax.broadcasted_iota(jnp.int32, (16, HALF), 1)
        core_of = jnp.where(which < 8, 1 - c, c)
        tile = ((z * NY + (which & 7)) * 2 + core_of) * 2 + x // 2
        every = masks[...].reshape(64, HALF)
        dims = (((1,), (1,)), ((), ()))
        low = lax.dot_general((tile == lane).astype(F32), every, dims, preferred_element_type=F32)
        high = lax.dot_general(
            (tile == lane + HALF).astype(F32), every, dims, preferred_element_type=F32
        )
        entry = lax.broadcasted_iota(jnp.int32, (64, 512), 0)
        slot = lax.broadcasted_iota(jnp.int32, (64, 512), 1) >> 6
        for n, xx in enumerate((x, x_one, x_two, x_opp)):
            same = (entry >> 3) == slot
            pick_low = jnp.where(same & ((entry & 7) == xx // 2), 1.0, 0.0).astype(F32)
            pick_high = jnp.where(same & ((entry & 7) == xx // 2 + 2), 1.0, 0.0).astype(F32)
            chosen = jnp.dot(low, pick_low, preferred_element_type=F32) + jnp.dot(
                high, pick_high, preferred_element_type=F32
            )
            cm[:, n * 512:(n + 1) * 512] = jnp.where(chosen > 0.5, coef, 0.0)

    def make_block(n, side):
        xx = (x, x_one, x_two, x_opp)[n]
        b = col_base + xx * ROWS
        a = ((z * NY) * 2 + side_core(side)) * 256 + x * ROWS + row_i
        first = fold(fold(a * b))
        hashed = reduce_once(fold(fold(first * 20011 + (a + b) * 7919)))
        step = reduce_once(fold(fold(b * 20011 + 7919)))
        step16 = reduce_once(fold(step * 16)).astype(F32)
        step512 = reduce_once(fold(step * 512)).astype(F32)

        def run(yy, q0):
            coefs = cm[pl.ds(side * 8 + yy, 1), n * 512:(n + 1) * 512]
            q = q0
            for s in range(4):
                at = pl.multiple_of(side * 512 + yy * ROWS + s * 16, 16)
                adj[pl.ds(at, 16), n * 512:(n + 1) * 512] = (
                    (q * (2.0 / 65521.0) - 1.0) * coefs
                ).astype(BF16)
                if s < 3:
                    q = add_mod(q, step16)
            return add_mod(q0, step512)

        lax.fori_loop(0, NY, run, hashed.astype(F32))

    state = start_pass(0)
    mask_copies = [
        copy(masks.at[0], masks.at[k], z_peer((NZ - OFFSET[k]) % NZ)) for k in range(1, NZ)
    ]
    forward(0, 0, 1, state)
    forward(0, 1, 1, state)
    relay(0, 0, 0, state)
    relay(0, 1, 0, state)
    for one in mask_copies:
        one.wait_recv()
    mask_columns()
    make_block(0, 0)
    forward(0, 0, 2, state)
    forward(0, 1, 2, state)
    relay(0, 0, 1, state)
    relay(0, 1, 1, state)
    make_block(1, 0)
    make_block(2, 0)
    forward(0, 0, 3, state)
    relay(0, 0, 2, state)
    make_block(3, 0)
    forward(0, 1, 3, state)
    relay(0, 1, 2, state)
    make_block(0, 1)
    make_block(1, 1)
    relay(0, 0, 3, state)
    make_block(2, 1)
    relay(0, 1, 3, state)
    make_block(3, 1)
    finish_gather(0, state)
    sums_first(0, 0, state)
    sums_second(0, 0, state)
    finish_gather(1, state)
    sums_first(0, 1, state)
    sums_second(0, 1, state)
    sums = jnp.concatenate([sums_last(0, 0, state), sums_last(0, 1, state)], axis=1)

    sums_high = sums.astype(BF16)
    sums_low = (sums - sums_high.astype(F32)).astype(BF16)
    scale = jnp.concatenate([scale_col[...], scale_col[...]], axis=1)
    presum = scale * (
        jnp.dot(sums_high, weight[...], preferred_element_type=F32)
        + jnp.dot(sums_low, weight[...], preferred_element_type=F32)
    )
    sigma = jax.nn.sigmoid(presum)
    layer_out[...] = (presum * sigma).astype(BF16)
    deriv = sigma * (1.0 + presum * (1.0 - sigma))
    error = (scale * cot[...].astype(F32) * deriv).astype(BF16)
    gath[1, 0, 0, 0] = error[:, :HALF]
    gath[1, 1, 0, 0] = error[:, HALF:]

    state = start_pass(1)
    part[...] = lax.dot_general(
        sums_high, error, (((0,), (0,)), ((), ())), preferred_element_type=F32
    )
    theirs = pl.multiple_of((1 - c) * 128, 128)
    mine = pl.multiple_of(c * 128, 128)
    a1s[...] = part[pl.ds(theirs, 128), :].astype(BF16)
    first = copy(a1s, a1r, sibling)
    forward(1, 0, 1, state)
    forward(1, 1, 1, state)
    relay(1, 0, 0, state)
    relay(1, 1, 0, state)

    first.wait_recv()
    half[...] = part[pl.ds(mine, 128), :] + a1r[...].astype(F32)
    a2s[...] = half[...].astype(BF16)
    second = []
    for e in range(1, NY):
        at = pl.multiple_of(((y + e) % NY) * 16, 16)
        second.append(copy(a2s.at[pl.ds(at, 16)], a2r.at[e], y_peer(e)))

    forward(1, 0, 2, state)
    forward(1, 1, 2, state)
    relay(1, 0, 1, state)
    relay(1, 1, 1, state)
    forward(1, 0, 3, state)
    relay(1, 0, 2, state)
    forward(1, 1, 3, state)
    relay(1, 1, 2, state)

    piece = half[pl.ds(pl.multiple_of(y * 16, 16), 16), :]
    for e in range(1, NY):
        second[e - 1].wait_recv()
        piece = piece + a2r[e].astype(F32)
    a3r[z] = piece.astype(BF16)
    third = [copy(a3r.at[z], a3r.at[z], z_peer(e)) for e in range(1, NZ)]

    relay(1, 0, 3, state)
    relay(1, 1, 3, state)
    finish_gather(0, state)
    sums_first(1, 0, state)
    sums_second(1, 0, state)

    for one in third:
        one.wait_recv()
    piece = a3r[0].astype(F32)
    for n in range(1, NZ):
        piece = piece + a3r[n].astype(F32)
    a4r[x] = piece
    fourth = [copy(a4r.at[x], a4r.at[x], x_peer(e)) for e in range(1, NX)]

    finish_gather(1, state)
    sums_first(1, 1, state)
    sums_second(1, 1, state)

    for one in fourth:
        one.wait_recv()
    piece = (a4r[0] + a4r[1]) + (a4r[2] + a4r[3])
    at = pl.multiple_of(c * 128 + y * 16, 16)
    wbuf[pl.ds(at, 16), :] = piece
    fifth = [copy(wbuf.at[pl.ds(at, 16)], wbuf.at[pl.ds(at, 16)], y_peer(e)) for e in range(1, NY)]

    back = jnp.concatenate([sums_last(1, 0, state), sums_last(1, 1, state)], axis=1)
    for one in fifth:
        one.wait_recv()
    sixth = copy(wbuf.at[pl.ds(mine, 128)], wbuf.at[pl.ds(mine, 128)], sibling)
    vgrad = (scale * back).astype(BF16)
    grad_feats[...] = lax.dot_general(
        vgrad, weight[...], (((1,), (1,)), ((), ())), preferred_element_type=F32
    ).astype(BF16)
    sixth.wait_recv()
    grad_weight[...] = wbuf[...]
    for one in started:
        one.wait_send()


def local(node_feats, weight, node_scale, tile_mask, cotangent, coef):
    hidden = weight.shape[0]
    vmem = pl.BlockSpec(memory_space=pltpu.VMEM)
    return pl.pallas_call(
        functools.partial(kernel, coef),
        out_shape=(
            jax.ShapeDtypeStruct((ROWS, hidden), BF16),
            jax.ShapeDtypeStruct((ROWS, hidden), BF16),
            jax.ShapeDtypeStruct((hidden, hidden), F32),
        ),
        in_specs=[vmem] * 5,
        out_specs=(vmem, vmem, vmem),
        scratch_shapes=[
            pltpu.VMEM((1024, 2048), BF16),
            pltpu.VMEM((16, 2048), F32),
            pltpu.VMEM((2, 2, NX, NZ, ROWS, HALF), BF16),
            pltpu.VMEM((NZ, 8, HALF), F32),
            pltpu.VMEM((2, 2, 512, HALF), BF16),
            pltpu.VMEM((2, 2, 512, HALF), BF16),
            pltpu.VMEM((512, HALF), F32),
            pltpu.VMEM((2, 2, 512, HALF), BF16),
            pltpu.VMEM((2, 2, NY, ROWS, HALF), BF16),
            pltpu.VMEM((256, 256), F32),
            pltpu.VMEM((128, 256), BF16),
            pltpu.VMEM((128, 256), BF16),
            pltpu.VMEM((128, 256), F32),
            pltpu.VMEM((128, 256), BF16),
            pltpu.VMEM((NY, 16, 256), BF16),
            pltpu.VMEM((NZ, 16, 256), BF16),
            pltpu.VMEM((NX, 16, 256), F32),
            pltpu.VMEM((256, 256), F32),
            pltpu.VMEM((ROWS, HALF), F32),
            pltpu.SemaphoreType.DMA((COPIES,)),
            pltpu.SemaphoreType.DMA((COPIES,)),
        ],
        compiler_params=pltpu.CompilerParams(
            collective_id=0, has_side_effects=True, vmem_limit_bytes=40 * 1024 * 1024
        ),
    )(node_feats, weight, node_scale.reshape(1, ROWS), tile_mask, cotangent)


def solution(mesh):
    in_specs = (
        P(("section", "rep"), None),
        P(),
        P(("section", "rep")),
        P("section", None),
        P(("section", "rep"), None),
    )
    out_specs = (P(("section", "rep"), None), P(("section", "rep"), None), P())
    coef = 4.0 / math.sqrt(128 * 256)
    return jax.shard_map(
        functools.partial(local, coef=coef), mesh=mesh, in_specs=in_specs, out_specs=out_specs,
        check_vma=False,
    )
```

```python
import functools
import math

import jax
import jax.numpy as jnp
from jax import lax
from jax.experimental import pallas as pl
from jax.experimental.pallas import tpu as pltpu
from jax.sharding import PartitionSpec as P


MESH = pl.DeviceIdType.MESH
NZ, NY, NX = 8, 8, 4
ROWS = 64
HALF = 128
MODULUS = 65521
OFFSET = (0, 1, 7, 2, 6, 3, 5, 4)
SLOT = {off: k for k, off in enumerate(OFFSET)}
GROUPS = ((0, 1), (1, 3), (3, 5), (5, 8))
COPIES = 160
BF16 = jnp.bfloat16
F32 = jnp.float32


def fold(v):
    return (v & 0xFFFF) + 15 * (v >> 16)


def reduce_once(v):
    return jnp.where(v >= MODULUS, v - MODULUS, v)


def add_mod(q, step):
    total = q + step
    return jnp.where(total >= float(MODULUS), total - float(MODULUS), total)


def kernel(
    coef,
    feats_hbm, weight_hbm, scale_hbm, mask_hbm, cot_hbm,
    layer_out, grad_feats, grad_weight,
    feats, weight, scale_row, mask, cot, load_sems,
    adj, cm, gath, masks, csend, crecv, acc, ysend, yrecv,
    part, a1s, a1r, half, a2s, a2r, a3r, a4r, wbuf, scale_col,
    send_sems, recv_sems,
):
    sec = lax.axis_index("section")
    x = lax.axis_index("rep")
    c = sec % 2
    y = (sec // 2) % NY
    z = sec // (2 * NY)
    x_one = x + 1 - 2 * (x % 2)
    x_two = 3 - x
    x_opp = (x + 2) % NX

    def device(zz, yy, cc, xx):
        return ((zz * NY + yy) * 2 + cc, xx)

    sibling = device(z, y, 1 - c, x)
    east, west = device(z, y, c, x_one), device(z, y, c, x_two)

    def z_peer(e):
        return device((z + e) % NZ, y, c, x)

    def y_peer(e):
        return device(z, (y + e) % NY, c, x)

    def x_peer(e):
        return device(z, y, c, (x + e) % NX)

    barrier = pltpu.get_barrier_semaphore()
    peers = [z_peer(e) for e in range(1, NZ)] + [y_peer(e) for e in range(1, NY)]
    peers += [x_peer(e) for e in range(1, NX)] + [sibling]
    for peer in peers:
        pl.semaphore_signal(barrier, inc=1, device_id=peer, device_id_type=MESH)

    loads = [
        pltpu.make_async_copy(src, dst, load_sems.at[n])
        for n, (src, dst) in enumerate((
            (feats_hbm, feats), (scale_hbm, scale_row), (mask_hbm, mask),
            (weight_hbm, weight), (cot_hbm, cot),
        ))
    ]
    for one in loads:
        one.start()

    started = []

    def copy(src, dst, target):
        number = len(started)
        one = pltpu.make_async_remote_copy(
            src_ref=src, dst_ref=dst, send_sem=send_sems.at[number],
            recv_sem=recv_sems.at[number], device_id=target, device_id_type=MESH,
        )
        one.start()
        started.append(one)
        return one

    for one in loads[:3]:
        one.wait()
    row = scale_row[...].astype(F32)
    pick = lax.broadcasted_iota(jnp.int32, (ROWS, ROWS), 0) == lax.broadcasted_iota(
        jnp.int32, (ROWS, ROWS), 1
    )
    column = jnp.sum(jnp.where(pick, jnp.broadcast_to(row, (ROWS, ROWS)), 0.0), axis=1, keepdims=True)
    scale_col[...] = jnp.broadcast_to(column, (ROWS, HALF))
    for f in range(2):
        lanes = slice(f * HALF, (f + 1) * HALF)
        gath[0, f, 0, 0] = (scale_col[...] * feats[:, lanes].astype(F32)).astype(BF16)
    masks[0] = jnp.zeros((8, HALF), F32)
    masks[0, 0:2, :] = mask[:, 0:HALF].astype(F32)
    masks[0, 2:4, :] = mask[:, HALF:].astype(F32)

    pl.semaphore_wait(barrier, len(peers))

    def start_pass(p):
        state = {}
        for f in range(2):
            own = gath.at[p, f, 0, 0]
            zs = {}
            for k in range(1, NZ):
                e = (NZ - OFFSET[k]) % NZ
                zs[k] = copy(own, gath.at[p, f, 0, k], z_peer(e))
            state[f] = {"z": zs, "one": {}, "two": {}, "opp": {}}
            forward(p, f, 0, state)
        return state

    def forward(p, f, g, state):
        lo, hi = GROUPS[g]
        for k in range(lo, hi):
            if k:
                state[f]["z"][k].wait_recv()
        run = pl.ds(lo, hi - lo)
        state[f]["one"][g] = copy(gath.at[p, f, 0, run], gath.at[p, f, 1, run], east)
        state[f]["two"][g] = copy(gath.at[p, f, 0, run], gath.at[p, f, 2, run], west)

    def relay(p, f, g, state):
        lo, hi = GROUPS[g]
        run = pl.ds(lo, hi - lo)
        if f == 0:
            state[f]["two"][g].wait_recv()
            state[f]["opp"][g] = copy(gath.at[p, f, 2, run], gath.at[p, f, 3, run], east)
        else:
            state[f]["one"][g].wait_recv()
            state[f]["opp"][g] = copy(gath.at[p, f, 1, run], gath.at[p, f, 3, run], west)

    def finish_gather(f, state):
        for g in range(len(GROUPS)):
            state[f]["one" if f == 0 else "two"][g].wait_recv()
            state[f]["opp"][g].wait_recv()

    def product(p, f, side):
        right = gath[p, f].reshape(NX * NZ * ROWS, HALF)

        value = jnp.dot(adj[side * 512:(side + 1) * 512, :], right, preferred_element_type=F32)
        if side == 0:
            csend[p, f] = value.astype(BF16)
        else:
            acc[f] = value

    def sums_first(p, f, state):
        product(p, f, 0)
        state[f]["core"] = copy(csend.at[p, f], crecv.at[p, f], sibling)

    def sums_second(p, f, state):
        state[f]["core"].wait_recv()
        total = acc[f] + crecv[p, f].astype(F32)
        acc[f] = total
        ysend[p, f] = total.astype(BF16)
        state[f]["y"] = {}
        for e in (1, 7, 2, 6, 3, 5, 4):
            at = pl.multiple_of(((y + e) % NY) * ROWS, ROWS)
            state[f]["y"][e] = copy(
                ysend.at[p, f, pl.ds(at, ROWS)], yrecv.at[p, f, e], y_peer(e)
            )
        state[f]["own"] = acc[f, pl.ds(pl.multiple_of(y * ROWS, ROWS), ROWS), :]

    def sums_last(p, f, state):
        total = state[f]["own"]
        for e in range(1, NY):
            state[f]["y"][e].wait_recv()
            total = total + yrecv[p, f, e].astype(F32)
        return total

    col_j = lax.broadcasted_iota(jnp.int32, (16, 512), 1)
    row_i = lax.broadcasted_iota(jnp.int32, (16, 512), 0)
    col_slot = col_j >> 6
    col_off = jnp.where((col_slot & 1) == 1, (col_slot + 1) >> 1, (8 - (col_slot >> 1)) & 7)
    col_base = ((((z + col_off) & 7) * NY + y) * 2 + c) * 256 + (col_j & 63)

    def side_core(side):
        return 1 - c if side == 0 else c

    def mask_columns():
        which = lax.broadcasted_iota(jnp.int32, (16, HALF), 0)
        lane = lax.broadcasted_iota(jnp.int32, (16, HALF), 1)
        core_of = jnp.where(which < 8, 1 - c, c)
        tile = ((z * NY + (which & 7)) * 2 + core_of) * 2 + x // 2
        every = masks[...].reshape(64, HALF)
        dims = (((1,), (1,)), ((), ()))
        low = lax.dot_general((tile == lane).astype(F32), every, dims, preferred_element_type=F32)
        high = lax.dot_general(
            (tile == lane + HALF).astype(F32), every, dims, preferred_element_type=F32
        )
        entry = lax.broadcasted_iota(jnp.int32, (64, 512), 0)
        slot = lax.broadcasted_iota(jnp.int32, (64, 512), 1) >> 6
        for n, xx in enumerate((x, x_one, x_two, x_opp)):
            same = (entry >> 3) == slot
            pick_low = jnp.where(same & ((entry & 7) == xx // 2), 1.0, 0.0).astype(F32)
            pick_high = jnp.where(same & ((entry & 7) == xx // 2 + 2), 1.0, 0.0).astype(F32)
            chosen = jnp.dot(low, pick_low, preferred_element_type=F32) + jnp.dot(
                high, pick_high, preferred_element_type=F32
            )
            cm[:, n * 512:(n + 1) * 512] = jnp.where(chosen > 0.5, coef, 0.0)

    def make_block(n, side):
        xx = (x, x_one, x_two, x_opp)[n]
        b = col_base + xx * ROWS
        a = ((z * NY) * 2 + side_core(side)) * 256 + x * ROWS + row_i
        first = fold(fold(a * b))
        hashed = reduce_once(fold(fold(first * 20011 + (a + b) * 7919)))
        step = reduce_once(fold(fold(b * 20011 + 7919)))
        step16 = reduce_once(fold(step * 16)).astype(F32)
        step512 = reduce_once(fold(step * 512)).astype(F32)

        def run(yy, q0):
            coefs = cm[pl.ds(side * 8 + yy, 1), n * 512:(n + 1) * 512]
            q = q0
            for s in range(4):
                at = pl.multiple_of(side * 512 + yy * ROWS + s * 16, 16)
                adj[pl.ds(at, 16), n * 512:(n + 1) * 512] = (
                    (q * (2.0 / 65521.0) - 1.0) * coefs
                ).astype(BF16)
                if s < 3:
                    q = add_mod(q, step16)
            return add_mod(q0, step512)

        lax.fori_loop(0, NY, run, hashed.astype(F32))

    state = start_pass(0)
    mask_copies = [
        copy(masks.at[0], masks.at[k], z_peer((NZ - OFFSET[k]) % NZ)) for k in range(1, NZ)
    ]
    forward(0, 0, 1, state)
    forward(0, 1, 1, state)
    relay(0, 0, 0, state)
    relay(0, 1, 0, state)
    for one in mask_copies:
        one.wait_recv()
    mask_columns()
    make_block(0, 0)
    forward(0, 0, 2, state)
    forward(0, 1, 2, state)
    relay(0, 0, 1, state)
    relay(0, 1, 1, state)
    make_block(1, 0)
    make_block(2, 0)
    forward(0, 0, 3, state)
    relay(0, 0, 2, state)
    make_block(3, 0)
    forward(0, 1, 3, state)
    relay(0, 1, 2, state)
    make_block(0, 1)
    make_block(1, 1)
    relay(0, 0, 3, state)
    make_block(2, 1)
    make_block(3, 1)
    relay(0, 1, 3, state)
    finish_gather(0, state)
    sums_first(0, 0, state)
    product(0, 0, 1)
    finish_gather(1, state)
    sums_first(0, 1, state)
    sums_second(0, 0, state)
    product(0, 1, 1)
    sums_second(0, 1, state)
    sums = jnp.concatenate([sums_last(0, 0, state), sums_last(0, 1, state)], axis=1)

    for one in loads[3:]:
        one.wait()
    sums_high = sums.astype(BF16)
    sums_low = (sums - sums_high.astype(F32)).astype(BF16)
    scale = jnp.concatenate([scale_col[...], scale_col[...]], axis=1)
    presum = scale * (
        jnp.dot(sums_high, weight[...], preferred_element_type=F32)
        + jnp.dot(sums_low, weight[...], preferred_element_type=F32)
    )
    sigma = jax.nn.sigmoid(presum)
    layer_out[...] = (presum * sigma).astype(BF16)
    deriv = sigma * (1.0 + presum * (1.0 - sigma))
    error = (scale * cot[...].astype(F32) * deriv).astype(BF16)
    gath[1, 0, 0, 0] = error[:, :HALF]
    gath[1, 1, 0, 0] = error[:, HALF:]

    state = start_pass(1)
    part[...] = lax.dot_general(
        sums_high, error, (((0,), (0,)), ((), ())), preferred_element_type=F32
    )
    theirs = pl.multiple_of((1 - c) * 128, 128)
    mine = pl.multiple_of(c * 128, 128)
    a1s[...] = part[pl.ds(theirs, 128), :].astype(BF16)
    first = copy(a1s, a1r, sibling)
    forward(1, 0, 1, state)
    relay(1, 0, 0, state)

    first.wait_recv()
    half[...] = part[pl.ds(mine, 128), :] + a1r[...].astype(F32)
    a2s[...] = half[...].astype(BF16)
    second = []
    for e in range(1, NY):
        at = pl.multiple_of(((y + e) % NY) * 16, 16)
        second.append(copy(a2s.at[pl.ds(at, 16)], a2r.at[e], y_peer(e)))

    forward(1, 1, 1, state)
    relay(1, 1, 0, state)
    forward(1, 0, 2, state)
    relay(1, 0, 1, state)
    forward(1, 0, 3, state)
    relay(1, 0, 2, state)

    piece = half[pl.ds(pl.multiple_of(y * 16, 16), 16), :]
    for e in range(1, NY):
        second[e - 1].wait_recv()
        piece = piece + a2r[e].astype(F32)
    a3r[z] = piece.astype(BF16)
    third = [copy(a3r.at[z], a3r.at[z], z_peer(e)) for e in range(1, NZ)]

    forward(1, 1, 2, state)
    relay(1, 1, 1, state)
    relay(1, 0, 3, state)
    forward(1, 1, 3, state)
    relay(1, 1, 2, state)
    finish_gather(0, state)
    sums_first(1, 0, state)
    relay(1, 1, 3, state)

    for one in third:
        one.wait_recv()
    piece = a3r[0].astype(F32)
    for n in range(1, NZ):
        piece = piece + a3r[n].astype(F32)
    a4r[x] = piece
    fourth = [copy(a4r.at[x], a4r.at[x], x_peer(e)) for e in range(1, NX)]

    product(1, 0, 1)
    finish_gather(1, state)
    sums_first(1, 1, state)
    sums_second(1, 0, state)

    for one in fourth:
        one.wait_recv()
    piece = (a4r[0] + a4r[1]) + (a4r[2] + a4r[3])
    at = pl.multiple_of(c * 128 + y * 16, 16)
    wbuf[pl.ds(at, 16), :] = piece
    fifth = [copy(wbuf.at[pl.ds(at, 16)], wbuf.at[pl.ds(at, 16)], y_peer(e)) for e in range(1, NY)]

    product(1, 1, 1)
    sums_second(1, 1, state)
    for one in fifth:
        one.wait_recv()
    sixth = copy(wbuf.at[pl.ds(mine, 128)], wbuf.at[pl.ds(mine, 128)], sibling)

    back = jnp.concatenate([sums_last(1, 0, state), sums_last(1, 1, state)], axis=1)
    vgrad = (scale * back).astype(BF16)
    grad_feats[...] = lax.dot_general(
        vgrad, weight[...], (((1,), (1,)), ((), ())), preferred_element_type=F32
    ).astype(BF16)
    sixth.wait_recv()
    grad_weight[...] = wbuf[...]
    for one in started:
        one.wait_send()


def local(node_feats, weight, node_scale, tile_mask, cotangent, coef):
    hidden = weight.shape[0]
    vmem = pl.BlockSpec(memory_space=pltpu.VMEM)
    return pl.pallas_call(
        functools.partial(kernel, coef),
        out_shape=(
            jax.ShapeDtypeStruct((ROWS, hidden), BF16),
            jax.ShapeDtypeStruct((ROWS, hidden), BF16),
            jax.ShapeDtypeStruct((hidden, hidden), F32),
        ),
        in_specs=[pl.BlockSpec(memory_space=pltpu.HBM)] * 5,
        out_specs=(vmem, vmem, vmem),
        scratch_shapes=[
            pltpu.VMEM((ROWS, hidden), BF16),
            pltpu.VMEM((hidden, hidden), BF16),
            pltpu.VMEM((1, ROWS), BF16),
            pltpu.VMEM(tile_mask.shape, jnp.int32),
            pltpu.VMEM((ROWS, hidden), BF16),
            pltpu.SemaphoreType.DMA((5,)),
            pltpu.VMEM((1024, 2048), BF16),
            pltpu.VMEM((16, 2048), F32),
            pltpu.VMEM((2, 2, NX, NZ, ROWS, HALF), BF16),
            pltpu.VMEM((NZ, 8, HALF), F32),
            pltpu.VMEM((2, 2, 512, HALF), BF16),
            pltpu.VMEM((2, 2, 512, HALF), BF16),
            pltpu.VMEM((2, 512, HALF), F32),
            pltpu.VMEM((2, 2, 512, HALF), BF16),
            pltpu.VMEM((2, 2, NY, ROWS, HALF), BF16),
            pltpu.VMEM((256, 256), F32),
            pltpu.VMEM((128, 256), BF16),
            pltpu.VMEM((128, 256), BF16),
            pltpu.VMEM((128, 256), F32),
            pltpu.VMEM((128, 256), BF16),
            pltpu.VMEM((NY, 16, 256), BF16),
            pltpu.VMEM((NZ, 16, 256), BF16),
            pltpu.VMEM((NX, 16, 256), F32),
            pltpu.VMEM((256, 256), F32),
            pltpu.VMEM((ROWS, HALF), F32),
            pltpu.SemaphoreType.DMA((COPIES,)),
            pltpu.SemaphoreType.DMA((COPIES,)),
        ],
        compiler_params=pltpu.CompilerParams(
            collective_id=0, has_side_effects=True, vmem_limit_bytes=56 * 1024 * 1024
        ),
    )(node_feats, weight, node_scale.reshape(1, ROWS), tile_mask, cotangent)


def solution(mesh):
    in_specs = (
        P(("section", "rep"), None),
        P(),
        P(("section", "rep")),
        P("section", None),
        P(("section", "rep"), None),
    )
    out_specs = (P(("section", "rep"), None), P(("section", "rep"), None), P())
    coef = 4.0 / math.sqrt(128 * 256)
    return jax.shard_map(
        functools.partial(local, coef=coef), mesh=mesh, in_specs=in_specs, out_specs=out_specs,
        check_vma=False,
    )
```

```python
import functools
import math

import jax
import jax.numpy as jnp
from jax import lax
from jax.experimental import pallas as pl
from jax.experimental.pallas import tpu as pltpu
from jax.sharding import PartitionSpec as P


MESH = pl.DeviceIdType.MESH
NZ, NY, NX = 8, 8, 4
ROWS = 64
HALF = 128
MODULUS = 65521
OFFSET = (0, 1, 7, 2, 6, 3, 5, 4)
SLOT = {off: k for k, off in enumerate(OFFSET)}
GROUPS = ((0, 1), (1, 3), (3, 5), (5, 8))
COPIES = 100
BF16 = jnp.bfloat16
F32 = jnp.float32


def fold(v):
    return (v & 0xFFFF) + 15 * (v >> 16)


def reduce_once(v):
    return jnp.where(v >= MODULUS, v - MODULUS, v)


def add_mod(q, step):
    total = q + step
    return jnp.where(total >= float(MODULUS), total - float(MODULUS), total)


def kernel(
    coef,
    feats_hbm, weight_hbm, scale_hbm, mask_hbm, cot_hbm,
    layer_out_hbm, grad_feats_hbm, grad_weight_hbm,
    feats, weight, scale_row, mask, cot, load_sems, layer_out, grad_feats, store_sems,
    adj, cm, gath, masks, csend, crecv, acc, ysend, yrecv,
    part, a1s, a1r, half, a2s, a2r, a3r, a4r, wbuf, scale_col,
    send_sems, recv_sems,
):
    sec = lax.axis_index("section")
    x = lax.axis_index("rep")
    c = sec % 2
    y = (sec // 2) % NY
    z = sec // (2 * NY)
    x_one = x + 1 - 2 * (x % 2)
    x_two = 3 - x
    x_opp = (x + 2) % NX

    def device(zz, yy, cc, xx):
        return ((zz * NY + yy) * 2 + cc, xx)

    sibling = device(z, y, 1 - c, x)
    east, west = device(z, y, c, x_one), device(z, y, c, x_two)

    def z_peer(e):
        return device((z + e) % NZ, y, c, x)

    def y_peer(e):
        return device(z, (y + e) % NY, c, x)

    def x_peer(e):
        return device(z, y, c, (x + e) % NX)

    barrier = pltpu.get_barrier_semaphore()
    peers = [z_peer(e) for e in range(1, NZ)] + [y_peer(e) for e in range(1, NY)]
    peers += [x_peer(e) for e in range(1, NX)] + [sibling]
    for peer in peers:
        pl.semaphore_signal(barrier, inc=1, device_id=peer, device_id_type=MESH)

    loads = [
        pltpu.make_async_copy(src, dst, load_sems.at[n])
        for n, (src, dst) in enumerate((
            (feats_hbm, feats), (scale_hbm, scale_row), (mask_hbm, mask),
            (weight_hbm, weight), (cot_hbm, cot),
        ))
    ]
    for one in loads:
        one.start()

    started = []

    def copy(src, dst, target):
        number = len(started)
        one = pltpu.make_async_remote_copy(
            src_ref=src, dst_ref=dst, send_sem=send_sems.at[number],
            recv_sem=recv_sems.at[number], device_id=target, device_id_type=MESH,
        )
        one.start()
        started.append(one)
        return one

    for one in loads[:3]:
        one.wait()
    row = scale_row[...].astype(F32)
    pick = lax.broadcasted_iota(jnp.int32, (ROWS, ROWS), 0) == lax.broadcasted_iota(
        jnp.int32, (ROWS, ROWS), 1
    )
    column = jnp.sum(jnp.where(pick, jnp.broadcast_to(row, (ROWS, ROWS)), 0.0), axis=1, keepdims=True)
    scale_col[...] = jnp.broadcast_to(column, (ROWS, 256))
    gath[0, 0, 0:ROWS] = (scale_col[...] * feats[...].astype(F32)).astype(BF16)
    masks[0] = jnp.zeros((8, HALF), F32)
    masks[0, 0:2, :] = mask[:, 0:HALF].astype(F32)
    masks[0, 2:4, :] = mask[:, HALF:].astype(F32)

    pl.semaphore_wait(barrier, len(peers))

    def start_pass(p):
        own = gath.at[p, 0, pl.ds(0, ROWS)]
        state = {"z": {}, "one": {}, "two": {}, "opp": []}
        for k in range(1, NZ):
            e = (NZ - OFFSET[k]) % NZ
            state["z"][k] = copy(own, gath.at[p, 0, pl.ds(k * ROWS, ROWS)], z_peer(e))
            if k == 2:
                forward(p, 0, state)
        return state

    def forward(p, g, state):
        lo, hi = GROUPS[g]
        for k in range(lo, hi):
            if k:
                state["z"][k].wait_recv()
        run = pl.ds(lo * ROWS, (hi - lo) * ROWS)
        state["one"][g] = copy(gath.at[p, 0, run], gath.at[p, 1, run], east)
        state["two"][g] = copy(gath.at[p, 0, run], gath.at[p, 2, run], west)

    def relay(p, g, state):
        lo, hi = GROUPS[g]
        size = (hi - lo) * ROWS // 2
        run = pl.ds(lo * ROWS, size)
        state["two"][g].wait_recv()
        state["opp"].append(copy(gath.at[p, 2, run], gath.at[p, 3, run], east))
        run = pl.ds(lo * ROWS + size, size)
        state["one"][g].wait_recv()
        state["opp"].append(copy(gath.at[p, 1, run], gath.at[p, 3, run], west))

    def finish_gather(state):
        for one in state["opp"]:
            one.wait_recv()

    def product(p, side):
        right = gath[p].reshape(NX * NZ * ROWS, 256)
        value = jnp.dot(adj[side * 512:(side + 1) * 512, :], right, preferred_element_type=F32)
        if side == 0:
            csend[p] = value.astype(BF16)
        else:
            acc[...] = value

    def sums_first(p, state):
        product(p, 0)
        state["core"] = copy(csend.at[p], crecv.at[p], sibling)

    def sums_second(p, state):
        state["core"].wait_recv()
        total = acc[...] + crecv[p].astype(F32)
        acc[...] = total
        ysend[p] = total.astype(BF16)
        state["y"] = {}
        for e in (4, 3, 5, 2, 6, 1, 7):
            at = pl.multiple_of(((y + e) % NY) * ROWS, ROWS)
            state["y"][e] = copy(ysend.at[p, pl.ds(at, ROWS)], yrecv.at[p, e], y_peer(e))

    def sums_last(p, state):
        total = acc[pl.ds(pl.multiple_of(y * ROWS, ROWS), ROWS), :]
        for e in (1, 7, 2, 6, 3, 5, 4):
            state["y"][e].wait_recv()
            total = total + yrecv[p, e].astype(F32)
        return total

    col_j = lax.broadcasted_iota(jnp.int32, (16, 512), 1)
    row_i = lax.broadcasted_iota(jnp.int32, (16, 512), 0)
    col_slot = col_j >> 6
    col_off = jnp.where((col_slot & 1) == 1, (col_slot + 1) >> 1, (8 - (col_slot >> 1)) & 7)
    col_base = ((((z + col_off) & 7) * NY + y) * 2 + c) * 256 + (col_j & 63)

    def side_core(side):
        return 1 - c if side == 0 else c

    def mask_columns():
        which = lax.broadcasted_iota(jnp.int32, (16, HALF), 0)
        lane = lax.broadcasted_iota(jnp.int32, (16, HALF), 1)
        core_of = jnp.where(which < 8, 1 - c, c)
        tile = ((z * NY + (which & 7)) * 2 + core_of) * 2 + x // 2
        every = masks[...].reshape(64, HALF)
        dims = (((1,), (1,)), ((), ()))
        low = lax.dot_general((tile == lane).astype(F32), every, dims, preferred_element_type=F32)
        high = lax.dot_general(
            (tile == lane + HALF).astype(F32), every, dims, preferred_element_type=F32
        )
        entry = lax.broadcasted_iota(jnp.int32, (64, 512), 0)
        slot = lax.broadcasted_iota(jnp.int32, (64, 512), 1) >> 6
        for n, xx in enumerate((x, x_one, x_two, x_opp)):
            same = (entry >> 3) == slot
            pick_low = jnp.where(same & ((entry & 7) == xx // 2), 1.0, 0.0).astype(F32)
            pick_high = jnp.where(same & ((entry & 7) == xx // 2 + 2), 1.0, 0.0).astype(F32)
            chosen = jnp.dot(low, pick_low, preferred_element_type=F32) + jnp.dot(
                high, pick_high, preferred_element_type=F32
            )
            cm[:, n * 512:(n + 1) * 512] = jnp.where(chosen > 0.5, coef, 0.0)

    def make_block(n, side):
        xx = (x, x_one, x_two, x_opp)[n]
        b = col_base + xx * ROWS
        a = ((z * NY) * 2 + side_core(side)) * 256 + x * ROWS + row_i
        first = fold(fold(a * b))
        hashed = reduce_once(fold(fold(first * 20011 + (a + b) * 7919)))
        step = reduce_once(fold(fold(b * 20011 + 7919)))
        step16 = reduce_once(fold(step * 16)).astype(F32)
        step512 = reduce_once(fold(step * 512)).astype(F32)

        def run(yy, q0):
            coefs = cm[pl.ds(side * 8 + yy, 1), n * 512:(n + 1) * 512]
            q = q0
            for s in range(4):
                at = pl.multiple_of(side * 512 + yy * ROWS + s * 16, 16)
                adj[pl.ds(at, 16), n * 512:(n + 1) * 512] = (
                    (q * (2.0 / 65521.0) - 1.0) * coefs
                ).astype(BF16)
                if s < 3:
                    q = add_mod(q, step16)
            return add_mod(q0, step512)

        lax.fori_loop(0, NY, run, hashed.astype(F32))

    state = start_pass(0)
    mask_copies = [
        copy(masks.at[0], masks.at[k], z_peer((NZ - OFFSET[k]) % NZ)) for k in range(1, NZ)
    ]
    forward(0, 1, state)
    relay(0, 0, state)
    for one in mask_copies:
        one.wait_recv()
    mask_columns()
    make_block(0, 0)
    forward(0, 2, state)
    relay(0, 1, state)
    make_block(1, 0)
    make_block(2, 0)
    forward(0, 3, state)
    relay(0, 2, state)
    make_block(3, 0)
    make_block(0, 1)
    make_block(1, 1)
    relay(0, 3, state)
    make_block(2, 1)
    make_block(3, 1)
    finish_gather(state)
    sums_first(0, state)
    product(0, 1)
    sums_second(0, state)
    sums = sums_last(0, state)

    for one in loads[3:]:
        one.wait()
    sums_high = sums.astype(BF16)
    sums_low = (sums - sums_high.astype(F32)).astype(BF16)
    scale = scale_col[...]
    presum = scale * (
        jnp.dot(sums_high, weight[...], preferred_element_type=F32)
        + jnp.dot(sums_low, weight[...], preferred_element_type=F32)
    )
    sigma = jax.nn.sigmoid(presum)
    layer_out[...] = (presum * sigma).astype(BF16)
    stores = [pltpu.make_async_copy(layer_out, layer_out_hbm, store_sems.at[0])]
    stores[0].start()
    deriv = sigma * (1.0 + presum * (1.0 - sigma))
    error = (scale * cot[...].astype(F32) * deriv).astype(BF16)
    gath[1, 0, 0:ROWS] = error

    state = start_pass(1)
    part[...] = lax.dot_general(
        sums_high, error, (((0,), (0,)), ((), ())), preferred_element_type=F32
    )
    theirs = pl.multiple_of((1 - c) * 128, 128)
    mine = pl.multiple_of(c * 128, 128)
    a1s[...] = part[pl.ds(theirs, 128), :].astype(BF16)
    first = copy(a1s, a1r, sibling)
    forward(1, 1, state)
    relay(1, 0, state)

    first.wait_recv()
    half[...] = part[pl.ds(mine, 128), :] + a1r[...].astype(F32)
    a2s[...] = half[...].astype(BF16)
    second = []
    for e in range(1, NY):
        at = pl.multiple_of(((y + e) % NY) * 16, 16)
        second.append(copy(a2s.at[pl.ds(at, 16)], a2r.at[e], y_peer(e)))

    forward(1, 2, state)
    relay(1, 1, state)
    forward(1, 3, state)
    relay(1, 2, state)

    piece = half[pl.ds(pl.multiple_of(y * 16, 16), 16), :]
    for e in range(1, NY):
        second[e - 1].wait_recv()
        piece = piece + a2r[e].astype(F32)
    a3r[z] = piece.astype(BF16)
    third = [copy(a3r.at[z], a3r.at[z], z_peer(e)) for e in range(1, NZ)]

    relay(1, 3, state)
    finish_gather(state)
    sums_first(1, state)

    for one in third:
        one.wait_recv()
    piece = a3r[0].astype(F32)
    for n in range(1, NZ):
        piece = piece + a3r[n].astype(F32)
    a4r[x] = piece
    fourth = [copy(a4r.at[x], a4r.at[x], x_peer(e)) for e in range(1, NX)]

    product(1, 1)
    sums_second(1, state)

    for one in fourth:
        one.wait_recv()
    piece = (a4r[0] + a4r[1]) + (a4r[2] + a4r[3])
    at = pl.multiple_of(c * 128 + y * 16, 16)
    wbuf[pl.ds(at, 16), :] = piece
    fifth = [copy(wbuf.at[pl.ds(at, 16)], wbuf.at[pl.ds(at, 16)], y_peer(e)) for e in range(1, NY)]
    back = sums_last(1, state)
    for one in fifth:
        one.wait_recv()
    sixth = copy(wbuf.at[pl.ds(mine, 128)], wbuf.at[pl.ds(mine, 128)], sibling)
    vgrad = (scale * back).astype(BF16)
    grad_feats[...] = lax.dot_general(
        vgrad, weight[...], (((1,), (1,)), ((), ())), preferred_element_type=F32
    ).astype(BF16)
    stores.append(pltpu.make_async_copy(grad_feats, grad_feats_hbm, store_sems.at[1]))
    stores[1].start()
    sixth.wait_recv()
    stores.append(pltpu.make_async_copy(wbuf, grad_weight_hbm, store_sems.at[2]))
    stores[2].start()
    for one in started:
        one.wait_send()
    for one in stores:
        one.wait()


def deliver(*refs):
    sems = refs[-1]
    copies = [pltpu.make_async_copy(refs[n], refs[n + 3], sems.at[n]) for n in range(3)]
    for one in copies:
        one.start()
    for one in copies:
        one.wait()


def local(node_feats, weight, node_scale, tile_mask, cotangent, coef):
    hidden = weight.shape[0]
    hbm = pl.BlockSpec(memory_space=pltpu.HBM)
    shapes = (
        jax.ShapeDtypeStruct((ROWS, hidden), BF16),
        jax.ShapeDtypeStruct((ROWS, hidden), BF16),
        jax.ShapeDtypeStruct((hidden, hidden), F32),
    )
    made = pl.pallas_call(
        functools.partial(kernel, coef),
        out_shape=shapes,
        in_specs=[hbm] * 5,
        out_specs=(hbm,) * 3,
        scratch_shapes=[
            pltpu.VMEM((ROWS, hidden), BF16),
            pltpu.VMEM((hidden, hidden), BF16),
            pltpu.VMEM((1, ROWS), BF16),
            pltpu.VMEM(tile_mask.shape, jnp.int32),
            pltpu.VMEM((ROWS, hidden), BF16),
            pltpu.SemaphoreType.DMA((5,)),
            pltpu.VMEM((ROWS, hidden), BF16),
            pltpu.VMEM((ROWS, hidden), BF16),
            pltpu.SemaphoreType.DMA((3,)),
            pltpu.VMEM((1024, 2048), BF16),
            pltpu.VMEM((16, 2048), F32),
            pltpu.VMEM((2, NX, NZ * ROWS, 256), BF16),
            pltpu.VMEM((NZ, 8, HALF), F32),
            pltpu.VMEM((2, 512, 256), BF16),
            pltpu.VMEM((2, 512, 256), BF16),
            pltpu.VMEM((512, 256), F32),
            pltpu.VMEM((2, 512, 256), BF16),
            pltpu.VMEM((2, NY, ROWS, 256), BF16),
            pltpu.VMEM((256, 256), F32),
            pltpu.VMEM((128, 256), BF16),
            pltpu.VMEM((128, 256), BF16),
            pltpu.VMEM((128, 256), F32),
            pltpu.VMEM((128, 256), BF16),
            pltpu.VMEM((NY, 16, 256), BF16),
            pltpu.VMEM((NZ, 16, 256), BF16),
            pltpu.VMEM((NX, 16, 256), F32),
            pltpu.VMEM((256, 256), F32),
            pltpu.VMEM((ROWS, 256), F32),
            pltpu.SemaphoreType.DMA((COPIES,)),
            pltpu.SemaphoreType.DMA((COPIES,)),
        ],
        compiler_params=pltpu.CompilerParams(
            collective_id=0, has_side_effects=True, vmem_limit_bytes=56 * 1024 * 1024
        ),
    )(node_feats, weight, node_scale.reshape(1, ROWS), tile_mask, cotangent)
    return pl.pallas_call(
        deliver,
        out_shape=shapes,
        in_specs=[hbm] * 3,
        out_specs=(hbm,) * 3,
        scratch_shapes=[pltpu.SemaphoreType.DMA((3,))],
        compiler_params=pltpu.CompilerParams(vmem_limit_bytes=56 * 1024 * 1024),
    )(*made)


def solution(mesh):
    in_specs = (
        P(("section", "rep"), None),
        P(),
        P(("section", "rep")),
        P("section", None),
        P(("section", "rep"), None),
    )
    out_specs = (P(("section", "rep"), None), P(("section", "rep"), None), P())
    coef = 4.0 / math.sqrt(128 * 256)
    return jax.shard_map(
        functools.partial(local, coef=coef), mesh=mesh, in_specs=in_specs, out_specs=out_specs,
        check_vma=False,
    )
```

```python
import functools
import math

import jax
import jax.numpy as jnp
from jax import lax
from jax.experimental import pallas as pl
from jax.experimental.pallas import tpu as pltpu
from jax.sharding import PartitionSpec as P


MESH = pl.DeviceIdType.MESH
NZ, NY, NX = 8, 8, 4
ROWS = 64
HALF = 128
MODULUS = 65521
OFFSET = (0, 1, 7, 2, 6, 3, 5, 4)
SLOT = {off: k for k, off in enumerate(OFFSET)}
GROUPS = ((0, 1), (1, 3), (3, 5), (5, 8))
COPIES = 160
BF16 = jnp.bfloat16
F32 = jnp.float32


def fold(v):
    return (v & 0xFFFF) + 15 * (v >> 16)


def reduce_once(v):
    return jnp.where(v >= MODULUS, v - MODULUS, v)


def add_mod(q, step):
    total = q + step
    return jnp.where(total >= float(MODULUS), total - float(MODULUS), total)


def kernel(
    coef,
    feats_hbm, weight_hbm, scale_hbm, mask_hbm, cot_hbm,
    layer_out_hbm, grad_feats_hbm, grad_weight_hbm,
    feats, weight, scale_row, mask, cot, load_sems, layer_out, grad_feats, store_sems,
    adj, adj_t, cm, cm_low, cm_high, gath, gath_t, masks, csend, crecv, acc, ysend, yrecv,
    near_send, near_recv, keep, keep_near, next_send, next_recv, zsend, zrecv,
    part, a1s, a1r, half, a2s, a2r, a3r, a4r, wbuf, scale_col,
    send_sems, recv_sems,
):
    sec = lax.axis_index("section")
    x = lax.axis_index("rep")
    c = sec % 2
    y = (sec // 2) % NY
    z = sec // (2 * NY)
    x_one = x + 1 - 2 * (x % 2)
    x_two = 3 - x
    x_opp = (x + 2) % NX

    def device(zz, yy, cc, xx):
        return ((zz * NY + yy) * 2 + cc, xx)

    sibling = device(z, y, 1 - c, x)
    east, west = device(z, y, c, x_one), device(z, y, c, x_two)

    def z_peer(e):
        return device((z + e) % NZ, y, c, x)

    def y_peer(e):
        return device(z, (y + e) % NY, c, x)

    def x_peer(e):
        return device(z, y, c, (x + e) % NX)

    barrier = pltpu.get_barrier_semaphore()
    peers = [z_peer(e) for e in range(1, NZ)] + [y_peer(e) for e in range(1, NY)]
    peers += [x_peer(e) for e in range(1, NX)] + [sibling]
    for peer in peers:
        pl.semaphore_signal(barrier, inc=1, device_id=peer, device_id_type=MESH)

    loads = [
        pltpu.make_async_copy(src, dst, load_sems.at[n])
        for n, (src, dst) in enumerate((
            (feats_hbm, feats), (scale_hbm, scale_row), (mask_hbm, mask),
            (weight_hbm, weight), (cot_hbm, cot),
        ))
    ]
    for one in loads:
        one.start()

    started = []

    def copy(src, dst, target):
        number = len(started)
        one = pltpu.make_async_remote_copy(
            src_ref=src, dst_ref=dst, send_sem=send_sems.at[number],
            recv_sem=recv_sems.at[number], device_id=target, device_id_type=MESH,
        )
        one.start()
        started.append(one)
        return one

    for one in loads[:3]:
        one.wait()
    row = scale_row[...].astype(F32)
    pick = lax.broadcasted_iota(jnp.int32, (ROWS, ROWS), 0) == lax.broadcasted_iota(
        jnp.int32, (ROWS, ROWS), 1
    )
    column = jnp.sum(jnp.where(pick, jnp.broadcast_to(row, (ROWS, ROWS)), 0.0), axis=1, keepdims=True)
    scale_col[...] = jnp.broadcast_to(column, (ROWS, 256))
    scaled = (scale_col[...] * feats[...].astype(F32)).astype(BF16)
    gath[0, 0, 0:ROWS] = scaled[:, :HALF]
    gath_t[0, 0, 0:ROWS] = scaled[:, HALF:]
    masks[z] = jnp.zeros((8, HALF), F32)
    masks[z, 0:2, :] = mask[:, 0:HALF].astype(F32)
    masks[z, 2:4, :] = mask[:, HALF:].astype(F32)

    pl.semaphore_wait(barrier, len(peers))

    def start_pass(p):
        own = gath.at[p, 0, pl.ds(0, ROWS)]
        own_t = gath_t.at[p, 0, pl.ds(0, ROWS)]
        state = {"z": {}, "one": {}, "two": {}, "opp": [], "y_t": {}, "core_t": []}
        for k in range(1, NZ):
            e = (NZ - OFFSET[k]) % NZ
            run = pl.ds(k * ROWS, ROWS)
            state["z"][k] = copy(own, gath.at[p, 0, run], z_peer(e))
            state["y_t"][k] = copy(own_t, gath_t.at[p, 0, run], y_peer(e))
            if k == 2:
                forward(p, 0, state)
                forward_t(p, 0, state)
        return state

    def forward_t(p, g, state):
        lo, hi = GROUPS[g]
        for k in range(lo, hi):
            if k:
                state["y_t"][k].wait_recv()
        run = pl.ds(lo * ROWS, (hi - lo) * ROWS)
        state["core_t"].append(copy(gath_t.at[p, 0, run], gath_t.at[p, 1, run], sibling))

    def forward(p, g, state):
        lo, hi = GROUPS[g]
        for k in range(lo, hi):
            if k:
                state["z"][k].wait_recv()
        run = pl.ds(lo * ROWS, (hi - lo) * ROWS)
        state["one"][g] = copy(gath.at[p, 0, run], gath.at[p, 1, run], east)
        state["two"][g] = copy(gath.at[p, 0, run], gath.at[p, 2, run], west)

    def relay(p, g, state):
        lo, hi = GROUPS[g]
        size = (hi - lo) * ROWS // 2
        run = pl.ds(lo * ROWS, size)
        state["two"][g].wait_recv()
        state["opp"].append(copy(gath.at[p, 2, run], gath.at[p, 3, run], east))
        run = pl.ds(lo * ROWS + size, size)
        state["one"][g].wait_recv()
        state["opp"].append(copy(gath.at[p, 1, run], gath.at[p, 3, run], west))

    def finish_gather(state):
        for one in state["opp"]:
            one.wait_recv()

    def product(p, side):
        right = gath[p].reshape(NX * NZ * ROWS, HALF)
        value = jnp.dot(adj[side * 512:(side + 1) * 512, :], right, preferred_element_type=F32)
        if side == 0:
            csend[p] = value.astype(BF16)
        else:
            acc[...] = value

    def sums_first(p, state):
        product(p, 0)
        state["core"] = copy(csend.at[p], crecv.at[p], sibling)

    def sums_second(p, state):
        state["core"].wait_recv()
        total = acc[...] + crecv[p].astype(F32)
        acc[...] = total
        ysend[p] = total.astype(BF16)
        state["y"] = {}
        for e in (4, 3, 5, 2, 6, 1, 7):
            at = pl.multiple_of(((y + e) % NY) * ROWS, ROWS)
            state["y"][e] = copy(ysend.at[p, pl.ds(at, ROWS)], yrecv.at[p, e], y_peer(e))

    def sums_last(p, state):
        total = acc[pl.ds(pl.multiple_of(y * ROWS, ROWS), ROWS), :]
        for e in (1, 7, 2, 6, 3, 5, 4):
            state["y"][e].wait_recv()
            total = total + yrecv[p, e].astype(F32)
        return total

    def product_t(p, lo, hi):
        right = gath_t[p].reshape(2 * NY * ROWS, HALF)
        return jnp.dot(adj_t[lo:hi, :], right, preferred_element_type=F32)

    def near_first(p, state):
        for one in state["core_t"]:
            one.wait_recv()
        opposite = product_t(p, 1536, 2048)
        near_send[p, 0, 256:512] = opposite[:256].astype(BF16)
        near_send[p, 1, 256:512] = opposite[256:].astype(BF16)
        near_send[p, 0, 0:256] = product_t(p, 512, 768).astype(BF16)
        state["near_e"] = copy(near_send.at[p, 0], near_recv.at[p, 0], east)
        near_send[p, 1, 0:256] = product_t(p, 1280, 1536).astype(BF16)
        state["near_w"] = copy(near_send.at[p, 1], near_recv.at[p, 1], west)

    def near_second(p):
        keep_near[0] = product_t(p, 1024, 1280)
        keep_near[1] = product_t(p, 768, 1024)
        keep[...] = product_t(p, 0, 512)

    def next_first(p, state):
        state["near_e"].wait_recv()
        next_send[p, 0] = (keep_near[0] + near_recv[p, 0, 256:512].astype(F32)).astype(BF16)
        state["next_w"] = copy(next_send.at[p, 0], next_recv.at[p, 0], west)
        state["near_w"].wait_recv()
        next_send[p, 1] = (keep_near[1] + near_recv[p, 1, 256:512].astype(F32)).astype(BF16)
        state["next_e"] = copy(next_send.at[p, 1], next_recv.at[p, 1], east)
        keep[0:256] = keep[0:256] + near_recv[p, 0, 0:256].astype(F32)
        keep[256:512] = keep[256:512] + near_recv[p, 1, 0:256].astype(F32)

    def next_second(p, state):
        state["next_w"].wait_recv()
        state["next_e"].wait_recv()
        total = keep[...] + next_recv[p].reshape(512, HALF).astype(F32)
        keep[...] = total
        zsend[p] = total.astype(BF16)
        state["z_t"] = {}
        for e in (4, 3, 5, 2, 6, 1, 7):
            at = pl.multiple_of(((z + e) % NZ) * ROWS, ROWS)
            state["z_t"][e] = copy(zsend.at[p, pl.ds(at, ROWS)], zrecv.at[p, e], z_peer(e))

    def sums_last_t(p, state):
        total = keep[pl.ds(pl.multiple_of(z * ROWS, ROWS), ROWS), :]
        for e in (1, 7, 2, 6, 3, 5, 4):
            state["z_t"][e].wait_recv()
            total = total + zrecv[p, e].astype(F32)
        return total

    col_j = lax.broadcasted_iota(jnp.int32, (16, 512), 1)
    row_i = lax.broadcasted_iota(jnp.int32, (16, 512), 0)
    col_slot = col_j >> 6
    col_off = jnp.where((col_slot & 1) == 1, (col_slot + 1) >> 1, (8 - (col_slot >> 1)) & 7)
    columns_x = (x, x_one, x_two, x_opp)

    def side_core(side):
        return 1 - c if side == 0 else c

    def mask_columns():
        which = lax.broadcasted_iota(jnp.int32, (16, HALF), 0)
        lane = lax.broadcasted_iota(jnp.int32, (16, HALF), 1)
        core_of = jnp.where(which < 8, 1 - c, c)
        tile = ((z * NY + (which & 7)) * 2 + core_of) * 2 + x // 2
        every = masks[...].reshape(64, HALF)
        dims = (((1,), (1,)), ((), ()))
        low = lax.dot_general((tile == lane).astype(F32), every, dims, preferred_element_type=F32)
        high = lax.dot_general(
            (tile == lane + HALF).astype(F32), every, dims, preferred_element_type=F32
        )
        entry = lax.broadcasted_iota(jnp.int32, (64, 512), 0)
        slot = lax.broadcasted_iota(jnp.int32, (64, 512), 1) >> 6
        off = jnp.where((slot & 1) == 1, (slot + 1) >> 1, (8 - (slot >> 1)) & 7)
        same = (entry >> 3) == ((z + off) & 7)
        for n, xx in enumerate(columns_x):
            pick_low = jnp.where(same & ((entry & 7) == xx // 2), 1.0, 0.0).astype(F32)
            pick_high = jnp.where(same & ((entry & 7) == xx // 2 + 2), 1.0, 0.0).astype(F32)
            chosen = jnp.dot(low, pick_low, preferred_element_type=F32) + jnp.dot(
                high, pick_high, preferred_element_type=F32
            )
            cm[:, n * 512:(n + 1) * 512] = jnp.where(chosen > 0.5, coef, 0.0)

    def mask_columns_t():
        every = masks[...].reshape(64, HALF)
        entry = lax.broadcasted_iota(jnp.int32, (HALF, 512), 0)
        slot = lax.broadcasted_iota(jnp.int32, (HALF, 512), 1) >> 6
        off = jnp.where((slot & 1) == 1, (slot + 1) >> 1, (8 - (slot >> 1)) & 7)
        for h in range(2):
            core_of = c if h == 0 else 1 - c
            tile = ((z * NY + ((y + off) & 7)) * 2 + core_of) * 2 + x // 2
            low = jnp.dot(every, (tile == entry).astype(F32), preferred_element_type=F32)
            high = jnp.dot(every, (tile == entry + HALF).astype(F32), preferred_element_type=F32)
            cm_low[:, h * 512:(h + 1) * 512] = jnp.where(low > 0.5, coef, 0.0)
            cm_high[:, h * 512:(h + 1) * 512] = jnp.where(high > 0.5, coef, 0.0)

    def make(a, b, stride, target, top, lanes, coefs_of):
        first = fold(fold(a * b))
        hashed = reduce_once(fold(fold(first * 20011 + (a + b) * 7919)))
        step = reduce_once(fold(fold(b * 20011 + 7919)))
        step16 = reduce_once(fold(step * 16)).astype(F32)
        leap = reduce_once(fold(step * stride)).astype(F32)

        def run(number, q0):
            coefs = coefs_of(number)
            q = q0
            for s in range(4):
                at = pl.multiple_of(top + number * ROWS + s * 16, 16)
                target[pl.ds(at, 16), lanes] = (
                    (q * (2.0 / 65521.0) - 1.0) * coefs
                ).astype(BF16)
                if s < 3:
                    q = add_mod(q, step16)
            return add_mod(q0, leap)

        lax.fori_loop(0, 8, run, hashed.astype(F32))

    def make_block(n, side):
        b = ((((z + col_off) & 7) * NY + y) * 2 + c) * 256 + columns_x[n] * ROWS + (col_j & 63)
        a = ((z * NY) * 2 + side_core(side)) * 256 + x * ROWS + row_i
        lanes = slice(n * 512, (n + 1) * 512)
        make(a, b, 512, adj, side * 512, lanes, lambda yy: cm[pl.ds(side * 8 + yy, 1), lanes])

    def make_block_t(n, h):
        core_of = c if h == 0 else 1 - c
        b = ((z * NY + ((y + col_off) & 7)) * 2 + core_of) * 256 + x * ROWS + (col_j & 63)
        a = (y * 2 + c) * 256 + columns_x[n] * ROWS + row_i
        lanes = slice(h * 512, (h + 1) * 512)
        tile = columns_x[n] // 2

        def coefs_of(zz):
            low = cm_low[pl.ds(zz * 8 + tile, 1), lanes]
            return low + cm_high[pl.ds(zz * 8 + tile + 2, 1), lanes]

        make(a, b, 4096, adj_t, n * 512, lanes, coefs_of)

    mask_copies = [copy(masks.at[z], masks.at[z], z_peer(e)) for e in range(1, NZ)]
    state = start_pass(0)
    for one in mask_copies:
        one.wait_recv()
    forward(0, 1, state)
    forward_t(0, 1, state)
    relay(0, 0, state)
    mask_columns_t()
    make_block_t(3, 0)
    make_block_t(3, 1)
    forward(0, 2, state)
    forward_t(0, 2, state)
    relay(0, 1, state)
    make_block_t(1, 0)
    make_block_t(1, 1)
    forward(0, 3, state)
    forward_t(0, 3, state)
    relay(0, 2, state)
    make_block_t(2, 0)
    make_block_t(2, 1)
    relay(0, 3, state)
    near_first(0, state)
    make_block_t(0, 0)
    make_block_t(0, 1)
    near_second(0)
    mask_columns()
    for n in range(NX):
        make_block(n, 0)
    next_first(0, state)
    finish_gather(state)
    sums_first(0, state)
    for n in range(NX):
        make_block(n, 1)
    product(0, 1)
    next_second(0, state)
    sums_second(0, state)
    sums = jnp.concatenate([sums_last(0, state), sums_last_t(0, state)], axis=1)

    for one in loads[3:]:
        one.wait()
    sums_high = sums.astype(BF16)
    sums_low = (sums - sums_high.astype(F32)).astype(BF16)
    scale = scale_col[...]
    presum = scale * (
        jnp.dot(sums_high, weight[...], preferred_element_type=F32)
        + jnp.dot(sums_low, weight[...], preferred_element_type=F32)
    )
    sigma = jax.nn.sigmoid(presum)
    layer_out[...] = (presum * sigma).astype(BF16)
    stores = [pltpu.make_async_copy(layer_out, layer_out_hbm, store_sems.at[0])]
    stores[0].start()
    deriv = sigma * (1.0 + presum * (1.0 - sigma))
    error = (scale * cot[...].astype(F32) * deriv).astype(BF16)
    gath[1, 0, 0:ROWS] = error[:, :HALF]
    gath_t[1, 0, 0:ROWS] = error[:, HALF:]

    state = start_pass(1)
    part[...] = lax.dot_general(
        sums_high, error, (((0,), (0,)), ((), ())), preferred_element_type=F32
    )
    theirs = pl.multiple_of((1 - c) * 128, 128)
    mine = pl.multiple_of(c * 128, 128)
    a1s[...] = part[pl.ds(theirs, 128), :].astype(BF16)
    first = copy(a1s, a1r, sibling)
    forward(1, 1, state)
    forward_t(1, 1, state)
    relay(1, 0, state)

    first.wait_recv()
    half[...] = part[pl.ds(mine, 128), :] + a1r[...].astype(F32)
    a2s[...] = half[...].astype(BF16)
    second = []
    for e in range(1, NY):
        at = pl.multiple_of(((y + e) % NY) * 16, 16)
        second.append(copy(a2s.at[pl.ds(at, 16)], a2r.at[e], y_peer(e)))

    forward(1, 2, state)
    forward_t(1, 2, state)
    relay(1, 1, state)
    forward(1, 3, state)
    forward_t(1, 3, state)
    relay(1, 2, state)

    piece = half[pl.ds(pl.multiple_of(y * 16, 16), 16), :]
    for e in range(1, NY):
        second[e - 1].wait_recv()
        piece = piece + a2r[e].astype(F32)
    a3r[z] = piece.astype(BF16)
    third = [copy(a3r.at[z], a3r.at[z], z_peer(e)) for e in range(1, NZ)]

    near_first(1, state)
    relay(1, 3, state)
    near_second(1)

    for one in third:
        one.wait_recv()
    piece = a3r[0].astype(F32)
    for n in range(1, NZ):
        piece = piece + a3r[n].astype(F32)
    a4r[x] = piece
    fourth = [copy(a4r.at[x], a4r.at[x], x_peer(e)) for e in range(1, NX)]

    finish_gather(state)
    sums_first(1, state)
    next_first(1, state)
    product(1, 1)

    for one in fourth:
        one.wait_recv()
    piece = (a4r[0] + a4r[1]) + (a4r[2] + a4r[3])
    at = pl.multiple_of(c * 128 + y * 16, 16)
    wbuf[pl.ds(at, 16), :] = piece
    fifth = [copy(wbuf.at[pl.ds(at, 16)], wbuf.at[pl.ds(at, 16)], y_peer(e)) for e in range(1, NY)]

    sums_second(1, state)
    next_second(1, state)
    for one in fifth:
        one.wait_recv()
    sixth = copy(wbuf.at[pl.ds(mine, 128)], wbuf.at[pl.ds(mine, 128)], sibling)
    back = jnp.concatenate([sums_last(1, state), sums_last_t(1, state)], axis=1)
    vgrad = (scale * back).astype(BF16)
    grad_feats[...] = lax.dot_general(
        vgrad, weight[...], (((1,), (1,)), ((), ())), preferred_element_type=F32
    ).astype(BF16)
    stores.append(pltpu.make_async_copy(grad_feats, grad_feats_hbm, store_sems.at[1]))
    stores[1].start()
    sixth.wait_recv()
    stores.append(pltpu.make_async_copy(wbuf, grad_weight_hbm, store_sems.at[2]))
    stores[2].start()
    for one in started:
        one.wait_send()
    for one in stores:
        one.wait()


def local(node_feats, weight, node_scale, tile_mask, cotangent, coef):
    hidden = weight.shape[0]
    hbm = pl.BlockSpec(memory_space=pltpu.HBM)
    shapes = (
        jax.ShapeDtypeStruct((ROWS, hidden), BF16),
        jax.ShapeDtypeStruct((ROWS, hidden), BF16),
        jax.ShapeDtypeStruct((hidden, hidden), F32),
    )
    return pl.pallas_call(
        functools.partial(kernel, coef),
        out_shape=shapes,
        in_specs=[hbm] * 5,
        out_specs=(hbm,) * 3,
        scratch_shapes=[
            pltpu.VMEM((ROWS, hidden), BF16),
            pltpu.VMEM((hidden, hidden), BF16),
            pltpu.VMEM((1, ROWS), BF16),
            pltpu.VMEM(tile_mask.shape, jnp.int32),
            pltpu.VMEM((ROWS, hidden), BF16),
            pltpu.SemaphoreType.DMA((5,)),
            pltpu.VMEM((ROWS, hidden), BF16),
            pltpu.VMEM((ROWS, hidden), BF16),
            pltpu.SemaphoreType.DMA((3,)),
            pltpu.VMEM((1024, 2048), BF16),
            pltpu.VMEM((2048, 1024), BF16),
            pltpu.VMEM((16, 2048), F32),
            pltpu.VMEM((64, 1024), F32),
            pltpu.VMEM((64, 1024), F32),
            pltpu.VMEM((2, NX, NZ * ROWS, HALF), BF16),
            pltpu.VMEM((2, 2, NY * ROWS, HALF), BF16),
            pltpu.VMEM((NZ, 8, HALF), F32),
            pltpu.VMEM((2, 512, HALF), BF16),
            pltpu.VMEM((2, 512, HALF), BF16),
            pltpu.VMEM((512, HALF), F32),
            pltpu.VMEM((2, 512, HALF), BF16),
            pltpu.VMEM((2, NY, ROWS, HALF), BF16),
            pltpu.VMEM((2, 2, 512, HALF), BF16),
            pltpu.VMEM((2, 2, 512, HALF), BF16),
            pltpu.VMEM((512, HALF), F32),
            pltpu.VMEM((2, 256, HALF), F32),
            pltpu.VMEM((2, 2, 256, HALF), BF16),
            pltpu.VMEM((2, 2, 256, HALF), BF16),
            pltpu.VMEM((2, 512, HALF), BF16),
            pltpu.VMEM((2, NZ, ROWS, HALF), BF16),
            pltpu.VMEM((256, 256), F32),
            pltpu.VMEM((128, 256), BF16),
            pltpu.VMEM((128, 256), BF16),
            pltpu.VMEM((128, 256), F32),
            pltpu.VMEM((128, 256), BF16),
            pltpu.VMEM((NY, 16, 256), BF16),
            pltpu.VMEM((NZ, 16, 256), BF16),
            pltpu.VMEM((NX, 16, 256), F32),
            pltpu.VMEM((256, 256), F32),
            pltpu.VMEM((ROWS, 256), F32),
            pltpu.SemaphoreType.DMA((COPIES,)),
            pltpu.SemaphoreType.DMA((COPIES,)),
        ],
        compiler_params=pltpu.CompilerParams(
            collective_id=0, has_side_effects=True, vmem_limit_bytes=56 * 1024 * 1024
        ),
    )(node_feats, weight, node_scale.reshape(1, ROWS), tile_mask, cotangent)


def solution(mesh):
    in_specs = (
        P(("section", "rep"), None),
        P(),
        P(("section", "rep")),
        P("section", None),
        P(("section", "rep"), None),
    )
    out_specs = (P(("section", "rep"), None), P(("section", "rep"), None), P())
    coef = 4.0 / math.sqrt(128 * 256)
    return jax.shard_map(
        functools.partial(local, coef=coef), mesh=mesh, in_specs=in_specs, out_specs=out_specs,
        check_vma=False,
    )
```

```python
import functools
import math

import jax
import jax.numpy as jnp
from jax import lax
from jax.experimental import pallas as pl
from jax.experimental.pallas import tpu as pltpu
from jax.sharding import PartitionSpec as P


MESH = pl.DeviceIdType.MESH
NZ, NY, NX = 8, 8, 4
ROWS = 64
HALF = 128
MODULUS = 65521
OFFSET = (0, 1, 7, 2, 6, 3, 5, 4)
SLOT = {off: k for k, off in enumerate(OFFSET)}
GROUPS = ((0, 1), (1, 3), (3, 5), (5, 8))
COPIES = 160
BF16 = jnp.bfloat16
F32 = jnp.float32


def fold(v):
    return (v & 0xFFFF) + 15 * (v >> 16)


def reduce_once(v):
    return jnp.where(v >= MODULUS, v - MODULUS, v)


def add_mod(q, step):
    total = q + step
    return jnp.where(total >= float(MODULUS), total - float(MODULUS), total)


def kernel(
    coef,
    feats_hbm, weight_hbm, scale_hbm, mask_hbm, cot_hbm,
    layer_out, grad_feats, grad_weight,
    feats, weight, scale_row, mask, cot, load_sems,
    adj, adj_t, cm, cm_low, cm_high, gath, gath_t, masks, csend, crecv, acc, ysend, yrecv,
    near_send, near_recv, keep, keep_near, next_send, next_recv, zsend, zrecv,
    part, a1s, a1r, half, a2s, a2r, a3r, a4r, wbuf, scale_col,
    send_sems, recv_sems,
):
    sec = lax.axis_index("section")
    x = lax.axis_index("rep")
    c = sec % 2
    y = (sec // 2) % NY
    z = sec // (2 * NY)
    x_one = x + 1 - 2 * (x % 2)
    x_two = 3 - x
    x_opp = (x + 2) % NX

    def device(zz, yy, cc, xx):
        return ((zz * NY + yy) * 2 + cc, xx)

    sibling = device(z, y, 1 - c, x)
    east, west = device(z, y, c, x_one), device(z, y, c, x_two)

    def z_peer(e):
        return device((z + e) % NZ, y, c, x)

    def y_peer(e):
        return device(z, (y + e) % NY, c, x)

    def x_peer(e):
        return device(z, y, c, (x + e) % NX)

    barrier = pltpu.get_barrier_semaphore()
    peers = [z_peer(e) for e in range(1, NZ)] + [y_peer(e) for e in range(1, NY)]
    peers += [x_peer(e) for e in range(1, NX)] + [sibling]
    for peer in peers:
        pl.semaphore_signal(barrier, inc=1, device_id=peer, device_id_type=MESH)

    loads = [
        pltpu.make_async_copy(src, dst, load_sems.at[n])
        for n, (src, dst) in enumerate((
            (feats_hbm, feats), (scale_hbm, scale_row), (mask_hbm, mask),
            (weight_hbm, weight), (cot_hbm, cot),
        ))
    ]
    for one in loads:
        one.start()

    started = []

    def copy(src, dst, target):
        number = len(started)
        one = pltpu.make_async_remote_copy(
            src_ref=src, dst_ref=dst, send_sem=send_sems.at[number],
            recv_sem=recv_sems.at[number], device_id=target, device_id_type=MESH,
        )
        one.start()
        started.append(one)
        return one

    for one in loads[:3]:
        one.wait()
    row = scale_row[...].astype(F32)
    pick = lax.broadcasted_iota(jnp.int32, (ROWS, ROWS), 0) == lax.broadcasted_iota(
        jnp.int32, (ROWS, ROWS), 1
    )
    column = jnp.sum(jnp.where(pick, jnp.broadcast_to(row, (ROWS, ROWS)), 0.0), axis=1, keepdims=True)
    scale_col[...] = jnp.broadcast_to(column, (ROWS, 256))
    scaled = (scale_col[...] * feats[...].astype(F32)).astype(BF16)
    gath[0, 0, 0:ROWS] = scaled[:, :HALF]
    gath_t[0, 0, 0:ROWS] = scaled[:, HALF:]
    masks[z] = jnp.zeros((8, HALF), F32)
    masks[z, 0:2, :] = mask[:, 0:HALF].astype(F32)
    masks[z, 2:4, :] = mask[:, HALF:].astype(F32)

    pl.semaphore_wait(barrier, len(peers))

    def start_pass(p):
        own = gath.at[p, 0, pl.ds(0, ROWS)]
        own_t = gath_t.at[p, 0, pl.ds(0, ROWS)]
        state = {"z": {}, "one": {}, "two": {}, "opp": [], "y_t": {}, "core_t": []}
        for k in range(1, NZ):
            e = (NZ - OFFSET[k]) % NZ
            run = pl.ds(k * ROWS, ROWS)
            state["z"][k] = copy(own, gath.at[p, 0, run], z_peer(e))
            state["y_t"][k] = copy(own_t, gath_t.at[p, 0, run], y_peer(e))
            if k == 2:
                forward(p, 0, state)
                forward_t(p, 0, state)
        return state

    def forward_t(p, g, state):
        lo, hi = GROUPS[g]
        for k in range(lo, hi):
            if k:
                state["y_t"][k].wait_recv()
        run = pl.ds(lo * ROWS, (hi - lo) * ROWS)
        state["core_t"].append(copy(gath_t.at[p, 0, run], gath_t.at[p, 1, run], sibling))

    def forward(p, g, state):
        lo, hi = GROUPS[g]
        for k in range(lo, hi):
            if k:
                state["z"][k].wait_recv()
        run = pl.ds(lo * ROWS, (hi - lo) * ROWS)
        state["one"][g] = copy(gath.at[p, 0, run], gath.at[p, 1, run], east)
        state["two"][g] = copy(gath.at[p, 0, run], gath.at[p, 2, run], west)

    def relay(p, g, state):
        lo, hi = GROUPS[g]
        size = (hi - lo) * ROWS // 2
        run = pl.ds(lo * ROWS, size)
        state["two"][g].wait_recv()
        state["opp"].append(copy(gath.at[p, 2, run], gath.at[p, 3, run], east))
        run = pl.ds(lo * ROWS + size, size)
        state["one"][g].wait_recv()
        state["opp"].append(copy(gath.at[p, 1, run], gath.at[p, 3, run], west))

    def finish_gather(state):
        for one in state["opp"]:
            one.wait_recv()

    def product(p, side):
        right = gath[p].reshape(NX * NZ * ROWS, HALF)
        value = jnp.dot(adj[side * 512:(side + 1) * 512, :], right, preferred_element_type=F32)
        if side == 0:
            csend[p] = value.astype(BF16)
        else:
            acc[...] = value

    def sums_first(p, state):
        product(p, 0)
        state["core"] = copy(csend.at[p], crecv.at[p], sibling)

    def sums_second(p, state):
        state["core"].wait_recv()
        total = acc[...] + crecv[p].astype(F32)
        acc[...] = total
        ysend[p] = total.astype(BF16)
        state["y"] = {}
        for e in (4, 3, 5, 2, 6, 1, 7):
            at = pl.multiple_of(((y + e) % NY) * ROWS, ROWS)
            state["y"][e] = copy(ysend.at[p, pl.ds(at, ROWS)], yrecv.at[p, e], y_peer(e))

    def sums_last(p, state):
        total = acc[pl.ds(pl.multiple_of(y * ROWS, ROWS), ROWS), :]
        for e in (1, 7, 2, 6, 3, 5, 4):
            state["y"][e].wait_recv()
            total = total + yrecv[p, e].astype(F32)
        return total

    def product_t(p, lo, hi):
        right = gath_t[p].reshape(2 * NY * ROWS, HALF)
        return jnp.dot(adj_t[lo:hi, :], right, preferred_element_type=F32)

    def near_first(p, state):
        for one in state["core_t"]:
            one.wait_recv()
        opposite = product_t(p, 1536, 2048)
        near_send[p, 0, 256:512] = opposite[:256].astype(BF16)
        near_send[p, 1, 256:512] = opposite[256:].astype(BF16)
        far, close = pl.ds(256, 256), pl.ds(0, 256)
        state["far_e"] = copy(near_send.at[p, 0, far], near_recv.at[p, 0, far], east)
        state["far_w"] = copy(near_send.at[p, 1, far], near_recv.at[p, 1, far], west)
        near_send[p, 0, 0:256] = product_t(p, 512, 768).astype(BF16)
        state["near_e"] = copy(near_send.at[p, 0, close], near_recv.at[p, 0, close], east)
        near_send[p, 1, 0:256] = product_t(p, 1280, 1536).astype(BF16)
        state["near_w"] = copy(near_send.at[p, 1, close], near_recv.at[p, 1, close], west)

    def near_second(p):
        keep_near[0] = product_t(p, 1024, 1280)
        keep_near[1] = product_t(p, 768, 1024)

    def next_first(p, state):
        state["far_e"].wait_recv()
        next_send[p, 0] = (keep_near[0] + near_recv[p, 0, 256:512].astype(F32)).astype(BF16)
        state["next_w"] = copy(next_send.at[p, 0], next_recv.at[p, 0], west)
        state["far_w"].wait_recv()
        next_send[p, 1] = (keep_near[1] + near_recv[p, 1, 256:512].astype(F32)).astype(BF16)
        state["next_e"] = copy(next_send.at[p, 1], next_recv.at[p, 1], east)
        value = product_t(p, 0, 512)
        state["near_e"].wait_recv()
        state["near_w"].wait_recv()
        keep[0:256] = value[:256] + near_recv[p, 0, 0:256].astype(F32)
        keep[256:512] = value[256:] + near_recv[p, 1, 0:256].astype(F32)

    def next_second(p, state):
        state["next_w"].wait_recv()
        state["next_e"].wait_recv()
        total = keep[...] + next_recv[p].reshape(512, HALF).astype(F32)
        keep[...] = total
        zsend[p] = total.astype(BF16)
        state["z_t"] = {}
        for e in (4, 3, 5, 2, 6, 1, 7):
            at = pl.multiple_of(((z + e) % NZ) * ROWS, ROWS)
            state["z_t"][e] = copy(zsend.at[p, pl.ds(at, ROWS)], zrecv.at[p, e], z_peer(e))

    def sums_last_t(p, state):
        total = keep[pl.ds(pl.multiple_of(z * ROWS, ROWS), ROWS), :]
        for e in (1, 7, 2, 6, 3, 5, 4):
            state["z_t"][e].wait_recv()
            total = total + zrecv[p, e].astype(F32)
        return total

    col_j = lax.broadcasted_iota(jnp.int32, (16, 512), 1)
    row_i = lax.broadcasted_iota(jnp.int32, (16, 512), 0)
    col_slot = col_j >> 6
    col_off = jnp.where((col_slot & 1) == 1, (col_slot + 1) >> 1, (8 - (col_slot >> 1)) & 7)
    columns_x = (x, x_one, x_two, x_opp)

    def side_core(side):
        return 1 - c if side == 0 else c

    def mask_columns():
        which = lax.broadcasted_iota(jnp.int32, (16, HALF), 0)
        lane = lax.broadcasted_iota(jnp.int32, (16, HALF), 1)
        core_of = jnp.where(which < 8, 1 - c, c)
        tile = ((z * NY + (which & 7)) * 2 + core_of) * 2 + x // 2
        every = masks[...].reshape(64, HALF)
        dims = (((1,), (1,)), ((), ()))
        low = lax.dot_general((tile == lane).astype(F32), every, dims, preferred_element_type=F32)
        high = lax.dot_general(
            (tile == lane + HALF).astype(F32), every, dims, preferred_element_type=F32
        )
        entry = lax.broadcasted_iota(jnp.int32, (64, 512), 0)
        slot = lax.broadcasted_iota(jnp.int32, (64, 512), 1) >> 6
        off = jnp.where((slot & 1) == 1, (slot + 1) >> 1, (8 - (slot >> 1)) & 7)
        same = (entry >> 3) == ((z + off) & 7)
        for n, xx in enumerate(columns_x):
            pick_low = jnp.where(same & ((entry & 7) == xx // 2), 1.0, 0.0).astype(F32)
            pick_high = jnp.where(same & ((entry & 7) == xx // 2 + 2), 1.0, 0.0).astype(F32)
            chosen = jnp.dot(low, pick_low, preferred_element_type=F32) + jnp.dot(
                high, pick_high, preferred_element_type=F32
            )
            cm[:, n * 512:(n + 1) * 512] = jnp.where(chosen > 0.5, coef, 0.0)

    def mask_columns_t():
        every = masks[...].reshape(64, HALF)
        entry = lax.broadcasted_iota(jnp.int32, (HALF, 512), 0)
        slot = lax.broadcasted_iota(jnp.int32, (HALF, 512), 1) >> 6
        off = jnp.where((slot & 1) == 1, (slot + 1) >> 1, (8 - (slot >> 1)) & 7)
        for h in range(2):
            core_of = c if h == 0 else 1 - c
            tile = ((z * NY + ((y + off) & 7)) * 2 + core_of) * 2 + x // 2
            low = jnp.dot(every, (tile == entry).astype(F32), preferred_element_type=F32)
            high = jnp.dot(every, (tile == entry + HALF).astype(F32), preferred_element_type=F32)
            cm_low[:, h * 512:(h + 1) * 512] = jnp.where(low > 0.5, coef, 0.0)
            cm_high[:, h * 512:(h + 1) * 512] = jnp.where(high > 0.5, coef, 0.0)

    def make(a, b, stride, target, top, lanes, coefs_of):
        first = fold(fold(a * b))
        hashed = reduce_once(fold(fold(first * 20011 + (a + b) * 7919)))
        step = reduce_once(fold(fold(b * 20011 + 7919)))
        step16 = reduce_once(fold(step * 16)).astype(F32)
        leap = reduce_once(fold(step * stride)).astype(F32)

        def run(number, q0):
            coefs = coefs_of(number)
            q = q0
            for s in range(4):
                at = pl.multiple_of(top + number * ROWS + s * 16, 16)
                target[pl.ds(at, 16), lanes] = (
                    (q * (2.0 / 65521.0) - 1.0) * coefs
                ).astype(BF16)
                if s < 3:
                    q = add_mod(q, step16)
            return add_mod(q0, leap)

        lax.fori_loop(0, 8, run, hashed.astype(F32))

    def make_block(n, side):
        b = ((((z + col_off) & 7) * NY + y) * 2 + c) * 256 + columns_x[n] * ROWS + (col_j & 63)
        a = ((z * NY) * 2 + side_core(side)) * 256 + x * ROWS + row_i
        lanes = slice(n * 512, (n + 1) * 512)
        make(a, b, 512, adj, side * 512, lanes, lambda yy: cm[pl.ds(side * 8 + yy, 1), lanes])

    def make_block_t(n, h):
        core_of = c if h == 0 else 1 - c
        b = ((z * NY + ((y + col_off) & 7)) * 2 + core_of) * 256 + x * ROWS + (col_j & 63)
        a = (y * 2 + c) * 256 + columns_x[n] * ROWS + row_i
        lanes = slice(h * 512, (h + 1) * 512)
        tile = columns_x[n] // 2

        def coefs_of(zz):
            low = cm_low[pl.ds(zz * 8 + tile, 1), lanes]
            return low + cm_high[pl.ds(zz * 8 + tile + 2, 1), lanes]

        make(a, b, 4096, adj_t, n * 512, lanes, coefs_of)

    mask_copies = [copy(masks.at[z], masks.at[z], z_peer(e)) for e in range(1, NZ)]
    state = start_pass(0)
    for one in mask_copies:
        one.wait_recv()
    forward(0, 1, state)
    forward_t(0, 1, state)
    relay(0, 0, state)
    mask_columns_t()
    make_block_t(3, 0)
    make_block_t(3, 1)
    forward(0, 2, state)
    forward_t(0, 2, state)
    relay(0, 1, state)
    make_block_t(1, 0)
    make_block_t(1, 1)
    forward(0, 3, state)
    forward_t(0, 3, state)
    relay(0, 2, state)
    make_block_t(2, 0)
    make_block_t(2, 1)
    relay(0, 3, state)
    near_first(0, state)
    near_second(0)
    mask_columns()
    make_block(0, 0)
    make_block(1, 0)
    make_block_t(0, 0)
    make_block_t(0, 1)
    next_first(0, state)
    make_block(2, 0)
    make_block(3, 0)
    finish_gather(state)
    sums_first(0, state)
    for n in range(NX):
        make_block(n, 1)
    product(0, 1)
    next_second(0, state)
    sums_second(0, state)
    sums = jnp.concatenate([sums_last(0, state), sums_last_t(0, state)], axis=1)

    for one in loads[3:]:
        one.wait()
    sums_high = sums.astype(BF16)
    sums_low = (sums - sums_high.astype(F32)).astype(BF16)
    scale = scale_col[...]
    presum = scale * (
        jnp.dot(sums_high, weight[...], preferred_element_type=F32)
        + jnp.dot(sums_low, weight[...], preferred_element_type=F32)
    )
    sigma = jax.nn.sigmoid(presum)
    layer_out[...] = (presum * sigma).astype(BF16)
    deriv = sigma * (1.0 + presum * (1.0 - sigma))
    error = (scale * cot[...].astype(F32) * deriv).astype(BF16)
    gath[1, 0, 0:ROWS] = error[:, :HALF]
    gath_t[1, 0, 0:ROWS] = error[:, HALF:]

    state = start_pass(1)
    part[...] = lax.dot_general(
        sums_high, error, (((0,), (0,)), ((), ())), preferred_element_type=F32
    )
    theirs = pl.multiple_of((1 - c) * 128, 128)
    mine = pl.multiple_of(c * 128, 128)
    a1s[...] = part[pl.ds(theirs, 128), :].astype(BF16)
    first = copy(a1s, a1r, sibling)
    forward(1, 1, state)
    forward_t(1, 1, state)
    relay(1, 0, state)

    first.wait_recv()
    half[...] = part[pl.ds(mine, 128), :] + a1r[...].astype(F32)
    a2s[...] = half[...].astype(BF16)
    second = []
    for e in range(1, NY):
        at = pl.multiple_of(((y + e) % NY) * 16, 16)
        second.append(copy(a2s.at[pl.ds(at, 16)], a2r.at[e], y_peer(e)))

    forward(1, 2, state)
    forward_t(1, 2, state)
    relay(1, 1, state)
    forward(1, 3, state)
    forward_t(1, 3, state)
    relay(1, 2, state)

    piece = half[pl.ds(pl.multiple_of(y * 16, 16), 16), :]
    for e in range(1, NY):
        second[e - 1].wait_recv()
        piece = piece + a2r[e].astype(F32)
    a3r[z] = piece.astype(BF16)
    third = [copy(a3r.at[z], a3r.at[z], z_peer(e)) for e in range(1, NZ)]

    near_first(1, state)
    relay(1, 3, state)
    near_second(1)

    for one in third:
        one.wait_recv()
    piece = a3r[0].astype(F32)
    for n in range(1, NZ):
        piece = piece + a3r[n].astype(F32)
    a4r[x] = piece
    fourth = [copy(a4r.at[x], a4r.at[x], x_peer(e)) for e in range(1, NX)]

    next_first(1, state)
    finish_gather(state)
    sums_first(1, state)
    product(1, 1)

    for one in fourth:
        one.wait_recv()
    piece = (a4r[0] + a4r[1]) + (a4r[2] + a4r[3])
    at = pl.multiple_of(c * 128 + y * 16, 16)
    wbuf[pl.ds(at, 16), :] = piece
    fifth = [copy(wbuf.at[pl.ds(at, 16)], wbuf.at[pl.ds(at, 16)], y_peer(e)) for e in range(1, NY)]

    sums_second(1, state)
    next_second(1, state)
    for one in fifth:
        one.wait_recv()
    sixth = copy(wbuf.at[pl.ds(mine, 128)], wbuf.at[pl.ds(mine, 128)], sibling)
    back = jnp.concatenate([sums_last(1, state), sums_last_t(1, state)], axis=1)
    vgrad = (scale * back).astype(BF16)
    grad_feats[...] = lax.dot_general(
        vgrad, weight[...], (((1,), (1,)), ((), ())), preferred_element_type=F32
    ).astype(BF16)
    sixth.wait_recv()
    grad_weight[...] = wbuf[...]
    for one in started:
        one.wait_send()


def deliver(*refs):
    sems = refs[-1]
    copies = [pltpu.make_async_copy(refs[n], refs[n + 3], sems.at[n]) for n in range(3)]
    for one in copies:
        one.start()
    for one in copies:
        one.wait()


def local(node_feats, weight, node_scale, tile_mask, cotangent, coef):
    hidden = weight.shape[0]
    hbm = pl.BlockSpec(memory_space=pltpu.HBM)
    vmem = pl.BlockSpec(memory_space=pltpu.VMEM)
    shapes = (((ROWS, hidden), BF16), ((ROWS, hidden), BF16), ((hidden, hidden), F32))
    args = (node_feats, weight, node_scale.reshape(1, ROWS), tile_mask, cotangent)
    made = pl.pallas_call(
        functools.partial(kernel, coef),
        out_shape=tuple(pltpu.VMEM(*shape) for shape in shapes),
        in_specs=[hbm] * 5,
        out_specs=(vmem,) * 3,
        scratch_shapes=[
            pltpu.VMEM((ROWS, hidden), BF16),
            pltpu.VMEM((hidden, hidden), BF16),
            pltpu.VMEM((1, ROWS), BF16),
            pltpu.VMEM(tile_mask.shape, jnp.int32),
            pltpu.VMEM((ROWS, hidden), BF16),
            pltpu.SemaphoreType.DMA((5,)),
            pltpu.VMEM((1024, 2048), BF16),
            pltpu.VMEM((2048, 1024), BF16),
            pltpu.VMEM((16, 2048), F32),
            pltpu.VMEM((64, 1024), F32),
            pltpu.VMEM((64, 1024), F32),
            pltpu.VMEM((2, NX, NZ * ROWS, HALF), BF16),
            pltpu.VMEM((2, 2, NY * ROWS, HALF), BF16),
            pltpu.VMEM((NZ, 8, HALF), F32),
            pltpu.VMEM((2, 512, HALF), BF16),
            pltpu.VMEM((2, 512, HALF), BF16),
            pltpu.VMEM((512, HALF), F32),
            pltpu.VMEM((2, 512, HALF), BF16),
            pltpu.VMEM((2, NY, ROWS, HALF), BF16),
            pltpu.VMEM((2, 2, 512, HALF), BF16),
            pltpu.VMEM((2, 2, 512, HALF), BF16),
            pltpu.VMEM((512, HALF), F32),
            pltpu.VMEM((2, 256, HALF), F32),
            pltpu.VMEM((2, 2, 256, HALF), BF16),
            pltpu.VMEM((2, 2, 256, HALF), BF16),
            pltpu.VMEM((2, 512, HALF), BF16),
            pltpu.VMEM((2, NZ, ROWS, HALF), BF16),
            pltpu.VMEM((256, 256), F32),
            pltpu.VMEM((128, 256), BF16),
            pltpu.VMEM((128, 256), BF16),
            pltpu.VMEM((128, 256), F32),
            pltpu.VMEM((128, 256), BF16),
            pltpu.VMEM((NY, 16, 256), BF16),
            pltpu.VMEM((NZ, 16, 256), BF16),
            pltpu.VMEM((NX, 16, 256), F32),
            pltpu.VMEM((256, 256), F32),
            pltpu.VMEM((ROWS, 256), F32),
            pltpu.SemaphoreType.DMA((COPIES,)),
            pltpu.SemaphoreType.DMA((COPIES,)),
        ],
        compiler_params=pltpu.CompilerParams(
            collective_id=0, has_side_effects=True, vmem_limit_bytes=40 * 1024 * 1024
        ),
    )(*(pltpu.with_memory_space_constraint(arg, pltpu.HBM) for arg in args))
    return pl.pallas_call(
        deliver,
        out_shape=tuple(jax.ShapeDtypeStruct(*shape) for shape in shapes),
        in_specs=[vmem] * 3,
        out_specs=(hbm,) * 3,
        scratch_shapes=[pltpu.SemaphoreType.DMA((3,))],
        compiler_params=pltpu.CompilerParams(vmem_limit_bytes=8 * 1024 * 1024),
    )(*(pltpu.with_memory_space_constraint(one, pltpu.VMEM) for one in made))


def solution(mesh):
    in_specs = (
        P(("section", "rep"), None),
        P(),
        P(("section", "rep")),
        P("section", None),
        P(("section", "rep"), None),
    )
    out_specs = (P(("section", "rep"), None), P(("section", "rep"), None), P())
    coef = 4.0 / math.sqrt(128 * 256)
    return jax.shard_map(
        functools.partial(local, coef=coef), mesh=mesh, in_specs=in_specs, out_specs=out_specs,
        check_vma=False,
    )
```

```python
import functools
import math

import jax
import jax.numpy as jnp
from jax import lax
from jax.experimental import pallas as pl
from jax.experimental.pallas import tpu as pltpu
from jax.sharding import PartitionSpec as P


MESH = pl.DeviceIdType.MESH
NZ, NY, NX = 8, 8, 4
ROWS = 64
HALF = 128
MODULUS = 65521
OFFSET = (0, 1, 7, 2, 6, 3, 5, 4)
SLOT = {off: k for k, off in enumerate(OFFSET)}
GROUPS = ((0, 1), (1, 3), (3, 5), (5, 8))
COPIES = 160
BF16 = jnp.bfloat16
F32 = jnp.float32


def fold(v):
    return (v & 0xFFFF) + 15 * (v >> 16)


def reduce_once(v):
    return jnp.where(v >= MODULUS, v - MODULUS, v)


SCALE = 2.0 / MODULUS
WRAP = 1.0 - 0.5 * SCALE


def add_wrapped(u, step):
    total = u + step
    return jnp.where(total >= WRAP, total - 2.0, total)


def kernel(
    coef,
    feats_hbm, weight_hbm, scale_hbm, mask_hbm, cot_hbm,
    layer_out, grad_feats, grad_weight,
    feats, weight, scale_row, mask, cot, load_sems,
    adj, adj_t, cm, cm_low, cm_high, gath, gath_t, masks, csend, crecv, acc, ysend, yrecv,
    near_send, near_recv, keep, keep_near, next_send, next_recv, zsend, zrecv,
    starts, steps, part, a1s, a1r, half, a2s, a2r, a3r, a4r, wbuf, scale_col,
    send_sems, recv_sems,
):
    sec = lax.axis_index("section")
    x = lax.axis_index("rep")
    c = sec % 2
    y = (sec // 2) % NY
    z = sec // (2 * NY)
    x_one = x + 1 - 2 * (x % 2)
    x_two = 3 - x
    x_opp = (x + 2) % NX

    def device(zz, yy, cc, xx):
        return ((zz * NY + yy) * 2 + cc, xx)

    sibling = device(z, y, 1 - c, x)
    east, west = device(z, y, c, x_one), device(z, y, c, x_two)

    def z_peer(e):
        return device((z + e) % NZ, y, c, x)

    def y_peer(e):
        return device(z, (y + e) % NY, c, x)

    def x_peer(e):
        return device(z, y, c, (x + e) % NX)

    loads = [
        pltpu.make_async_copy(src, dst, load_sems.at[n])
        for n, (src, dst) in enumerate((
            (feats_hbm, feats), (scale_hbm, scale_row), (mask_hbm, mask),
            (weight_hbm, weight), (cot_hbm, cot),
        ))
    ]
    for one in loads:
        one.start()

    barrier = pltpu.get_barrier_semaphore()
    peers = [z_peer(e) for e in range(1, NZ)] + [y_peer(e) for e in range(1, NY)]
    peers += [x_peer(e) for e in range(1, NX)] + [sibling]
    for peer in peers:
        pl.semaphore_signal(barrier, inc=1, device_id=peer, device_id_type=MESH)

    started = []

    def copy(src, dst, target):
        number = len(started)
        one = pltpu.make_async_remote_copy(
            src_ref=src, dst_ref=dst, send_sem=send_sems.at[number],
            recv_sem=recv_sems.at[number], device_id=target, device_id_type=MESH,
        )
        one.start()
        started.append(one)
        return one

    col_j = lax.broadcasted_iota(jnp.int32, (16, 512), 1)
    row_i = lax.broadcasted_iota(jnp.int32, (16, 512), 0)
    col_slot = col_j >> 6
    col_off = jnp.where((col_slot & 1) == 1, (col_slot + 1) >> 1, (8 - (col_slot >> 1)) & 7)
    columns_x = (x, x_one, x_two, x_opp)

    def side_core(side):
        return 1 - c if side == 0 else c

    def mask_columns():
        which = lax.broadcasted_iota(jnp.int32, (16, HALF), 0)
        lane = lax.broadcasted_iota(jnp.int32, (16, HALF), 1)
        core_of = jnp.where(which < 8, 1 - c, c)
        tile = ((z * NY + (which & 7)) * 2 + core_of) * 2 + x // 2
        every = masks[...].reshape(64, HALF)
        dims = (((1,), (1,)), ((), ()))
        low = lax.dot_general((tile == lane).astype(F32), every, dims, preferred_element_type=F32)
        high = lax.dot_general(
            (tile == lane + HALF).astype(F32), every, dims, preferred_element_type=F32
        )
        entry = lax.broadcasted_iota(jnp.int32, (64, 512), 0)
        slot = lax.broadcasted_iota(jnp.int32, (64, 512), 1) >> 6
        off = jnp.where((slot & 1) == 1, (slot + 1) >> 1, (8 - (slot >> 1)) & 7)
        same = (entry >> 3) == ((z + off) & 7)
        for n, xx in enumerate(columns_x):
            pick_low = jnp.where(same & ((entry & 7) == xx // 2), 1.0, 0.0).astype(F32)
            pick_high = jnp.where(same & ((entry & 7) == xx // 2 + 2), 1.0, 0.0).astype(F32)
            chosen = jnp.dot(low, pick_low, preferred_element_type=F32) + jnp.dot(
                high, pick_high, preferred_element_type=F32
            )
            cm[:, n * 512:(n + 1) * 512] = jnp.where(chosen > 0.5, coef, 0.0)

    def mask_columns_t():
        every = masks[...].reshape(64, HALF)
        entry = lax.broadcasted_iota(jnp.int32, (HALF, 512), 0)
        slot = lax.broadcasted_iota(jnp.int32, (HALF, 512), 1) >> 6
        off = jnp.where((slot & 1) == 1, (slot + 1) >> 1, (8 - (slot >> 1)) & 7)
        for h in range(2):
            core_of = c if h == 0 else 1 - c
            tile = ((z * NY + ((y + off) & 7)) * 2 + core_of) * 2 + x // 2
            low = jnp.dot(every, (tile == entry).astype(F32), preferred_element_type=F32)
            high = jnp.dot(every, (tile == entry + HALF).astype(F32), preferred_element_type=F32)
            cm_low[:, h * 512:(h + 1) * 512] = jnp.where(low > 0.5, coef, 0.0)
            cm_high[:, h * 512:(h + 1) * 512] = jnp.where(high > 0.5, coef, 0.0)

    def column_ids(n):
        return ((((z + col_off) & 7) * NY + y) * 2 + c) * 256 + columns_x[n] * ROWS + (col_j & 63)

    def column_ids_t(h):
        core_of = c if h == 0 else 1 - c
        return ((z * NY + ((y + col_off) & 7)) * 2 + core_of) * 256 + x * ROWS + (col_j & 63)

    def prepare(unit, a, b):
        first = fold(fold(a * b))
        hashed = reduce_once(fold(fold(first * 20011 + (a + b) * 7919)))
        starts[unit] = hashed.astype(F32) * SCALE - 1.0

    def prepare_steps(number, b, stride):
        step = reduce_once(fold(fold(b[0:8] * 20011 + 7919)))
        steps[number, 0] = reduce_once(fold(step * 16)).astype(F32) * SCALE
        steps[number, 1] = reduce_once(fold(step * stride)).astype(F32) * SCALE

    def prepare_block():
        for n in range(NX):
            b = column_ids(n)
            prepare_steps(n, b, 512)
            for side in range(2):
                a = ((z * NY) * 2 + side_core(side)) * 256 + x * ROWS + row_i
                prepare(n * 2 + side, a, b)

    def prepare_block_t():
        for h in range(2):
            b = column_ids_t(h)
            prepare_steps(NX + h, b, 4096)
            for n in range(NX):
                a = (y * 2 + c) * 256 + columns_x[n] * ROWS + row_i
                prepare(8 + n * 2 + h, a, b)

    def make(unit, number, target, top, lanes, coefs_of):
        step16 = jnp.concatenate([steps[number, 0]] * 2, axis=0)
        leap = jnp.concatenate([steps[number, 1]] * 2, axis=0)

        def run(turn, u0):
            coefs = coefs_of(turn)
            u = u0
            for s in range(4):
                at = pl.multiple_of(top + turn * ROWS + s * 16, 16)
                target[pl.ds(at, 16), lanes] = (u * coefs).astype(BF16)
                if s < 3:
                    u = add_wrapped(u, step16)
            return add_wrapped(u0, leap)

        lax.fori_loop(0, 8, run, starts[unit])

    def make_block(n, side):
        lanes = slice(n * 512, (n + 1) * 512)
        make(n * 2 + side, n, adj, side * 512, lanes, lambda yy: cm[pl.ds(side * 8 + yy, 1), lanes])

    def make_block_t(n, h):
        lanes = slice(h * 512, (h + 1) * 512)
        tile = columns_x[n] // 2

        def coefs_of(zz):
            low = cm_low[pl.ds(zz * 8 + tile, 1), lanes]
            return low + cm_high[pl.ds(zz * 8 + tile + 2, 1), lanes]

        make(8 + n * 2 + h, NX + h, adj_t, n * 512, lanes, coefs_of)

    prepare_block_t()

    for one in loads[:3]:
        one.wait()
    row = scale_row[...].astype(F32)
    pick = lax.broadcasted_iota(jnp.int32, (ROWS, ROWS), 0) == lax.broadcasted_iota(
        jnp.int32, (ROWS, ROWS), 1
    )
    column = jnp.sum(jnp.where(pick, jnp.broadcast_to(row, (ROWS, ROWS)), 0.0), axis=1, keepdims=True)
    scale_col[...] = jnp.broadcast_to(column, (ROWS, 256))
    scaled = (scale_col[...] * feats[...].astype(F32)).astype(BF16)
    gath[0, 0, 0:ROWS] = scaled[:, :HALF]
    gath_t[0, 0, 0:ROWS] = scaled[:, HALF:]
    masks[z] = jnp.zeros((8, HALF), F32)
    masks[z, 0:2, :] = mask[:, 0:HALF].astype(F32)
    masks[z, 2:4, :] = mask[:, HALF:].astype(F32)

    pl.semaphore_wait(barrier, len(peers))

    def start_pass(p):
        own = gath.at[p, 0, pl.ds(0, ROWS)]
        own_t = gath_t.at[p, 0, pl.ds(0, ROWS)]
        state = {"z": {}, "one": {}, "two": {}, "opp": [], "y_t": {}, "core_t": []}
        for k in range(1, NZ):
            e = (NZ - OFFSET[k]) % NZ
            run = pl.ds(k * ROWS, ROWS)
            state["z"][k] = copy(own, gath.at[p, 0, run], z_peer(e))
            state["y_t"][k] = copy(own_t, gath_t.at[p, 0, run], y_peer(e))
            if k == 2:
                forward(p, 0, state)
                forward_t(p, 0, state)
        return state

    def forward_t(p, g, state):
        lo, hi = GROUPS[g]
        for k in range(lo, hi):
            if k:
                state["y_t"][k].wait_recv()
        run = pl.ds(lo * ROWS, (hi - lo) * ROWS)
        state["core_t"].append(copy(gath_t.at[p, 0, run], gath_t.at[p, 1, run], sibling))

    def forward(p, g, state):
        lo, hi = GROUPS[g]
        for k in range(lo, hi):
            if k:
                state["z"][k].wait_recv()
        run = pl.ds(lo * ROWS, (hi - lo) * ROWS)
        state["one"][g] = copy(gath.at[p, 0, run], gath.at[p, 1, run], east)
        state["two"][g] = copy(gath.at[p, 0, run], gath.at[p, 2, run], west)

    def relay(p, g, state):
        lo, hi = GROUPS[g]
        size = (hi - lo) * ROWS // 2
        run = pl.ds(lo * ROWS, size)
        state["two"][g].wait_recv()
        state["opp"].append(copy(gath.at[p, 2, run], gath.at[p, 3, run], east))
        run = pl.ds(lo * ROWS + size, size)
        state["one"][g].wait_recv()
        state["opp"].append(copy(gath.at[p, 1, run], gath.at[p, 3, run], west))

    def finish_gather(state):
        for one in state["opp"]:
            one.wait_recv()

    def product(p, side):
        right = gath[p].reshape(NX * NZ * ROWS, HALF)
        value = jnp.dot(adj[side * 512:(side + 1) * 512, :], right, preferred_element_type=F32)
        if side == 0:
            csend[p] = value.astype(BF16)
        else:
            acc[...] = value

    def sums_first(p, state):
        product(p, 0)
        state["core"] = copy(csend.at[p], crecv.at[p], sibling)

    def sums_second(p, state):
        state["core"].wait_recv()
        total = acc[...] + crecv[p].astype(F32)
        acc[...] = total
        ysend[p] = total.astype(BF16)
        state["y"] = {}
        for e in (4, 3, 5, 2, 6, 1, 7):
            at = pl.multiple_of(((y + e) % NY) * ROWS, ROWS)
            state["y"][e] = copy(ysend.at[p, pl.ds(at, ROWS)], yrecv.at[p, e], y_peer(e))

    def sums_last(p, state):
        total = acc[pl.ds(pl.multiple_of(y * ROWS, ROWS), ROWS), :]
        for e in (1, 7, 2, 6, 3, 5, 4):
            state["y"][e].wait_recv()
            total = total + yrecv[p, e].astype(F32)
        return total

    def product_t(p, lo, hi):
        right = gath_t[p].reshape(2 * NY * ROWS, HALF)
        return jnp.dot(adj_t[lo:hi, :], right, preferred_element_type=F32)

    def near_first(p, state):
        for one in state["core_t"]:
            one.wait_recv()
        opposite = product_t(p, 1536, 2048)
        near_send[p, 0, 256:512] = opposite[:256].astype(BF16)
        near_send[p, 1, 256:512] = opposite[256:].astype(BF16)
        far, close = pl.ds(256, 256), pl.ds(0, 256)
        state["far_e"] = copy(near_send.at[p, 0, far], near_recv.at[p, 0, far], east)
        state["far_w"] = copy(near_send.at[p, 1, far], near_recv.at[p, 1, far], west)
        near_send[p, 0, 0:256] = product_t(p, 512, 768).astype(BF16)
        state["near_e"] = copy(near_send.at[p, 0, close], near_recv.at[p, 0, close], east)
        near_send[p, 1, 0:256] = product_t(p, 1280, 1536).astype(BF16)
        state["near_w"] = copy(near_send.at[p, 1, close], near_recv.at[p, 1, close], west)

    def near_second(p):
        keep_near[0] = product_t(p, 1024, 1280)
        keep_near[1] = product_t(p, 768, 1024)

    def next_first(p, state):
        state["far_e"].wait_recv()
        next_send[p, 0] = (keep_near[0] + near_recv[p, 0, 256:512].astype(F32)).astype(BF16)
        state["next_w"] = copy(next_send.at[p, 0], next_recv.at[p, 0], west)
        state["far_w"].wait_recv()
        next_send[p, 1] = (keep_near[1] + near_recv[p, 1, 256:512].astype(F32)).astype(BF16)
        state["next_e"] = copy(next_send.at[p, 1], next_recv.at[p, 1], east)
        value = product_t(p, 0, 512)
        state["near_e"].wait_recv()
        state["near_w"].wait_recv()
        keep[0:256] = value[:256] + near_recv[p, 0, 0:256].astype(F32)
        keep[256:512] = value[256:] + near_recv[p, 1, 0:256].astype(F32)

    def next_second(p, state):
        state["next_w"].wait_recv()
        state["next_e"].wait_recv()
        total = keep[...] + next_recv[p].reshape(512, HALF).astype(F32)
        keep[...] = total
        zsend[p] = total.astype(BF16)
        state["z_t"] = {}
        for e in (4, 3, 5, 2, 6, 1, 7):
            at = pl.multiple_of(((z + e) % NZ) * ROWS, ROWS)
            state["z_t"][e] = copy(zsend.at[p, pl.ds(at, ROWS)], zrecv.at[p, e], z_peer(e))

    def sums_last_t(p, state):
        total = keep[pl.ds(pl.multiple_of(z * ROWS, ROWS), ROWS), :]
        for e in (1, 7, 2, 6, 3, 5, 4):
            state["z_t"][e].wait_recv()
            total = total + zrecv[p, e].astype(F32)
        return total

    mask_copies = [copy(masks.at[z], masks.at[z], z_peer(e)) for e in range(1, NZ)]
    state = start_pass(0)
    prepare_block()
    for one in mask_copies:
        one.wait_recv()
    forward(0, 1, state)
    forward_t(0, 1, state)
    relay(0, 0, state)
    mask_columns_t()
    make_block_t(3, 0)
    make_block_t(3, 1)
    forward(0, 2, state)
    forward_t(0, 2, state)
    relay(0, 1, state)
    make_block_t(1, 0)
    make_block_t(1, 1)
    make_block_t(2, 0)
    forward(0, 3, state)
    forward_t(0, 3, state)
    relay(0, 2, state)
    make_block_t(2, 1)
    mask_columns()
    for n in range(3):
        make_block(n, 0)
    near_first(0, state)
    relay(0, 3, state)
    near_second(0)
    make_block(3, 0)
    make_block_t(0, 0)
    make_block_t(0, 1)
    make_block(0, 1)
    make_block(1, 1)
    next_first(0, state)
    finish_gather(state)
    sums_first(0, state)
    make_block(2, 1)
    make_block(3, 1)
    product(0, 1)
    sums_second(0, state)
    next_second(0, state)
    sums = jnp.concatenate([sums_last(0, state), sums_last_t(0, state)], axis=1)

    for one in loads[3:]:
        one.wait()
    sums_high = sums.astype(BF16)
    sums_low = (sums - sums_high.astype(F32)).astype(BF16)
    scale = scale_col[...]
    presum = scale * (
        jnp.dot(sums_high, weight[...], preferred_element_type=F32)
        + jnp.dot(sums_low, weight[...], preferred_element_type=F32)
    )
    sigma = jax.nn.sigmoid(presum)
    layer_out[...] = (presum * sigma).astype(BF16)
    deriv = sigma * (1.0 + presum * (1.0 - sigma))
    error = (scale * cot[...].astype(F32) * deriv).astype(BF16)
    gath[1, 0, 0:ROWS] = error[:, :HALF]
    gath_t[1, 0, 0:ROWS] = error[:, HALF:]

    state = start_pass(1)
    part[...] = lax.dot_general(
        sums_high, error, (((0,), (0,)), ((), ())), preferred_element_type=F32
    )
    theirs = pl.multiple_of((1 - c) * 128, 128)
    mine = pl.multiple_of(c * 128, 128)
    a1s[...] = part[pl.ds(theirs, 128), :].astype(BF16)
    first = copy(a1s, a1r, sibling)
    forward(1, 1, state)
    forward_t(1, 1, state)
    relay(1, 0, state)

    first.wait_recv()
    half[...] = part[pl.ds(mine, 128), :] + a1r[...].astype(F32)
    a2s[...] = half[...].astype(BF16)
    second = []
    for e in range(1, NY):
        at = pl.multiple_of(((y + e) % NY) * 16, 16)
        second.append(copy(a2s.at[pl.ds(at, 16)], a2r.at[e], y_peer(e)))

    forward(1, 2, state)
    forward_t(1, 2, state)
    relay(1, 1, state)
    forward(1, 3, state)
    forward_t(1, 3, state)
    relay(1, 2, state)

    piece = half[pl.ds(pl.multiple_of(y * 16, 16), 16), :]
    for e in range(1, NY):
        second[e - 1].wait_recv()
        piece = piece + a2r[e].astype(F32)
    a3r[z] = piece.astype(BF16)
    third = [copy(a3r.at[z], a3r.at[z], z_peer(e)) for e in range(1, NZ)]

    near_first(1, state)
    relay(1, 3, state)
    near_second(1)

    for one in third:
        one.wait_recv()
    piece = a3r[0].astype(F32)
    for n in range(1, NZ):
        piece = piece + a3r[n].astype(F32)
    a4r[x] = piece
    fourth = [copy(a4r.at[x], a4r.at[x], x_peer(e)) for e in range(1, NX)]

    next_first(1, state)
    finish_gather(state)
    sums_first(1, state)
    product(1, 1)

    for one in fourth:
        one.wait_recv()
    piece = (a4r[0] + a4r[1]) + (a4r[2] + a4r[3])
    at = pl.multiple_of(c * 128 + y * 16, 16)
    wbuf[pl.ds(at, 16), :] = piece.astype(BF16)
    fifth = [copy(wbuf.at[pl.ds(at, 16)], wbuf.at[pl.ds(at, 16)], y_peer(e)) for e in range(1, NY)]

    sums_second(1, state)
    next_second(1, state)
    for one in fifth:
        one.wait_recv()
    sixth = copy(wbuf.at[pl.ds(mine, 128)], wbuf.at[pl.ds(mine, 128)], sibling)
    back = jnp.concatenate([sums_last(1, state), sums_last_t(1, state)], axis=1)
    vgrad = (scale * back).astype(BF16)
    grad_feats[...] = lax.dot_general(
        vgrad, weight[...], (((1,), (1,)), ((), ())), preferred_element_type=F32
    ).astype(BF16)
    sixth.wait_recv()
    grad_weight[...] = wbuf[...].astype(F32)
    for one in started:
        one.wait_send()


def deliver(*refs):
    sems = refs[-1]
    copies = [pltpu.make_async_copy(refs[n], refs[n + 3], sems.at[n]) for n in range(3)]
    for one in copies:
        one.start()
    for one in copies:
        one.wait()


def local(node_feats, weight, node_scale, tile_mask, cotangent, coef):
    hidden = weight.shape[0]
    hbm = pl.BlockSpec(memory_space=pltpu.HBM)
    vmem = pl.BlockSpec(memory_space=pltpu.VMEM)
    shapes = (((ROWS, hidden), BF16), ((ROWS, hidden), BF16), ((hidden, hidden), F32))
    args = (node_feats, weight, node_scale.reshape(1, ROWS), tile_mask, cotangent)
    made = pl.pallas_call(
        functools.partial(kernel, coef),
        out_shape=tuple(pltpu.VMEM(*shape) for shape in shapes),
        in_specs=[hbm] * 5,
        out_specs=(vmem,) * 3,
        scratch_shapes=[
            pltpu.VMEM((ROWS, hidden), BF16),
            pltpu.VMEM((hidden, hidden), BF16),
            pltpu.VMEM((1, ROWS), BF16),
            pltpu.VMEM(tile_mask.shape, jnp.int32),
            pltpu.VMEM((ROWS, hidden), BF16),
            pltpu.SemaphoreType.DMA((5,)),
            pltpu.VMEM((1024, 2048), BF16),
            pltpu.VMEM((2048, 1024), BF16),
            pltpu.VMEM((16, 2048), F32),
            pltpu.VMEM((64, 1024), F32),
            pltpu.VMEM((64, 1024), F32),
            pltpu.VMEM((2, NX, NZ * ROWS, HALF), BF16),
            pltpu.VMEM((2, 2, NY * ROWS, HALF), BF16),
            pltpu.VMEM((NZ, 8, HALF), F32),
            pltpu.VMEM((2, 512, HALF), BF16),
            pltpu.VMEM((2, 512, HALF), BF16),
            pltpu.VMEM((512, HALF), F32),
            pltpu.VMEM((2, 512, HALF), BF16),
            pltpu.VMEM((2, NY, ROWS, HALF), BF16),
            pltpu.VMEM((2, 2, 512, HALF), BF16),
            pltpu.VMEM((2, 2, 512, HALF), BF16),
            pltpu.VMEM((512, HALF), F32),
            pltpu.VMEM((2, 256, HALF), F32),
            pltpu.VMEM((2, 2, 256, HALF), BF16),
            pltpu.VMEM((2, 2, 256, HALF), BF16),
            pltpu.VMEM((2, 512, HALF), BF16),
            pltpu.VMEM((2, NZ, ROWS, HALF), BF16),
            pltpu.VMEM((16, 16, 512), F32),
            pltpu.VMEM((NX + 2, 2, 8, 512), F32),
            pltpu.VMEM((256, 256), F32),
            pltpu.VMEM((128, 256), BF16),
            pltpu.VMEM((128, 256), BF16),
            pltpu.VMEM((128, 256), F32),
            pltpu.VMEM((128, 256), BF16),
            pltpu.VMEM((NY, 16, 256), BF16),
            pltpu.VMEM((NZ, 16, 256), BF16),
            pltpu.VMEM((NX, 16, 256), F32),
            pltpu.VMEM((256, 256), BF16),
            pltpu.VMEM((ROWS, 256), F32),
            pltpu.SemaphoreType.DMA((COPIES,)),
            pltpu.SemaphoreType.DMA((COPIES,)),
        ],
        compiler_params=pltpu.CompilerParams(
            collective_id=0, has_side_effects=True, vmem_limit_bytes=40 * 1024 * 1024
        ),
    )(*(pltpu.with_memory_space_constraint(arg, pltpu.HBM) for arg in args))
    return pl.pallas_call(
        deliver,
        out_shape=tuple(jax.ShapeDtypeStruct(*shape) for shape in shapes),
        in_specs=[vmem] * 3,
        out_specs=(hbm,) * 3,
        scratch_shapes=[pltpu.SemaphoreType.DMA((3,))],
        compiler_params=pltpu.CompilerParams(vmem_limit_bytes=8 * 1024 * 1024),
    )(*(pltpu.with_memory_space_constraint(one, pltpu.VMEM) for one in made))


def solution(mesh):
    in_specs = (
        P(("section", "rep"), None),
        P(),
        P(("section", "rep")),
        P("section", None),
        P(("section", "rep"), None),
    )
    out_specs = (P(("section", "rep"), None), P(("section", "rep"), None), P())
    coef = 4.0 / math.sqrt(128 * 256)
    return jax.shard_map(
        functools.partial(local, coef=coef), mesh=mesh, in_specs=in_specs, out_specs=out_specs,
        check_vma=False,
    )
```

```python
import functools
import math

import jax
import jax.numpy as jnp
from jax import lax
from jax.experimental import pallas as pl
from jax.experimental.pallas import tpu as pltpu
from jax.sharding import PartitionSpec as P


MESH = pl.DeviceIdType.MESH
NZ, NY, NX = 8, 8, 4
ROWS = 64
HALF = 128
MODULUS = 65521
OFFSET = (0, 1, 7, 2, 6, 3, 5, 4)
SLOT = {off: k for k, off in enumerate(OFFSET)}
GROUPS = ((0, 1), (1, 5), (5, 8))
COPIES = 160
BF16 = jnp.bfloat16
F32 = jnp.float32


def fold(v):
    return (v & 0xFFFF) + 15 * (v >> 16)


def reduce_once(v):
    return jnp.where(v >= MODULUS, v - MODULUS, v)


SCALE = 2.0 / MODULUS
WRAP = 1.0 - 0.5 * SCALE


def add_wrapped(u, step):
    total = u + step
    return jnp.where(total >= WRAP, total - 2.0, total)


def kernel(
    coef,
    feats_hbm, weight_hbm, scale_hbm, mask_hbm, cot_hbm,
    layer_out, grad_feats, grad_weight,
    feats, weight, scale_row, mask, cot, load_sems,
    adj, adj_t, cm, cm_low, cm_high, gath, gath_t, masks, csend, crecv, acc, ysend, yrecv,
    near_send, near_recv, keep, keep_near, next_send, next_recv, zsend, zrecv,
    starts, steps, part, a1r, half, a2s, a2r, a3r, a4r, wbuf, scale_col,
    send_sems, recv_sems,
):
    sec = lax.axis_index("section")
    x = lax.axis_index("rep")
    c = sec % 2
    y = (sec // 2) % NY
    z = sec // (2 * NY)
    x_one = x + 1 - 2 * (x % 2)
    x_two = 3 - x
    x_opp = (x + 2) % NX

    def device(zz, yy, cc, xx):
        return ((zz * NY + yy) * 2 + cc, xx)

    sibling = device(z, y, 1 - c, x)
    east, west = device(z, y, c, x_one), device(z, y, c, x_two)

    def z_peer(e):
        return device((z + e) % NZ, y, c, x)

    def y_peer(e):
        return device(z, (y + e) % NY, c, x)

    def x_peer(e):
        return device(z, y, c, (x + e) % NX)

    loads = [
        pltpu.make_async_copy(src, dst, load_sems.at[n])
        for n, (src, dst) in enumerate((
            (feats_hbm, feats), (scale_hbm, scale_row), (mask_hbm, mask),
            (weight_hbm, weight), (cot_hbm, cot),
        ))
    ]
    for one in loads:
        one.start()

    barrier = pltpu.get_barrier_semaphore()
    peers = [z_peer(e) for e in range(1, NZ)] + [y_peer(e) for e in range(1, NY)]
    peers += [x_peer(e) for e in range(1, NX)] + [sibling]
    for peer in peers:
        pl.semaphore_signal(barrier, inc=1, device_id=peer, device_id_type=MESH)

    started = []

    def copy(src, dst, target):
        number = len(started)
        one = pltpu.make_async_remote_copy(
            src_ref=src, dst_ref=dst, send_sem=send_sems.at[number],
            recv_sem=recv_sems.at[number], device_id=target, device_id_type=MESH,
        )
        one.start()
        started.append(one)
        return one

    col_j = lax.broadcasted_iota(jnp.int32, (16, 512), 1)
    row_i = lax.broadcasted_iota(jnp.int32, (16, 512), 0)
    col_slot = col_j >> 6
    col_off = jnp.where((col_slot & 1) == 1, (col_slot + 1) >> 1, (8 - (col_slot >> 1)) & 7)
    columns_x = (x, x_one, x_two, x_opp)

    def side_core(side):
        return 1 - c if side == 0 else c

    def mask_columns():
        which = lax.broadcasted_iota(jnp.int32, (16, HALF), 0)
        lane = lax.broadcasted_iota(jnp.int32, (16, HALF), 1)
        core_of = jnp.where(which < 8, 1 - c, c)
        tile = ((z * NY + (which & 7)) * 2 + core_of) * 2 + x // 2
        every = masks[...].reshape(64, HALF)
        dims = (((1,), (1,)), ((), ()))
        low = lax.dot_general((tile == lane).astype(F32), every, dims, preferred_element_type=F32)
        high = lax.dot_general(
            (tile == lane + HALF).astype(F32), every, dims, preferred_element_type=F32
        )
        entry = lax.broadcasted_iota(jnp.int32, (64, 512), 0)
        slot = lax.broadcasted_iota(jnp.int32, (64, 512), 1) >> 6
        off = jnp.where((slot & 1) == 1, (slot + 1) >> 1, (8 - (slot >> 1)) & 7)
        same = (entry >> 3) == ((z + off) & 7)
        for n, xx in enumerate(columns_x):
            pick_low = jnp.where(same & ((entry & 7) == xx // 2), 1.0, 0.0).astype(F32)
            pick_high = jnp.where(same & ((entry & 7) == xx // 2 + 2), 1.0, 0.0).astype(F32)
            chosen = jnp.dot(low, pick_low, preferred_element_type=F32) + jnp.dot(
                high, pick_high, preferred_element_type=F32
            )
            cm[:, n * 512:(n + 1) * 512] = jnp.where(chosen > 0.5, coef, 0.0)

    def mask_columns_t():
        every = masks[...].reshape(64, HALF)
        entry = lax.broadcasted_iota(jnp.int32, (HALF, 512), 0)
        slot = lax.broadcasted_iota(jnp.int32, (HALF, 512), 1) >> 6
        off = jnp.where((slot & 1) == 1, (slot + 1) >> 1, (8 - (slot >> 1)) & 7)
        for h in range(2):
            core_of = c if h == 0 else 1 - c
            tile = ((z * NY + ((y + off) & 7)) * 2 + core_of) * 2 + x // 2
            low = jnp.dot(every, (tile == entry).astype(F32), preferred_element_type=F32)
            high = jnp.dot(every, (tile == entry + HALF).astype(F32), preferred_element_type=F32)
            cm_low[:, h * 512:(h + 1) * 512] = jnp.where(low > 0.5, coef, 0.0)
            cm_high[:, h * 512:(h + 1) * 512] = jnp.where(high > 0.5, coef, 0.0)

    def column_ids(n):
        return ((((z + col_off) & 7) * NY + y) * 2 + c) * 256 + columns_x[n] * ROWS + (col_j & 63)

    def column_ids_t(h):
        core_of = c if h == 0 else 1 - c
        return ((z * NY + ((y + col_off) & 7)) * 2 + core_of) * 256 + x * ROWS + (col_j & 63)

    def prepare(unit, a, b):
        first = fold(fold(a * b))
        hashed = reduce_once(fold(fold(first * 20011 + (a + b) * 7919)))
        starts[unit] = hashed.astype(F32) * SCALE - 1.0

    def prepare_steps(number, b, stride):
        step = reduce_once(fold(fold(b[0:8] * 20011 + 7919)))
        steps[number, 0] = reduce_once(fold(step * 16)).astype(F32) * SCALE
        steps[number, 1] = reduce_once(fold(step * stride)).astype(F32) * SCALE

    def prepare_block():
        for n in range(NX):
            b = column_ids(n)
            prepare_steps(n, b, 512)
            for side in range(2):
                a = ((z * NY) * 2 + side_core(side)) * 256 + x * ROWS + row_i
                prepare(n * 2 + side, a, b)

    def prepare_block_t():
        for h in range(2):
            b = column_ids_t(h)
            prepare_steps(NX + h, b, 4096)
            for n in range(NX):
                a = (y * 2 + c) * 256 + columns_x[n] * ROWS + row_i
                prepare(8 + n * 2 + h, a, b)

    def make(unit, number, target, top, lanes, coefs_of):
        step16 = jnp.concatenate([steps[number, 0]] * 2, axis=0)
        leap = jnp.concatenate([steps[number, 1]] * 2, axis=0)

        def run(turn, u0):
            coefs = coefs_of(turn)
            u = u0
            for s in range(4):
                at = pl.multiple_of(top + turn * ROWS + s * 16, 16)
                target[pl.ds(at, 16), lanes] = (u * coefs).astype(BF16)
                if s < 3:
                    u = add_wrapped(u, step16)
            return add_wrapped(u0, leap)

        lax.fori_loop(0, 8, run, starts[unit])

    def make_block(n, side):
        lanes = slice(n * 512, (n + 1) * 512)
        make(n * 2 + side, n, adj, side * 512, lanes, lambda yy: cm[pl.ds(side * 8 + yy, 1), lanes])

    def make_block_t(n, h):
        lanes = slice(h * 512, (h + 1) * 512)
        tile = columns_x[n] // 2

        def coefs_of(zz):
            low = cm_low[pl.ds(zz * 8 + tile, 1), lanes]
            return low + cm_high[pl.ds(zz * 8 + tile + 2, 1), lanes]

        make(8 + n * 2 + h, NX + h, adj_t, n * 512, lanes, coefs_of)

    for one in loads[:3]:
        one.wait()
    row = scale_row[...].astype(F32)
    pick = lax.broadcasted_iota(jnp.int32, (ROWS, ROWS), 0) == lax.broadcasted_iota(
        jnp.int32, (ROWS, ROWS), 1
    )
    column = jnp.sum(jnp.where(pick, jnp.broadcast_to(row, (ROWS, ROWS)), 0.0), axis=1, keepdims=True)
    scale_col[...] = jnp.broadcast_to(column, (ROWS, 256))
    scaled = (scale_col[...] * feats[...].astype(F32)).astype(BF16)
    gath[0, 0, 0:ROWS] = scaled[:, :HALF]
    gath_t[0, 0, 0:ROWS] = scaled[:, HALF:]
    masks[z] = jnp.zeros((8, HALF), F32)
    masks[z, 0:2, :] = mask[:, 0:HALF].astype(F32)
    masks[z, 2:4, :] = mask[:, HALF:].astype(F32)

    pl.semaphore_wait(barrier, len(peers))

    def start_pass(p):
        own = gath.at[p, 0, pl.ds(0, ROWS)]
        own_t = gath_t.at[p, 0, pl.ds(0, ROWS)]
        state = {"z": {}, "one": {}, "two": {}, "opp": [], "y_t": {}, "core_t": []}
        for k in range(1, NZ):
            e = (NZ - OFFSET[k]) % NZ
            state["z"][k] = copy(own, gath.at[p, 0, pl.ds(k * ROWS, ROWS)], z_peer(e))
            far = NY - k
            e = (NY - OFFSET[far]) % NY
            state["y_t"][far] = copy(own_t, gath_t.at[p, 0, pl.ds(far * ROWS, ROWS)], y_peer(e))
            if k == 2:
                forward(p, 0, state)
        return state

    def forward_t(p, state):
        for k in range(NY - 1, 0, -1):
            state["y_t"][k].wait_recv()
        state["core_t"].append(copy(gath_t.at[p, 0], gath_t.at[p, 1], sibling))

    def forward(p, g, state):
        lo, hi = GROUPS[g]
        for k in range(lo, hi):
            if k:
                state["z"][k].wait_recv()
        run = pl.ds(lo * ROWS, (hi - lo) * ROWS)
        state["one"][g] = copy(gath.at[p, 0, run], gath.at[p, 1, run], east)
        state["two"][g] = copy(gath.at[p, 0, run], gath.at[p, 2, run], west)

    def relay(p, g, state):
        lo, hi = GROUPS[g]
        size = (hi - lo) * ROWS // 2
        run = pl.ds(lo * ROWS, size)
        state["two"][g].wait_recv()
        state["opp"].append(copy(gath.at[p, 2, run], gath.at[p, 3, run], east))
        run = pl.ds(lo * ROWS + size, size)
        state["one"][g].wait_recv()
        state["opp"].append(copy(gath.at[p, 1, run], gath.at[p, 3, run], west))

    def finish_gather(state):
        for one in state["opp"]:
            one.wait_recv()

    def product(p, side):
        right = gath[p].reshape(NX * NZ * ROWS, HALF)
        value = jnp.dot(adj[side * 512:(side + 1) * 512, :], right, preferred_element_type=F32)
        if side == 0:
            csend[p] = value.astype(BF16)
        else:
            acc[...] = value

    def sums_first(p, state):
        product(p, 0)
        state["core"] = copy(csend.at[p], crecv.at[p], sibling)

    def sums_second(p, state):
        state["core"].wait_recv()
        total = acc[...] + crecv[p].astype(F32)
        acc[...] = total
        ysend[p] = total.astype(BF16)
        state["y"] = {}
        for e in (4, 3, 5, 2, 6, 1, 7):
            at = pl.multiple_of(((y + e) % NY) * ROWS, ROWS)
            state["y"][e] = copy(ysend.at[p, pl.ds(at, ROWS)], yrecv.at[p, e], y_peer(e))

    def sums_last(p, state):
        total = acc[pl.ds(pl.multiple_of(y * ROWS, ROWS), ROWS), :]
        for e in (1, 7, 2, 6, 3, 5, 4):
            state["y"][e].wait_recv()
            total = total + yrecv[p, e].astype(F32)
        return total

    def product_t(p, lo, hi):
        right = gath_t[p].reshape(2 * NY * ROWS, HALF)
        return jnp.dot(adj_t[lo:hi, :], right, preferred_element_type=F32)

    def near_first(p, state):
        for one in state["core_t"]:
            one.wait_recv()
        opposite = product_t(p, 1536, 2048)
        near_send[p, 0, 256:512] = opposite[:256].astype(BF16)
        near_send[p, 1, 256:512] = opposite[256:].astype(BF16)
        far, close = pl.ds(256, 256), pl.ds(0, 256)
        state["far_e"] = copy(near_send.at[p, 0, far], near_recv.at[p, 0, far], east)
        state["far_w"] = copy(near_send.at[p, 1, far], near_recv.at[p, 1, far], west)
        near_send[p, 0, 0:256] = product_t(p, 512, 768).astype(BF16)
        state["near_e"] = copy(near_send.at[p, 0, close], near_recv.at[p, 0, close], east)
        near_send[p, 1, 0:256] = product_t(p, 1280, 1536).astype(BF16)
        state["near_w"] = copy(near_send.at[p, 1, close], near_recv.at[p, 1, close], west)

    def near_second(p):
        keep_near[0] = product_t(p, 1024, 1280)
        keep_near[1] = product_t(p, 768, 1024)

    def next_first(p, state):
        state["far_e"].wait_recv()
        next_send[p, 0] = (keep_near[0] + near_recv[p, 0, 256:512].astype(F32)).astype(BF16)
        state["next_w"] = copy(next_send.at[p, 0], next_recv.at[p, 0], west)
        state["far_w"].wait_recv()
        next_send[p, 1] = (keep_near[1] + near_recv[p, 1, 256:512].astype(F32)).astype(BF16)
        state["next_e"] = copy(next_send.at[p, 1], next_recv.at[p, 1], east)
        value = product_t(p, 0, 512)
        state["near_e"].wait_recv()
        state["near_w"].wait_recv()
        keep[0:256] = value[:256] + near_recv[p, 0, 0:256].astype(F32)
        keep[256:512] = value[256:] + near_recv[p, 1, 0:256].astype(F32)

    def next_second(p, state):
        state["next_w"].wait_recv()
        state["next_e"].wait_recv()
        total = keep[...] + next_recv[p].reshape(512, HALF).astype(F32)
        keep[...] = total
        zsend[p] = total.astype(BF16)
        state["z_t"] = {}
        for e in (4, 3, 5, 2, 6, 1, 7):
            at = pl.multiple_of(((z + e) % NZ) * ROWS, ROWS)
            state["z_t"][e] = copy(zsend.at[p, pl.ds(at, ROWS)], zrecv.at[p, e], z_peer(e))

    def sums_last_t(p, state):
        total = keep[pl.ds(pl.multiple_of(z * ROWS, ROWS), ROWS), :]
        for e in (1, 7, 2, 6, 3, 5, 4):
            state["z_t"][e].wait_recv()
            total = total + zrecv[p, e].astype(F32)
        return total

    mask_copies = [copy(masks.at[z], masks.at[z], z_peer(e)) for e in range(1, NZ)]
    state = start_pass(0)
    prepare_block_t()
    prepare_block()
    for one in mask_copies:
        one.wait_recv()
    mask_columns_t()
    make_block_t(3, 0)
    relay(0, 0, state)
    make_block_t(3, 1)
    forward(0, 1, state)
    make_block_t(1, 0)
    make_block_t(1, 1)
    forward_t(0, state)
    forward(0, 2, state)
    relay(0, 1, state)
    make_block_t(2, 0)
    make_block_t(2, 1)
    mask_columns()
    make_block(0, 0)
    near_first(0, state)
    relay(0, 2, state)
    near_second(0)
    make_block(1, 0)
    make_block(2, 0)
    make_block(3, 0)
    make_block_t(0, 0)
    make_block_t(0, 1)
    make_block(0, 1)
    next_first(0, state)
    finish_gather(state)
    sums_first(0, state)
    make_block(1, 1)
    make_block(2, 1)
    make_block(3, 1)
    product(0, 1)
    sums_second(0, state)
    next_second(0, state)
    sums = jnp.concatenate([sums_last(0, state), sums_last_t(0, state)], axis=1)

    for one in loads[3:]:
        one.wait()
    sums_high = sums.astype(BF16)
    sums_low = (sums - sums_high.astype(F32)).astype(BF16)
    scale = scale_col[...]
    presum = scale * (
        jnp.dot(sums_high, weight[...], preferred_element_type=F32)
        + jnp.dot(sums_low, weight[...], preferred_element_type=F32)
    )
    sigma = jax.nn.sigmoid(presum)
    layer_out[...] = (presum * sigma).astype(BF16)
    deriv = sigma * (1.0 + presum * (1.0 - sigma))
    error = (scale * cot[...].astype(F32) * deriv).astype(BF16)
    gath[1, 0, 0:ROWS] = error[:, :HALF]
    gath_t[1, 0, 0:ROWS] = error[:, HALF:]

    state = start_pass(1)
    dims = (((0,), (0,)), ((), ()))
    part[...] = lax.dot_general(
        sums_high, error, dims, preferred_element_type=F32
    ) + lax.dot_general(sums_low, error, dims, preferred_element_type=F32)
    theirs = pl.multiple_of((1 - c) * 128, 128)
    mine = pl.multiple_of(c * 128, 128)
    first = copy(part.at[pl.ds(theirs, 128)], a1r, sibling)
    relay(1, 0, state)
    forward(1, 1, state)

    first.wait_recv()
    half[...] = part[pl.ds(mine, 128), :] + a1r[...]
    a2s[...] = half[...].astype(BF16)
    second = []
    for e in range(1, NY):
        at = pl.multiple_of(((y + e) % NY) * 16, 16)
        second.append(copy(a2s.at[pl.ds(at, 16)], a2r.at[e], y_peer(e)))

    forward_t(1, state)
    forward(1, 2, state)
    relay(1, 1, state)
    near_first(1, state)

    piece = half[pl.ds(pl.multiple_of(y * 16, 16), 16), :]
    for e in range(1, NY):
        second[e - 1].wait_recv()
        piece = piece + a2r[e].astype(F32)
    a3r[z] = piece.astype(BF16)
    third = [copy(a3r.at[z], a3r.at[z], z_peer(e)) for e in range(1, NZ)]

    relay(1, 2, state)
    near_second(1)

    for one in third:
        one.wait_recv()
    piece = a3r[0].astype(F32)
    for n in range(1, NZ):
        piece = piece + a3r[n].astype(F32)
    a4r[x] = piece
    fourth = [copy(a4r.at[x], a4r.at[x], x_peer(e)) for e in range(1, NX)]

    next_first(1, state)
    finish_gather(state)
    sums_first(1, state)
    product(1, 1)

    for one in fourth:
        one.wait_recv()
    piece = (a4r[0] + a4r[1]) + (a4r[2] + a4r[3])
    at = pl.multiple_of(c * 128 + y * 16, 16)
    wbuf[pl.ds(at, 16), :] = piece.astype(BF16)
    fifth = [copy(wbuf.at[pl.ds(at, 16)], wbuf.at[pl.ds(at, 16)], y_peer(e)) for e in range(1, NY)]

    sums_second(1, state)
    next_second(1, state)
    for one in fifth:
        one.wait_recv()
    sixth = copy(wbuf.at[pl.ds(mine, 128)], wbuf.at[pl.ds(mine, 128)], sibling)
    back = jnp.concatenate([sums_last(1, state), sums_last_t(1, state)], axis=1)
    vgrad = (scale * back).astype(BF16)
    grad_feats[...] = lax.dot_general(
        vgrad, weight[...], (((1,), (1,)), ((), ())), preferred_element_type=F32
    ).astype(BF16)
    sixth.wait_recv()
    grad_weight[...] = wbuf[...].astype(F32)
    for one in started:
        one.wait_send()


def deliver(*refs):
    sems = refs[-1]
    copies = [pltpu.make_async_copy(refs[n], refs[n + 3], sems.at[n]) for n in range(3)]
    for one in copies:
        one.start()
    for one in copies:
        one.wait()


def local(node_feats, weight, node_scale, tile_mask, cotangent, coef):
    hidden = weight.shape[0]
    hbm = pl.BlockSpec(memory_space=pltpu.HBM)
    vmem = pl.BlockSpec(memory_space=pltpu.VMEM)
    shapes = (((ROWS, hidden), BF16), ((ROWS, hidden), BF16), ((hidden, hidden), F32))
    args = (node_feats, weight, node_scale.reshape(1, ROWS), tile_mask, cotangent)
    made = pl.pallas_call(
        functools.partial(kernel, coef),
        out_shape=tuple(pltpu.VMEM(*shape) for shape in shapes),
        in_specs=[hbm] * 5,
        out_specs=(vmem,) * 3,
        scratch_shapes=[
            pltpu.VMEM((ROWS, hidden), BF16),
            pltpu.VMEM((hidden, hidden), BF16),
            pltpu.VMEM((1, ROWS), BF16),
            pltpu.VMEM(tile_mask.shape, jnp.int32),
            pltpu.VMEM((ROWS, hidden), BF16),
            pltpu.SemaphoreType.DMA((5,)),
            pltpu.VMEM((1024, 2048), BF16),
            pltpu.VMEM((2048, 1024), BF16),
            pltpu.VMEM((16, 2048), F32),
            pltpu.VMEM((64, 1024), F32),
            pltpu.VMEM((64, 1024), F32),
            pltpu.VMEM((2, NX, NZ * ROWS, HALF), BF16),
            pltpu.VMEM((2, 2, NY * ROWS, HALF), BF16),
            pltpu.VMEM((NZ, 8, HALF), F32),
            pltpu.VMEM((2, 512, HALF), BF16),
            pltpu.VMEM((2, 512, HALF), BF16),
            pltpu.VMEM((512, HALF), F32),
            pltpu.VMEM((2, 512, HALF), BF16),
            pltpu.VMEM((2, NY, ROWS, HALF), BF16),
            pltpu.VMEM((2, 2, 512, HALF), BF16),
            pltpu.VMEM((2, 2, 512, HALF), BF16),
            pltpu.VMEM((512, HALF), F32),
            pltpu.VMEM((2, 256, HALF), F32),
            pltpu.VMEM((2, 2, 256, HALF), BF16),
            pltpu.VMEM((2, 2, 256, HALF), BF16),
            pltpu.VMEM((2, 512, HALF), BF16),
            pltpu.VMEM((2, NZ, ROWS, HALF), BF16),
            pltpu.VMEM((16, 16, 512), F32),
            pltpu.VMEM((NX + 2, 2, 8, 512), F32),
            pltpu.VMEM((256, 256), F32),
            pltpu.VMEM((128, 256), F32),
            pltpu.VMEM((128, 256), F32),
            pltpu.VMEM((128, 256), BF16),
            pltpu.VMEM((NY, 16, 256), BF16),
            pltpu.VMEM((NZ, 16, 256), BF16),
            pltpu.VMEM((NX, 16, 256), F32),
            pltpu.VMEM((256, 256), BF16),
            pltpu.VMEM((ROWS, 256), F32),
            pltpu.SemaphoreType.DMA((COPIES,)),
            pltpu.SemaphoreType.DMA((COPIES,)),
        ],
        compiler_params=pltpu.CompilerParams(
            collective_id=0, has_side_effects=True, vmem_limit_bytes=40 * 1024 * 1024
        ),
    )(*(pltpu.with_memory_space_constraint(arg, pltpu.HBM) for arg in args))
    return pl.pallas_call(
        deliver,
        out_shape=tuple(jax.ShapeDtypeStruct(*shape) for shape in shapes),
        in_specs=[vmem] * 3,
        out_specs=(hbm,) * 3,
        scratch_shapes=[pltpu.SemaphoreType.DMA((3,))],
        compiler_params=pltpu.CompilerParams(vmem_limit_bytes=8 * 1024 * 1024),
    )(*(pltpu.with_memory_space_constraint(one, pltpu.VMEM) for one in made))


def solution(mesh):
    in_specs = (
        P(("section", "rep"), None),
        P(),
        P(("section", "rep")),
        P("section", None),
        P(("section", "rep"), None),
    )
    out_specs = (P(("section", "rep"), None), P(("section", "rep"), None), P())
    coef = 4.0 / math.sqrt(128 * 256)
    return jax.shard_map(
        functools.partial(local, coef=coef), mesh=mesh, in_specs=in_specs, out_specs=out_specs,
        check_vma=False,
    )
```

```python
import functools
import math

import jax
import jax.numpy as jnp
from jax import lax
from jax.experimental import pallas as pl
from jax.experimental.pallas import tpu as pltpu
from jax.sharding import PartitionSpec as P


MESH = pl.DeviceIdType.MESH
NZ, NY, NX = 8, 8, 4
ROWS = 64
HALF = 128
MODULUS = 65521
OFFSET = (0, 1, 7, 2, 6, 3, 5, 4)
SLOT = {off: k for k, off in enumerate(OFFSET)}
GROUPS = ((0, 1), (1, 5), (5, 8))
COPIES = 160
BF16 = jnp.bfloat16
F32 = jnp.float32


def fold(v):
    return (v & 0xFFFF) + 15 * (v >> 16)


def reduce_once(v):
    return jnp.where(v >= MODULUS, v - MODULUS, v)


SCALE = 2.0 / MODULUS
WRAP = 1.0 - 0.5 * SCALE


def add_wrapped(u, step):
    total = u + step
    return jnp.where(total >= WRAP, total - 2.0, total)


def kernel(
    coef,
    feats_hbm, weight_hbm, scale_hbm, mask_hbm, cot_hbm,
    layer_out, grad_feats, grad_weight,
    feats, weight, scale_row, mask, cot, load_sems,
    adj, cm, gath, gath_t, masks, csend, crecv, acc, ysend, yrecv,
    near_send, near_recv, keep, keep_near, next_send, next_recv, zsend, zrecv,
    starts, steps, part, a1r, half, a2s, a2r, a3r, a4r, wbuf, scale_col,
    send_sems, recv_sems,
):
    sec = lax.axis_index("section")
    x = lax.axis_index("rep")
    c = sec % 2
    y = (sec // 2) % NY
    z = sec // (2 * NY)
    x_one = x + 1 - 2 * (x % 2)
    x_two = 3 - x
    x_opp = (x + 2) % NX

    def device(zz, yy, cc, xx):
        return ((zz * NY + yy) * 2 + cc, xx)

    sibling = device(z, y, 1 - c, x)
    east, west = device(z, y, c, x_one), device(z, y, c, x_two)

    def z_peer(e):
        return device((z + e) % NZ, y, c, x)

    def y_peer(e):
        return device(z, (y + e) % NY, c, x)

    def x_peer(e):
        return device(z, y, c, (x + e) % NX)

    loads = [
        pltpu.make_async_copy(src, dst, load_sems.at[n])
        for n, (src, dst) in enumerate((
            (feats_hbm, feats), (scale_hbm, scale_row), (mask_hbm, mask),
            (weight_hbm, weight), (cot_hbm, cot),
        ))
    ]
    for one in loads:
        one.start()

    barrier = pltpu.get_barrier_semaphore()
    peers = [z_peer(e) for e in range(1, NZ)] + [y_peer(e) for e in range(1, NY)]
    peers += [x_peer(e) for e in range(1, NX)] + [sibling]
    for peer in peers:
        pl.semaphore_signal(barrier, inc=1, device_id=peer, device_id_type=MESH)

    started = []

    def copy(src, dst, target):
        number = len(started)
        one = pltpu.make_async_remote_copy(
            src_ref=src, dst_ref=dst, send_sem=send_sems.at[number],
            recv_sem=recv_sems.at[number], device_id=target, device_id_type=MESH,
        )
        one.start()
        started.append(one)
        return one

    col_j = lax.broadcasted_iota(jnp.int32, (16, 512), 1)
    row_i = lax.broadcasted_iota(jnp.int32, (16, 512), 0)
    col_slot = col_j >> 6
    col_off = jnp.where((col_slot & 1) == 1, (col_slot + 1) >> 1, (8 - (col_slot >> 1)) & 7)
    columns_x = (x, x_one, x_two, x_opp)

    def side_core(side):
        return 1 - c if side == 0 else c

    def mask_columns():
        which = lax.broadcasted_iota(jnp.int32, (16, HALF), 0)
        lane = lax.broadcasted_iota(jnp.int32, (16, HALF), 1)
        core_of = jnp.where(which < 8, 1 - c, c)
        tile = ((z * NY + (which & 7)) * 2 + core_of) * 2 + x // 2
        every = masks[...].reshape(64, HALF)
        dims = (((1,), (1,)), ((), ()))
        low = lax.dot_general((tile == lane).astype(F32), every, dims, preferred_element_type=F32)
        high = lax.dot_general(
            (tile == lane + HALF).astype(F32), every, dims, preferred_element_type=F32
        )
        entry = lax.broadcasted_iota(jnp.int32, (64, 512), 0)
        slot = lax.broadcasted_iota(jnp.int32, (64, 512), 1) >> 6
        off = jnp.where((slot & 1) == 1, (slot + 1) >> 1, (8 - (slot >> 1)) & 7)
        same = (entry >> 3) == ((z + off) & 7)
        for n, xx in enumerate(columns_x):
            pick_low = jnp.where(same & ((entry & 7) == xx // 2), 1.0, 0.0).astype(F32)
            pick_high = jnp.where(same & ((entry & 7) == xx // 2 + 2), 1.0, 0.0).astype(F32)
            chosen = jnp.dot(low, pick_low, preferred_element_type=F32) + jnp.dot(
                high, pick_high, preferred_element_type=F32
            )
            cm[:, n * 512:(n + 1) * 512] = jnp.where(chosen > 0.5, coef, 0.0)

    def column_ids(n):
        return ((((z + col_off) & 7) * NY + y) * 2 + c) * 256 + columns_x[n] * ROWS + (col_j & 63)

    def prepare(unit, a, b):
        first = fold(fold(a * b))
        hashed = reduce_once(fold(fold(first * 20011 + (a + b) * 7919)))
        starts[unit] = hashed.astype(F32) * SCALE - 1.0

    def prepare_steps(number, b, stride):
        step = reduce_once(fold(fold(b[0:8] * 20011 + 7919)))
        steps[number, 0] = reduce_once(fold(step * 16)).astype(F32) * SCALE
        steps[number, 1] = reduce_once(fold(step * stride)).astype(F32) * SCALE

    def prepare_block():
        for n in range(NX):
            b = column_ids(n)
            prepare_steps(n, b, 512)
            for side in range(2):
                a = ((z * NY) * 2 + side_core(side)) * 256 + x * ROWS + row_i
                prepare(n * 2 + side, a, b)

    def make_block(n, side):
        lanes = slice(n * 512, (n + 1) * 512)
        step16 = jnp.concatenate([steps[n, 0]] * 2, axis=0)
        leap = jnp.concatenate([steps[n, 1]] * 2, axis=0)

        def run(yy, u0):
            off = (yy - y + NY) % NY
            late = off // 5
            slot = (off + 7) // 8 * ((1 - late) * (2 * off - 1) + late * (16 - 2 * off))
            coefs = cm[pl.ds(side * 8 + yy, 1), lanes]
            u = u0
            for s in range(4):
                at = pl.multiple_of(side * 512 + slot * ROWS + s * 16, 16)
                adj[pl.ds(at, 16), lanes] = (u * coefs).astype(BF16)
                if s < 3:
                    u = add_wrapped(u, step16)
            return add_wrapped(u0, leap)

        lax.fori_loop(0, 8, run, starts[n * 2 + side])

    for one in loads[:3]:
        one.wait()
    row = scale_row[...].astype(F32)
    pick = lax.broadcasted_iota(jnp.int32, (ROWS, ROWS), 0) == lax.broadcasted_iota(
        jnp.int32, (ROWS, ROWS), 1
    )
    column = jnp.sum(jnp.where(pick, jnp.broadcast_to(row, (ROWS, ROWS)), 0.0), axis=1, keepdims=True)
    scale_col[...] = jnp.broadcast_to(column, (ROWS, 256))
    scaled = (scale_col[...] * feats[...].astype(F32)).astype(BF16)
    gath[0, 0, 0:ROWS] = scaled[:, :HALF]
    gath_t[0, 0, 0:ROWS] = scaled[:, HALF:]
    masks[z] = jnp.zeros((8, HALF), F32)
    masks[z, 0:2, :] = mask[:, 0:HALF].astype(F32)
    masks[z, 2:4, :] = mask[:, HALF:].astype(F32)

    pl.semaphore_wait(barrier, len(peers))

    def start_pass(p):
        own = gath.at[p, 0, pl.ds(0, ROWS)]
        own_t = gath_t.at[p, 0, pl.ds(0, ROWS)]
        state = {"z": {}, "one": {}, "two": {}, "opp": [], "y_t": {}, "core_t": []}
        for k in range(1, NZ):
            e = (NZ - OFFSET[k]) % NZ
            state["z"][k] = copy(own, gath.at[p, 0, pl.ds(k * ROWS, ROWS)], z_peer(e))
            far = NY - k
            e = (NY - OFFSET[far]) % NY
            state["y_t"][far] = copy(own_t, gath_t.at[p, 0, pl.ds(far * ROWS, ROWS)], y_peer(e))
            if k == 2:
                forward(p, 0, state)
        return state

    def forward_t(p, state):
        for k in range(NY - 1, 0, -1):
            state["y_t"][k].wait_recv()
        state["core_t"].append(copy(gath_t.at[p, 0], gath_t.at[p, 1], sibling))

    def forward(p, g, state):
        lo, hi = GROUPS[g]
        for k in range(lo, hi):
            if k:
                state["z"][k].wait_recv()
        run = pl.ds(lo * ROWS, (hi - lo) * ROWS)
        state["one"][g] = copy(gath.at[p, 0, run], gath.at[p, 1, run], east)
        state["two"][g] = copy(gath.at[p, 0, run], gath.at[p, 2, run], west)

    def relay(p, g, state):
        lo, hi = GROUPS[g]
        size = (hi - lo) * ROWS // 2
        run = pl.ds(lo * ROWS, size)
        state["two"][g].wait_recv()
        state["opp"].append(copy(gath.at[p, 2, run], gath.at[p, 3, run], east))
        run = pl.ds(lo * ROWS + size, size)
        state["one"][g].wait_recv()
        state["opp"].append(copy(gath.at[p, 1, run], gath.at[p, 3, run], west))

    def finish_gather(state):
        for one in state["opp"]:
            one.wait_recv()

    def product(p, side):
        right = gath[p].reshape(NX * NZ * ROWS, HALF)
        value = jnp.dot(adj[side * 512:(side + 1) * 512, :], right, preferred_element_type=F32)
        if side == 0:
            csend[p] = value.astype(BF16)
        else:
            acc[...] = value

    def sums_first(p, state):
        product(p, 0)
        state["core"] = copy(csend.at[p], crecv.at[p], sibling)

    def sums_second(p, state):
        state["core"].wait_recv()
        total = acc[...] + crecv[p].astype(F32)
        acc[...] = total
        ysend[p] = total.astype(BF16)
        state["y"] = {}
        for e in (4, 3, 5, 2, 6, 1, 7):
            run = pl.ds(SLOT[e] * ROWS, ROWS)
            state["y"][e] = copy(ysend.at[p, run], yrecv.at[p, e], y_peer(e))

    def sums_last(p, state):
        total = acc[0:ROWS]
        for e in (1, 7, 2, 6, 3, 5, 4):
            state["y"][e].wait_recv()
            total = total + yrecv[p, e].astype(F32)
        return total

    def product_t(p, lo, hi):
        dims = (((0,), (0,)), ((), ()))
        turned = lax.dot_general(
            gath_t[p, 1], adj[0:512, lo:hi], dims, preferred_element_type=F32
        ) + lax.dot_general(
            gath_t[p, 0], adj[512:1024, lo:hi], dims, preferred_element_type=F32
        )
        return turned.T

    def near_first(p, state):
        for one in state["core_t"]:
            one.wait_recv()
        opposite = product_t(p, 1536, 2048)
        near_send[p, 0, 256:512] = opposite[:256].astype(BF16)
        near_send[p, 1, 256:512] = opposite[256:].astype(BF16)
        far, close = pl.ds(256, 256), pl.ds(0, 256)
        state["far_e"] = copy(near_send.at[p, 0, far], near_recv.at[p, 0, far], east)
        state["far_w"] = copy(near_send.at[p, 1, far], near_recv.at[p, 1, far], west)
        near_send[p, 0, 0:256] = product_t(p, 512, 768).astype(BF16)
        state["near_e"] = copy(near_send.at[p, 0, close], near_recv.at[p, 0, close], east)
        near_send[p, 1, 0:256] = product_t(p, 1280, 1536).astype(BF16)
        state["near_w"] = copy(near_send.at[p, 1, close], near_recv.at[p, 1, close], west)

    def near_second(p):
        keep_near[0] = product_t(p, 1024, 1280)
        keep_near[1] = product_t(p, 768, 1024)

    def next_first(p, state):
        state["far_e"].wait_recv()
        next_send[p, 0] = (keep_near[0] + near_recv[p, 0, 256:512].astype(F32)).astype(BF16)
        state["next_w"] = copy(next_send.at[p, 0], next_recv.at[p, 0], west)
        state["far_w"].wait_recv()
        next_send[p, 1] = (keep_near[1] + near_recv[p, 1, 256:512].astype(F32)).astype(BF16)
        state["next_e"] = copy(next_send.at[p, 1], next_recv.at[p, 1], east)
        value = product_t(p, 0, 512)
        state["near_e"].wait_recv()
        state["near_w"].wait_recv()
        keep[0:256] = value[:256] + near_recv[p, 0, 0:256].astype(F32)
        keep[256:512] = value[256:] + near_recv[p, 1, 0:256].astype(F32)

    def next_second(p, state):
        state["next_w"].wait_recv()
        state["next_e"].wait_recv()
        total = keep[...] + next_recv[p].reshape(512, HALF).astype(F32)
        keep[...] = total
        zsend[p] = total.astype(BF16)
        state["z_t"] = {}
        for e in (4, 3, 5, 2, 6, 1, 7):
            run = pl.ds(SLOT[e] * ROWS, ROWS)
            state["z_t"][e] = copy(zsend.at[p, run], zrecv.at[p, e], z_peer(e))

    def sums_last_t(p, state):
        total = keep[0:ROWS]
        for e in (1, 7, 2, 6, 3, 5, 4):
            state["z_t"][e].wait_recv()
            total = total + zrecv[p, e].astype(F32)
        return total

    mask_copies = [copy(masks.at[z], masks.at[z], z_peer(e)) for e in range(1, NZ)]
    state = start_pass(0)
    prepare_block()
    for one in mask_copies:
        one.wait_recv()
    mask_columns()
    make_block(3, 0)
    relay(0, 0, state)
    make_block(3, 1)
    forward(0, 1, state)
    make_block(1, 0)
    make_block(1, 1)
    forward_t(0, state)
    forward(0, 2, state)
    relay(0, 1, state)
    make_block(2, 0)
    make_block(2, 1)
    near_first(0, state)
    relay(0, 2, state)
    near_second(0)
    make_block(0, 0)
    make_block(0, 1)
    next_first(0, state)
    finish_gather(state)
    sums_first(0, state)
    product(0, 1)
    next_second(0, state)
    sums_second(0, state)
    sums = jnp.concatenate([sums_last(0, state), sums_last_t(0, state)], axis=1)

    for one in loads[3:]:
        one.wait()
    sums_high = sums.astype(BF16)
    sums_low = (sums - sums_high.astype(F32)).astype(BF16)
    scale = scale_col[...]
    presum = scale * (
        jnp.dot(sums_high, weight[...], preferred_element_type=F32)
        + jnp.dot(sums_low, weight[...], preferred_element_type=F32)
    )
    sigma = jax.nn.sigmoid(presum)
    layer_out[...] = (presum * sigma).astype(BF16)
    deriv = sigma * (1.0 + presum * (1.0 - sigma))
    error = (scale * cot[...].astype(F32) * deriv).astype(BF16)
    gath[1, 0, 0:ROWS] = error[:, :HALF]
    gath_t[1, 0, 0:ROWS] = error[:, HALF:]

    earlier = list(started)

    state = start_pass(1)
    dims = (((0,), (0,)), ((), ()))
    part[...] = lax.dot_general(
        sums_high, error, dims, preferred_element_type=F32
    ) + lax.dot_general(sums_low, error, dims, preferred_element_type=F32)
    theirs = pl.multiple_of((1 - c) * 128, 128)
    mine = pl.multiple_of(c * 128, 128)
    first = copy(part.at[pl.ds(theirs, 128)], a1r, sibling)
    for one in earlier:
        one.wait_send()
    relay(1, 0, state)
    forward(1, 1, state)

    first.wait_recv()
    half[...] = part[pl.ds(mine, 128), :] + a1r[...]
    a2s[...] = half[...].astype(BF16)
    second = []
    for e in range(1, NY):
        at = pl.multiple_of(((y + e) % NY) * 16, 16)
        second.append(copy(a2s.at[pl.ds(at, 16)], a2r.at[e], y_peer(e)))

    forward_t(1, state)
    forward(1, 2, state)
    relay(1, 1, state)
    near_first(1, state)

    piece = half[pl.ds(pl.multiple_of(y * 16, 16), 16), :]
    for e in range(1, NY):
        second[e - 1].wait_recv()
        piece = piece + a2r[e].astype(F32)
    a3r[z] = piece.astype(BF16)
    third = [copy(a3r.at[z], a3r.at[z], z_peer(e)) for e in range(1, NZ)]

    relay(1, 2, state)
    near_second(1)

    for one in third:
        one.wait_recv()
    piece = a3r[0].astype(F32)
    for n in range(1, NZ):
        piece = piece + a3r[n].astype(F32)
    a4r[x] = piece
    fourth = [copy(a4r.at[x], a4r.at[x], x_peer(e)) for e in range(1, NX)]

    next_first(1, state)
    finish_gather(state)
    sums_first(1, state)
    product(1, 1)

    for one in fourth:
        one.wait_recv()
    piece = (a4r[0] + a4r[1]) + (a4r[2] + a4r[3])
    at = pl.multiple_of(c * 128 + y * 16, 16)
    wbuf[pl.ds(at, 16), :] = piece.astype(BF16)
    fifth = [copy(wbuf.at[pl.ds(at, 16)], wbuf.at[pl.ds(at, 16)], y_peer(e)) for e in range(1, NY)]

    sums_second(1, state)
    next_second(1, state)
    for one in fifth:
        one.wait_recv()
    sixth = copy(wbuf.at[pl.ds(mine, 128)], wbuf.at[pl.ds(mine, 128)], sibling)
    back = jnp.concatenate([sums_last(1, state), sums_last_t(1, state)], axis=1)
    vgrad = (scale * back).astype(BF16)
    grad_feats[...] = lax.dot_general(
        vgrad, weight[...], (((1,), (1,)), ((), ())), preferred_element_type=F32
    ).astype(BF16)
    sixth.wait_recv()
    grad_weight[...] = wbuf[...].astype(F32)
    for one in started[len(earlier):]:
        one.wait_send()


def deliver(*refs):
    sems = refs[-1]
    copies = [pltpu.make_async_copy(refs[n], refs[n + 3], sems.at[n]) for n in range(3)]
    for one in copies:
        one.start()
    for one in copies:
        one.wait()


def local(node_feats, weight, node_scale, tile_mask, cotangent, coef):
    hidden = weight.shape[0]
    hbm = pl.BlockSpec(memory_space=pltpu.HBM)
    vmem = pl.BlockSpec(memory_space=pltpu.VMEM)
    shapes = (((ROWS, hidden), BF16), ((ROWS, hidden), BF16), ((hidden, hidden), F32))
    args = (node_feats, weight, node_scale.reshape(1, ROWS), tile_mask, cotangent)
    made = pl.pallas_call(
        functools.partial(kernel, coef),
        out_shape=tuple(pltpu.VMEM(*shape) for shape in shapes),
        in_specs=[hbm] * 5,
        out_specs=(vmem,) * 3,
        scratch_shapes=[
            pltpu.VMEM((ROWS, hidden), BF16),
            pltpu.VMEM((hidden, hidden), BF16),
            pltpu.VMEM((1, ROWS), BF16),
            pltpu.VMEM(tile_mask.shape, jnp.int32),
            pltpu.VMEM((ROWS, hidden), BF16),
            pltpu.SemaphoreType.DMA((5,)),
            pltpu.VMEM((1024, 2048), BF16),
            pltpu.VMEM((16, 2048), F32),
            pltpu.VMEM((2, NX, NZ * ROWS, HALF), BF16),
            pltpu.VMEM((2, 2, NY * ROWS, HALF), BF16),
            pltpu.VMEM((NZ, 8, HALF), F32),
            pltpu.VMEM((2, 512, HALF), BF16),
            pltpu.VMEM((2, 512, HALF), BF16),
            pltpu.VMEM((512, HALF), F32),
            pltpu.VMEM((2, 512, HALF), BF16),
            pltpu.VMEM((2, NY, ROWS, HALF), BF16),
            pltpu.VMEM((2, 2, 512, HALF), BF16),
            pltpu.VMEM((2, 2, 512, HALF), BF16),
            pltpu.VMEM((512, HALF), F32),
            pltpu.VMEM((2, 256, HALF), F32),
            pltpu.VMEM((2, 2, 256, HALF), BF16),
            pltpu.VMEM((2, 2, 256, HALF), BF16),
            pltpu.VMEM((2, 512, HALF), BF16),
            pltpu.VMEM((2, NZ, ROWS, HALF), BF16),
            pltpu.VMEM((8, 16, 512), F32),
            pltpu.VMEM((NX, 2, 8, 512), F32),
            pltpu.VMEM((256, 256), F32),
            pltpu.VMEM((128, 256), F32),
            pltpu.VMEM((128, 256), F32),
            pltpu.VMEM((128, 256), BF16),
            pltpu.VMEM((NY, 16, 256), BF16),
            pltpu.VMEM((NZ, 16, 256), BF16),
            pltpu.VMEM((NX, 16, 256), F32),
            pltpu.VMEM((256, 256), BF16),
            pltpu.VMEM((ROWS, 256), F32),
            pltpu.SemaphoreType.DMA((COPIES,)),
            pltpu.SemaphoreType.DMA((COPIES,)),
        ],
        compiler_params=pltpu.CompilerParams(
            collective_id=0, has_side_effects=True, vmem_limit_bytes=40 * 1024 * 1024
        ),
    )(*(pltpu.with_memory_space_constraint(arg, pltpu.HBM) for arg in args))
    return pl.pallas_call(
        deliver,
        out_shape=tuple(jax.ShapeDtypeStruct(*shape) for shape in shapes),
        in_specs=[vmem] * 3,
        out_specs=(hbm,) * 3,
        scratch_shapes=[pltpu.SemaphoreType.DMA((3,))],
        compiler_params=pltpu.CompilerParams(vmem_limit_bytes=8 * 1024 * 1024),
    )(*(pltpu.with_memory_space_constraint(one, pltpu.VMEM) for one in made))


def solution(mesh):
    in_specs = (
        P(("section", "rep"), None),
        P(),
        P(("section", "rep")),
        P("section", None),
        P(("section", "rep"), None),
    )
    out_specs = (P(("section", "rep"), None), P(("section", "rep"), None), P())
    coef = 4.0 / math.sqrt(128 * 256)
    return jax.shard_map(
        functools.partial(local, coef=coef), mesh=mesh, in_specs=in_specs, out_specs=out_specs,
        check_vma=False,
    )
```

```python
import functools
import math

import jax
import jax.numpy as jnp
from jax import lax
from jax.experimental import pallas as pl
from jax.experimental.pallas import tpu as pltpu
from jax.sharding import PartitionSpec as P


MESH = pl.DeviceIdType.MESH
NZ, NY, NX = 8, 8, 4
ROWS = 64
HALF = 128
MODULUS = 65521
OFFSET = (0, 1, 7, 2, 6, 3, 5, 4)
SLOT = {off: k for k, off in enumerate(OFFSET)}
GROUPS = ((0, 1), (1, 5), (5, 8))
COPIES = 80
BF16 = jnp.bfloat16
F32 = jnp.float32


def fold(v):
    return (v & 0xFFFF) + 15 * (v >> 16)


def reduce_once(v):
    return jnp.where(v >= MODULUS, v - MODULUS, v)


SCALE = 2.0 / MODULUS
WRAP = 1.0 - 0.5 * SCALE


def add_wrapped(u, step):
    total = u + step
    return jnp.where(total >= WRAP, total - 2.0, total)


def kernel(
    coef,
    feats_hbm, weight_hbm, scale_hbm, mask_hbm, cot_hbm,
    layer_out, grad_feats, grad_weight,
    feats, weight, scale_row, mask, cot, load_sems,
    adj, cm, gath, gath_t, masks, csend, crecv, acc, ysend, yrecv,
    near_send, near_recv, keep, keep_near, next_send, next_recv, zsend, zrecv,
    starts, steps, part, a1r, half, a2s, a2r, a3r, a4r, wbuf, scale_col,
    send_sems, recv_sems,
):
    sec = lax.axis_index("section")
    x = lax.axis_index("rep")
    c = sec % 2
    y = (sec // 2) % NY
    z = sec // (2 * NY)
    x_one = x + 1 - 2 * (x % 2)
    x_two = 3 - x
    x_opp = (x + 2) % NX

    def device(zz, yy, cc, xx):
        return ((zz * NY + yy) * 2 + cc, xx)

    sibling = device(z, y, 1 - c, x)
    east, west = device(z, y, c, x_one), device(z, y, c, x_two)

    def z_peer(e):
        return device((z + e) % NZ, y, c, x)

    def y_peer(e):
        return device(z, (y + e) % NY, c, x)

    def x_peer(e):
        return device(z, y, c, (x + e) % NX)

    loads = [
        pltpu.make_async_copy(src, dst, load_sems.at[n])
        for n, (src, dst) in enumerate((
            (feats_hbm, feats), (scale_hbm, scale_row), (mask_hbm, mask),
            (weight_hbm, weight), (cot_hbm, cot),
        ))
    ]
    for one in loads:
        one.start()

    barrier = pltpu.get_barrier_semaphore()
    peers = [z_peer(e) for e in range(1, NZ)] + [y_peer(e) for e in range(1, NY)]
    peers += [x_peer(e) for e in range(1, NX)] + [sibling]
    for peer in peers:
        pl.semaphore_signal(barrier, inc=1, device_id=peer, device_id_type=MESH)

    started = []
    numbers = iter(range(COPIES))

    class Batch:
        def __init__(self, view, target):
            number = next(numbers)
            self.send_sem, self.recv_sem = send_sems.at[number], recv_sems.at[number]
            self.whole = self.describe(view, view, target)
            started.append(self.whole)

        def describe(self, src, dst, target):
            return pltpu.make_async_remote_copy(
                src_ref=src, dst_ref=dst, send_sem=self.send_sem, recv_sem=self.recv_sem,
                device_id=target, device_id_type=MESH,
            )

        def start(self, src, dst, target):
            self.describe(src, dst, target).start()

        def wait_recv(self):
            self.whole.wait_recv()

    def copy(src, dst, target):
        one = Batch(dst, target)
        one.start(src, dst, target)
        return one

    col_j = lax.broadcasted_iota(jnp.int32, (16, 512), 1)
    row_i = lax.broadcasted_iota(jnp.int32, (16, 512), 0)
    col_slot = col_j >> 6
    col_off = jnp.where((col_slot & 1) == 1, (col_slot + 1) >> 1, (8 - (col_slot >> 1)) & 7)
    columns_x = (x, x_one, x_two, x_opp)

    def side_core(side):
        return 1 - c if side == 0 else c

    def mask_columns():
        which = lax.broadcasted_iota(jnp.int32, (16, HALF), 0)
        lane = lax.broadcasted_iota(jnp.int32, (16, HALF), 1)
        core_of = jnp.where(which < 8, 1 - c, c)
        tile = ((z * NY + (which & 7)) * 2 + core_of) * 2 + x // 2
        every = masks[...].reshape(64, HALF)
        dims = (((1,), (1,)), ((), ()))
        low = lax.dot_general((tile == lane).astype(F32), every, dims, preferred_element_type=F32)
        high = lax.dot_general(
            (tile == lane + HALF).astype(F32), every, dims, preferred_element_type=F32
        )
        entry = lax.broadcasted_iota(jnp.int32, (64, 512), 0)
        slot = lax.broadcasted_iota(jnp.int32, (64, 512), 1) >> 6
        off = jnp.where((slot & 1) == 1, (slot + 1) >> 1, (8 - (slot >> 1)) & 7)
        same = (entry >> 3) == ((z + off) & 7)
        for n, xx in enumerate(columns_x):
            pick_low = jnp.where(same & ((entry & 7) == xx // 2), 1.0, 0.0).astype(F32)
            pick_high = jnp.where(same & ((entry & 7) == xx // 2 + 2), 1.0, 0.0).astype(F32)
            chosen = jnp.dot(low, pick_low, preferred_element_type=F32) + jnp.dot(
                high, pick_high, preferred_element_type=F32
            )
            cm[:, n * 512:(n + 1) * 512] = jnp.where(chosen > 0.5, coef, 0.0)

    def column_ids(n):
        return ((((z + col_off) & 7) * NY + y) * 2 + c) * 256 + columns_x[n] * ROWS + (col_j & 63)

    def prepare(unit, a, b):
        first = fold(fold(a * b))
        hashed = reduce_once(fold(fold(first * 20011 + (a + b) * 7919)))
        starts[unit] = hashed.astype(F32) * SCALE - 1.0

    def prepare_steps(number, b, stride):
        step = reduce_once(fold(fold(b[0:8] * 20011 + 7919)))
        steps[number, 0] = reduce_once(fold(step * 16)).astype(F32) * SCALE
        steps[number, 1] = reduce_once(fold(step * stride)).astype(F32) * SCALE

    def prepare_block():
        for n in range(NX):
            b = column_ids(n)
            prepare_steps(n, b, 512)
            for side in range(2):
                a = ((z * NY) * 2 + side_core(side)) * 256 + x * ROWS + row_i
                prepare(n * 2 + side, a, b)

    def make_block(n, side):
        lanes = slice(n * 512, (n + 1) * 512)
        step16 = jnp.concatenate([steps[n, 0]] * 2, axis=0)
        leap = jnp.concatenate([steps[n, 1]] * 2, axis=0)

        def run(yy, u0):
            off = (yy - y + NY) % NY
            late = off // 5
            slot = (off + 7) // 8 * ((1 - late) * (2 * off - 1) + late * (16 - 2 * off))
            coefs = cm[pl.ds(side * 8 + yy, 1), lanes]
            u = u0
            for s in range(4):
                at = pl.multiple_of(side * 512 + slot * ROWS + s * 16, 16)
                adj[pl.ds(at, 16), lanes] = (u * coefs).astype(BF16)
                if s < 3:
                    u = add_wrapped(u, step16)
            return add_wrapped(u0, leap)

        lax.fori_loop(0, 8, run, starts[n * 2 + side])

    for one in loads[:3]:
        one.wait()
    row = scale_row[...].astype(F32)
    pick = lax.broadcasted_iota(jnp.int32, (ROWS, ROWS), 0) == lax.broadcasted_iota(
        jnp.int32, (ROWS, ROWS), 1
    )
    column = jnp.sum(jnp.where(pick, jnp.broadcast_to(row, (ROWS, ROWS)), 0.0), axis=1, keepdims=True)
    scale_col[...] = jnp.broadcast_to(column, (ROWS, 256))
    scaled = (scale_col[...] * feats[...].astype(F32)).astype(BF16)
    gath[0, 0, 0:ROWS] = scaled[:, :HALF]
    gath_t[0, 0, 0:ROWS] = scaled[:, HALF:]
    masks[z] = jnp.zeros((8, HALF), F32)
    masks[z, 0:2, :] = mask[:, 0:HALF].astype(F32)
    masks[z, 2:4, :] = mask[:, HALF:].astype(F32)

    pl.semaphore_wait(barrier, len(peers))

    def start_pass(p):
        own = gath.at[p, 0, pl.ds(0, ROWS)]
        own_t = gath_t.at[p, 0, pl.ds(0, ROWS)]
        state = {"z": {}, "one": {}, "two": {}, "opp": [], "y_t": {}, "core_t": []}
        for g, (lo, hi) in enumerate(GROUPS[1:], 1):
            state["z"][g] = Batch(gath.at[p, 0, pl.ds(lo * ROWS, (hi - lo) * ROWS)], z_peer(1))
        state["y_t"] = Batch(gath_t.at[p, 0, pl.ds(ROWS, (NY - 1) * ROWS)], y_peer(1))
        for k in range(1, NZ):
            e = (NZ - OFFSET[k]) % NZ
            g = 1 if k < GROUPS[1][1] else 2
            state["z"][g].start(own, gath.at[p, 0, pl.ds(k * ROWS, ROWS)], z_peer(e))
            far = NY - k
            e = (NY - OFFSET[far]) % NY
            state["y_t"].start(own_t, gath_t.at[p, 0, pl.ds(far * ROWS, ROWS)], y_peer(e))
            if k == 2:
                forward(p, 0, state)
        return state

    def forward_t(p, state):
        state["y_t"].wait_recv()
        state["core_t"].append(copy(gath_t.at[p, 0], gath_t.at[p, 1], sibling))

    def forward(p, g, state):
        lo, hi = GROUPS[g]
        if g:
            state["z"][g].wait_recv()
        run = pl.ds(lo * ROWS, (hi - lo) * ROWS)
        state["one"][g] = copy(gath.at[p, 0, run], gath.at[p, 1, run], east)
        state["two"][g] = copy(gath.at[p, 0, run], gath.at[p, 2, run], west)

    def relay(p, g, state):
        lo, hi = GROUPS[g]
        size = (hi - lo) * ROWS // 2
        run = pl.ds(lo * ROWS, size)
        state["two"][g].wait_recv()
        state["opp"].append(copy(gath.at[p, 2, run], gath.at[p, 3, run], east))
        run = pl.ds(lo * ROWS + size, size)
        state["one"][g].wait_recv()
        state["opp"].append(copy(gath.at[p, 1, run], gath.at[p, 3, run], west))

    def finish_gather(state):
        for one in state["opp"]:
            one.wait_recv()

    def product(p, side):
        right = gath[p].reshape(NX * NZ * ROWS, HALF)
        value = jnp.dot(adj[side * 512:(side + 1) * 512, :], right, preferred_element_type=F32)
        if side == 0:
            csend[p] = value.astype(BF16)
        else:
            acc[...] = value

    def sums_first(p, state):
        product(p, 0)
        state["core"] = copy(csend.at[p], crecv.at[p], sibling)

    def sums_second(p, state):
        state["core"].wait_recv()
        total = acc[...] + crecv[p].astype(F32)
        acc[...] = total
        ysend[p] = total.astype(BF16)
        state["y"] = Batch(yrecv.at[p, pl.ds(1, NY - 1)], y_peer(1))
        for e in (4, 3, 5, 2, 6, 1, 7):
            run = pl.ds(SLOT[e] * ROWS, ROWS)
            state["y"].start(ysend.at[p, run], yrecv.at[p, e], y_peer(e))

    def sums_last(p, state):
        total = acc[0:ROWS]
        state["y"].wait_recv()
        for e in range(1, NY):
            total = total + yrecv[p, e].astype(F32)
        return total

    def product_t(p, lo, hi):
        dims = (((0,), (0,)), ((), ()))
        turned = lax.dot_general(
            gath_t[p, 1], adj[0:512, lo:hi], dims, preferred_element_type=F32
        ) + lax.dot_general(
            gath_t[p, 0], adj[512:1024, lo:hi], dims, preferred_element_type=F32
        )
        return turned.T

    def near_first(p, state):
        for one in state["core_t"]:
            one.wait_recv()
        opposite = product_t(p, 1536, 2048)
        near_send[p, 0, 256:512] = opposite[:256].astype(BF16)
        near_send[p, 1, 256:512] = opposite[256:].astype(BF16)
        far, close = pl.ds(256, 256), pl.ds(0, 256)
        state["far_e"] = copy(near_send.at[p, 0, far], near_recv.at[p, 0, far], east)
        state["far_w"] = copy(near_send.at[p, 1, far], near_recv.at[p, 1, far], west)
        near_send[p, 0, 0:256] = product_t(p, 512, 768).astype(BF16)
        state["near_e"] = copy(near_send.at[p, 0, close], near_recv.at[p, 0, close], east)
        near_send[p, 1, 0:256] = product_t(p, 1280, 1536).astype(BF16)
        state["near_w"] = copy(near_send.at[p, 1, close], near_recv.at[p, 1, close], west)

    def near_second(p):
        keep_near[0] = product_t(p, 1024, 1280)
        keep_near[1] = product_t(p, 768, 1024)

    def next_first(p, state):
        state["far_e"].wait_recv()
        next_send[p, 0] = (keep_near[0] + near_recv[p, 0, 256:512].astype(F32)).astype(BF16)
        state["next_w"] = copy(next_send.at[p, 0], next_recv.at[p, 0], west)
        state["far_w"].wait_recv()
        next_send[p, 1] = (keep_near[1] + near_recv[p, 1, 256:512].astype(F32)).astype(BF16)
        state["next_e"] = copy(next_send.at[p, 1], next_recv.at[p, 1], east)
        value = product_t(p, 0, 512)
        state["near_e"].wait_recv()
        state["near_w"].wait_recv()
        keep[0:256] = value[:256] + near_recv[p, 0, 0:256].astype(F32)
        keep[256:512] = value[256:] + near_recv[p, 1, 0:256].astype(F32)

    def next_second(p, state):
        state["next_w"].wait_recv()
        state["next_e"].wait_recv()
        total = keep[...] + next_recv[p].reshape(512, HALF).astype(F32)
        keep[...] = total
        zsend[p] = total.astype(BF16)
        state["z_t"] = Batch(zrecv.at[p, pl.ds(1, NZ - 1)], z_peer(1))
        for e in (4, 3, 5, 2, 6, 1, 7):
            run = pl.ds(SLOT[e] * ROWS, ROWS)
            state["z_t"].start(zsend.at[p, run], zrecv.at[p, e], z_peer(e))

    def sums_last_t(p, state):
        total = keep[0:ROWS]
        state["z_t"].wait_recv()
        for e in range(1, NZ):
            total = total + zrecv[p, e].astype(F32)
        return total

    mask_copies = Batch(masks.at[pl.ds(0, NZ - 1)], z_peer(1))
    for e in range(1, NZ):
        mask_copies.start(masks.at[z], masks.at[z], z_peer(e))
    state = start_pass(0)
    prepare_block()
    mask_copies.wait_recv()
    mask_columns()
    make_block(3, 0)
    relay(0, 0, state)
    make_block(3, 1)
    forward(0, 1, state)
    make_block(1, 0)
    make_block(1, 1)
    forward_t(0, state)
    forward(0, 2, state)
    relay(0, 1, state)
    make_block(2, 0)
    make_block(2, 1)
    near_first(0, state)
    relay(0, 2, state)
    near_second(0)
    make_block(0, 0)
    make_block(0, 1)
    next_first(0, state)
    finish_gather(state)
    sums_first(0, state)
    product(0, 1)
    next_second(0, state)
    sums_second(0, state)
    sums = jnp.concatenate([sums_last(0, state), sums_last_t(0, state)], axis=1)

    for one in loads[3:]:
        one.wait()
    sums_high = sums.astype(BF16)
    sums_low = (sums - sums_high.astype(F32)).astype(BF16)
    scale = scale_col[...]
    presum = scale * (
        jnp.dot(sums_high, weight[...], preferred_element_type=F32)
        + jnp.dot(sums_low, weight[...], preferred_element_type=F32)
    )
    sigma = jax.nn.sigmoid(presum)
    layer_out[...] = (presum * sigma).astype(BF16)
    deriv = sigma * (1.0 + presum * (1.0 - sigma))
    error = (scale * cot[...].astype(F32) * deriv).astype(BF16)
    gath[1, 0, 0:ROWS] = error[:, :HALF]
    gath_t[1, 0, 0:ROWS] = error[:, HALF:]

    earlier = list(started)

    state = start_pass(1)
    dims = (((0,), (0,)), ((), ()))
    part[...] = lax.dot_general(
        sums_high, error, dims, preferred_element_type=F32
    ) + lax.dot_general(sums_low, error, dims, preferred_element_type=F32)
    theirs = pl.multiple_of((1 - c) * 128, 128)
    mine = pl.multiple_of(c * 128, 128)
    first = copy(part.at[pl.ds(theirs, 128)], a1r, sibling)
    for one in earlier:
        one.wait_send()
    relay(1, 0, state)
    forward(1, 1, state)

    first.wait_recv()
    half[...] = part[pl.ds(mine, 128), :] + a1r[...]
    a2s[...] = half[...].astype(BF16)
    second = Batch(a2r.at[pl.ds(1, NY - 1)], y_peer(1))
    for e in range(1, NY):
        at = pl.multiple_of(((y + e) % NY) * 16, 16)
        second.start(a2s.at[pl.ds(at, 16)], a2r.at[e], y_peer(e))

    forward_t(1, state)
    forward(1, 2, state)
    relay(1, 1, state)
    near_first(1, state)

    piece = half[pl.ds(pl.multiple_of(y * 16, 16), 16), :]
    second.wait_recv()
    for e in range(1, NY):
        piece = piece + a2r[e].astype(F32)
    a3r[z] = piece.astype(BF16)
    third = Batch(a3r.at[pl.ds(0, NZ - 1)], z_peer(1))
    for e in range(1, NZ):
        third.start(a3r.at[z], a3r.at[z], z_peer(e))

    relay(1, 2, state)
    near_second(1)

    third.wait_recv()
    piece = a3r[0].astype(F32)
    for n in range(1, NZ):
        piece = piece + a3r[n].astype(F32)
    a4r[x] = piece
    fourth = Batch(a4r.at[pl.ds(0, NX - 1)], x_peer(1))
    for e in range(1, NX):
        fourth.start(a4r.at[x], a4r.at[x], x_peer(e))

    next_first(1, state)
    finish_gather(state)
    sums_first(1, state)
    product(1, 1)

    fourth.wait_recv()
    piece = (a4r[0] + a4r[1]) + (a4r[2] + a4r[3])
    at = pl.multiple_of(c * 128 + y * 16, 16)
    wbuf[pl.ds(at, 16), :] = piece.astype(BF16)
    fifth = Batch(wbuf.at[pl.ds(0, 16 * (NY - 1))], y_peer(1))
    for e in range(1, NY):
        fifth.start(wbuf.at[pl.ds(at, 16)], wbuf.at[pl.ds(at, 16)], y_peer(e))

    sums_second(1, state)
    next_second(1, state)
    fifth.wait_recv()
    sixth = copy(wbuf.at[pl.ds(mine, 128)], wbuf.at[pl.ds(mine, 128)], sibling)
    back = jnp.concatenate([sums_last(1, state), sums_last_t(1, state)], axis=1)
    vgrad = (scale * back).astype(BF16)
    grad_feats[...] = lax.dot_general(
        vgrad, weight[...], (((1,), (1,)), ((), ())), preferred_element_type=F32
    ).astype(BF16)
    sixth.wait_recv()
    grad_weight[...] = wbuf[...].astype(F32)
    for one in started[len(earlier):]:
        one.wait_send()


def deliver(*refs):
    sems = refs[-1]
    copies = [pltpu.make_async_copy(refs[n], refs[n + 3], sems.at[n]) for n in range(3)]
    for one in copies:
        one.start()
    for one in copies:
        one.wait()


def local(node_feats, weight, node_scale, tile_mask, cotangent, coef):
    hidden = weight.shape[0]
    hbm = pl.BlockSpec(memory_space=pltpu.HBM)
    vmem = pl.BlockSpec(memory_space=pltpu.VMEM)
    shapes = (((ROWS, hidden), BF16), ((ROWS, hidden), BF16), ((hidden, hidden), F32))
    args = (node_feats, weight, node_scale.reshape(1, ROWS), tile_mask, cotangent)
    made = pl.pallas_call(
        functools.partial(kernel, coef),
        out_shape=tuple(pltpu.VMEM(*shape) for shape in shapes),
        in_specs=[hbm] * 5,
        out_specs=(vmem,) * 3,
        scratch_shapes=[
            pltpu.VMEM((ROWS, hidden), BF16),
            pltpu.VMEM((hidden, hidden), BF16),
            pltpu.VMEM((1, ROWS), BF16),
            pltpu.VMEM(tile_mask.shape, jnp.int32),
            pltpu.VMEM((ROWS, hidden), BF16),
            pltpu.SemaphoreType.DMA((5,)),
            pltpu.VMEM((1024, 2048), BF16),
            pltpu.VMEM((16, 2048), F32),
            pltpu.VMEM((2, NX, NZ * ROWS, HALF), BF16),
            pltpu.VMEM((2, 2, NY * ROWS, HALF), BF16),
            pltpu.VMEM((NZ, 8, HALF), F32),
            pltpu.VMEM((2, 512, HALF), BF16),
            pltpu.VMEM((2, 512, HALF), BF16),
            pltpu.VMEM((512, HALF), F32),
            pltpu.VMEM((2, 512, HALF), BF16),
            pltpu.VMEM((2, NY, ROWS, HALF), BF16),
            pltpu.VMEM((2, 2, 512, HALF), BF16),
            pltpu.VMEM((2, 2, 512, HALF), BF16),
            pltpu.VMEM((512, HALF), F32),
            pltpu.VMEM((2, 256, HALF), F32),
            pltpu.VMEM((2, 2, 256, HALF), BF16),
            pltpu.VMEM((2, 2, 256, HALF), BF16),
            pltpu.VMEM((2, 512, HALF), BF16),
            pltpu.VMEM((2, NZ, ROWS, HALF), BF16),
            pltpu.VMEM((8, 16, 512), F32),
            pltpu.VMEM((NX, 2, 8, 512), F32),
            pltpu.VMEM((256, 256), F32),
            pltpu.VMEM((128, 256), F32),
            pltpu.VMEM((128, 256), F32),
            pltpu.VMEM((128, 256), BF16),
            pltpu.VMEM((NY, 16, 256), BF16),
            pltpu.VMEM((NZ, 16, 256), BF16),
            pltpu.VMEM((NX, 16, 256), F32),
            pltpu.VMEM((256, 256), BF16),
            pltpu.VMEM((ROWS, 256), F32),
            pltpu.SemaphoreType.DMA((COPIES,)),
            pltpu.SemaphoreType.DMA((COPIES,)),
        ],
        compiler_params=pltpu.CompilerParams(
            collective_id=0, has_side_effects=True, vmem_limit_bytes=40 * 1024 * 1024
        ),
    )(*(pltpu.with_memory_space_constraint(arg, pltpu.HBM) for arg in args))
    return pl.pallas_call(
        deliver,
        out_shape=tuple(jax.ShapeDtypeStruct(*shape) for shape in shapes),
        in_specs=[vmem] * 3,
        out_specs=(hbm,) * 3,
        scratch_shapes=[pltpu.SemaphoreType.DMA((3,))],
        compiler_params=pltpu.CompilerParams(vmem_limit_bytes=8 * 1024 * 1024),
    )(*(pltpu.with_memory_space_constraint(one, pltpu.VMEM) for one in made))


def solution(mesh):
    in_specs = (
        P(("section", "rep"), None),
        P(),
        P(("section", "rep")),
        P("section", None),
        P(("section", "rep"), None),
    )
    out_specs = (P(("section", "rep"), None), P(("section", "rep"), None), P())
    coef = 4.0 / math.sqrt(128 * 256)
    return jax.shard_map(
        functools.partial(local, coef=coef), mesh=mesh, in_specs=in_specs, out_specs=out_specs,
        check_vma=False,
    )
```

```python
import functools
import math

import jax
import jax.numpy as jnp
from jax import lax
from jax.experimental import pallas as pl
from jax.experimental.pallas import tpu as pltpu
from jax.sharding import PartitionSpec as P


MESH = pl.DeviceIdType.MESH
NZ, NY, NX = 8, 8, 4
ROWS = 64
HALF = 128
MODULUS = 65521
OFFSET = (0, 1, 7, 2, 6, 3, 5, 4)
SLOT = {off: k for k, off in enumerate(OFFSET)}
GROUPS = ((0, 1), (1, 5), (5, 8))
COPIES = 80
BF16 = jnp.bfloat16
F32 = jnp.float32


def fold(v):
    return (v & 0xFFFF) + 15 * (v >> 16)


def reduce_once(v):
    return jnp.where(v >= MODULUS, v - MODULUS, v)


SCALE = 2.0 / MODULUS
WRAP = 1.0 - 0.5 * SCALE


def add_wrapped(u, step):
    total = u + step
    return jnp.where(total >= WRAP, total - 2.0, total)


def kernel(
    coef,
    feats_hbm, weight_hbm, scale_hbm, mask_hbm, cot_hbm,
    layer_out, grad_feats, grad_weight,
    feats, weight, scale_row, mask, cot, load_sems,
    adj, cm, gath, gath_t, masks, csend, crecv, acc, ysend, yrecv,
    near_send, near_recv, keep, keep_near, next_send, next_recv, zsend, zrecv,
    starts, steps, part, a1r, half, a2s, a2r, a3r, a4r, wbuf, scale_col,
    send_sems, recv_sems,
):
    sec = lax.axis_index("section")
    x = lax.axis_index("rep")
    c = sec % 2
    y = (sec // 2) % NY
    z = sec // (2 * NY)
    x_one = x + 1 - 2 * (x % 2)
    x_two = 3 - x
    x_opp = (x + 2) % NX

    def device(zz, yy, cc, xx):
        return ((zz * NY + yy) * 2 + cc, xx)

    sibling = device(z, y, 1 - c, x)
    east, west = device(z, y, c, x_one), device(z, y, c, x_two)

    def z_peer(e):
        return device((z + e) % NZ, y, c, x)

    def y_peer(e):
        return device(z, (y + e) % NY, c, x)

    def x_peer(e):
        return device(z, y, c, (x + e) % NX)

    loads = [
        pltpu.make_async_copy(src, dst, load_sems.at[n])
        for n, (src, dst) in enumerate((
            (feats_hbm, feats), (scale_hbm, scale_row), (mask_hbm, mask),
            (weight_hbm, weight), (cot_hbm, cot),
        ))
    ]
    for one in loads:
        one.start()

    barrier = pltpu.get_barrier_semaphore()
    peers = [z_peer(e) for e in range(1, NZ)] + [y_peer(e) for e in range(1, NY)]
    peers += [x_peer(e) for e in range(1, NX)] + [sibling]
    for peer in peers:
        pl.semaphore_signal(barrier, inc=1, device_id=peer, device_id_type=MESH)

    started = []
    numbers = iter(range(COPIES))

    class Batch:
        def __init__(self, view, target):
            number = next(numbers)
            self.send_sem, self.recv_sem = send_sems.at[number], recv_sems.at[number]
            self.whole = self.describe(view, view, target)
            started.append(self.whole)

        def describe(self, src, dst, target):
            return pltpu.make_async_remote_copy(
                src_ref=src, dst_ref=dst, send_sem=self.send_sem, recv_sem=self.recv_sem,
                device_id=target, device_id_type=MESH,
            )

        def start(self, src, dst, target):
            self.describe(src, dst, target).start()

        def wait_recv(self):
            self.whole.wait_recv()

    def copy(src, dst, target):
        one = Batch(dst, target)
        one.start(src, dst, target)
        return one

    col_j = lax.broadcasted_iota(jnp.int32, (16, 512), 1)
    row_i = lax.broadcasted_iota(jnp.int32, (16, 512), 0)
    col_slot = col_j >> 6
    col_off = jnp.where((col_slot & 1) == 1, (col_slot + 1) >> 1, (8 - (col_slot >> 1)) & 7)
    columns_x = (x, x_one, x_two, x_opp)

    def side_core(side):
        return 1 - c if side == 0 else c

    def mask_columns():
        which = lax.broadcasted_iota(jnp.int32, (16, HALF), 0)
        lane = lax.broadcasted_iota(jnp.int32, (16, HALF), 1)
        core_of = jnp.where(which < 8, 1 - c, c)
        tile = ((z * NY + (which & 7)) * 2 + core_of) * 2 + x // 2
        every = masks[...].reshape(64, HALF)
        dims = (((1,), (1,)), ((), ()))
        low = lax.dot_general((tile == lane).astype(F32), every, dims, preferred_element_type=F32)
        high = lax.dot_general(
            (tile == lane + HALF).astype(F32), every, dims, preferred_element_type=F32
        )
        entry = lax.broadcasted_iota(jnp.int32, (64, 512), 0)
        slot = lax.broadcasted_iota(jnp.int32, (64, 512), 1) >> 6
        off = jnp.where((slot & 1) == 1, (slot + 1) >> 1, (8 - (slot >> 1)) & 7)
        same = (entry >> 3) == ((z + off) & 7)
        for n, xx in enumerate(columns_x):
            pick_low = jnp.where(same & ((entry & 7) == xx // 2), 1.0, 0.0).astype(F32)
            pick_high = jnp.where(same & ((entry & 7) == xx // 2 + 2), 1.0, 0.0).astype(F32)
            chosen = jnp.dot(low, pick_low, preferred_element_type=F32) + jnp.dot(
                high, pick_high, preferred_element_type=F32
            )
            cm[:, n * 512:(n + 1) * 512] = jnp.where(chosen > 0.5, coef, 0.0)

    def column_ids(n):
        return ((((z + col_off) & 7) * NY + y) * 2 + c) * 256 + columns_x[n] * ROWS + (col_j & 63)

    def prepare(unit, a, b):
        first = fold(fold(a * b))
        hashed = reduce_once(fold(fold(first * 20011 + (a + b) * 7919)))
        starts[unit] = hashed.astype(F32) * SCALE - 1.0

    def prepare_steps(number, b, stride):
        step = reduce_once(fold(fold(b[0:8] * 20011 + 7919)))
        steps[number, 0] = reduce_once(fold(step * 16)).astype(F32) * SCALE
        steps[number, 1] = reduce_once(fold(step * stride)).astype(F32) * SCALE

    def prepare_block():
        for n in range(NX):
            b = column_ids(n)
            prepare_steps(n, b, 512)
            for side in range(2):
                a = ((z * NY) * 2 + side_core(side)) * 256 + x * ROWS + row_i
                prepare(n * 2 + side, a, b)

    def make_block(n, side):
        lanes = slice(n * 512, (n + 1) * 512)
        step16 = jnp.concatenate([steps[n, 0]] * 2, axis=0)
        leap = jnp.concatenate([steps[n, 1]] * 2, axis=0)

        def run(yy, u0):
            off = (yy - y + NY) % NY
            late = off // 5
            slot = (off + 7) // 8 * ((1 - late) * (2 * off - 1) + late * (16 - 2 * off))
            coefs = cm[pl.ds(side * 8 + yy, 1), lanes]
            u = u0
            for s in range(4):
                at = pl.multiple_of(side * 512 + slot * ROWS + s * 16, 16)
                adj[pl.ds(at, 16), lanes] = (u * coefs).astype(BF16)
                if s < 3:
                    u = add_wrapped(u, step16)
            return add_wrapped(u0, leap)

        lax.fori_loop(0, 8, run, starts[n * 2 + side])

    for one in loads[:3]:
        one.wait()
    row = scale_row[...].astype(F32)
    pick = lax.broadcasted_iota(jnp.int32, (ROWS, ROWS), 0) == lax.broadcasted_iota(
        jnp.int32, (ROWS, ROWS), 1
    )
    column = jnp.sum(jnp.where(pick, jnp.broadcast_to(row, (ROWS, ROWS)), 0.0), axis=1, keepdims=True)
    scale_col[...] = jnp.broadcast_to(column, (ROWS, 256))
    scaled = (scale_col[...] * feats[...].astype(F32)).astype(BF16)
    gath[0, 0, 0:ROWS] = scaled[:, :HALF]
    gath_t[0, 0, 0:ROWS] = scaled[:, HALF:]
    masks[z] = jnp.zeros((8, HALF), F32)
    masks[z, 0:2, :] = mask[:, 0:HALF].astype(F32)
    masks[z, 2:4, :] = mask[:, HALF:].astype(F32)

    pl.semaphore_wait(barrier, len(peers))

    def start_pass(p):
        own = gath.at[p, 0, pl.ds(0, ROWS)]
        own_t = gath_t.at[p, 0, pl.ds(0, ROWS)]
        state = {"z": {}, "one": {}, "two": {}, "opp": [], "y_t": {}, "core_t": []}
        for g, (lo, hi) in enumerate(GROUPS[1:], 1):
            state["z"][g] = Batch(gath.at[p, 0, pl.ds(lo * ROWS, (hi - lo) * ROWS)], z_peer(1))
        state["y_t"] = Batch(gath_t.at[p, 0, pl.ds(ROWS, (NY - 1) * ROWS)], y_peer(1))
        for k in range(1, NZ):
            e = (NZ - OFFSET[k]) % NZ
            g = 1 if k < GROUPS[1][1] else 2
            state["z"][g].start(own, gath.at[p, 0, pl.ds(k * ROWS, ROWS)], z_peer(e))
            far = NY - k
            e = (NY - OFFSET[far]) % NY
            state["y_t"].start(own_t, gath_t.at[p, 0, pl.ds(far * ROWS, ROWS)], y_peer(e))
            if k == 2:
                forward(p, 0, state)
        return state

    def forward_t(p, state):
        state["y_t"].wait_recv()
        state["core_t"].append(copy(gath_t.at[p, 0], gath_t.at[p, 1], sibling))

    def forward(p, g, state):
        lo, hi = GROUPS[g]
        if g:
            state["z"][g].wait_recv()
        run = pl.ds(lo * ROWS, (hi - lo) * ROWS)
        state["one"][g] = copy(gath.at[p, 0, run], gath.at[p, 1, run], east)
        state["two"][g] = copy(gath.at[p, 0, run], gath.at[p, 2, run], west)

    def relay(p, g, state):
        lo, hi = GROUPS[g]
        size = (hi - lo) * ROWS // 2
        run = pl.ds(lo * ROWS, size)
        state["two"][g].wait_recv()
        state["opp"].append(copy(gath.at[p, 2, run], gath.at[p, 3, run], east))
        run = pl.ds(lo * ROWS + size, size)
        state["one"][g].wait_recv()
        state["opp"].append(copy(gath.at[p, 1, run], gath.at[p, 3, run], west))

    def finish_gather(state):
        for one in state["opp"]:
            one.wait_recv()

    def product(p, side):
        right = gath[p].reshape(NX * NZ * ROWS, HALF)
        value = jnp.dot(adj[side * 512:(side + 1) * 512, :], right, preferred_element_type=F32)
        if side == 0:
            csend[p] = value.astype(BF16)
        else:
            acc[...] = value

    def sums_first(p, state):
        product(p, 0)
        state["core"] = copy(csend.at[p], crecv.at[p], sibling)

    def sums_second(p, state):
        state["core"].wait_recv()
        total = acc[...] + crecv[p].astype(F32)
        acc[...] = total
        ysend[p] = total.astype(BF16)
        state["y"] = Batch(yrecv.at[p, pl.ds(1, NY - 1)], y_peer(1))
        for e in (4, 3, 5, 2, 6, 1, 7):
            run = pl.ds(SLOT[e] * ROWS, ROWS)
            state["y"].start(ysend.at[p, run], yrecv.at[p, e], y_peer(e))

    def sums_last(p, state):
        total = acc[0:ROWS]
        state["y"].wait_recv()
        for e in range(1, NY):
            total = total + yrecv[p, e].astype(F32)
        return total

    def product_t(p, lo, hi):
        dims = (((0,), (0,)), ((), ()))
        turned = lax.dot_general(
            gath_t[p, 1], adj[0:512, lo:hi], dims, preferred_element_type=F32
        ) + lax.dot_general(
            gath_t[p, 0], adj[512:1024, lo:hi], dims, preferred_element_type=F32
        )
        return turned.T

    def near_first(p, state):
        for one in state["core_t"]:
            one.wait_recv()
        opposite = product_t(p, 1536, 2048)
        near_send[p, 0, 256:512] = opposite[:256].astype(BF16)
        near_send[p, 1, 256:512] = opposite[256:].astype(BF16)
        far, close = pl.ds(256, 256), pl.ds(0, 256)
        state["far_e"] = copy(near_send.at[p, 0, far], near_recv.at[p, 0, far], east)
        state["far_w"] = copy(near_send.at[p, 1, far], near_recv.at[p, 1, far], west)
        near_send[p, 0, 0:256] = product_t(p, 512, 768).astype(BF16)
        state["near_e"] = copy(near_send.at[p, 0, close], near_recv.at[p, 0, close], east)
        near_send[p, 1, 0:256] = product_t(p, 1280, 1536).astype(BF16)
        state["near_w"] = copy(near_send.at[p, 1, close], near_recv.at[p, 1, close], west)

    def near_second(p):
        keep_near[0] = product_t(p, 1024, 1280)
        keep_near[1] = product_t(p, 768, 1024)

    def next_first(p, state):
        state["far_e"].wait_recv()
        next_send[p, 0] = (keep_near[0] + near_recv[p, 0, 256:512].astype(F32)).astype(BF16)
        state["next_w"] = copy(next_send.at[p, 0], next_recv.at[p, 0], west)
        state["far_w"].wait_recv()
        next_send[p, 1] = (keep_near[1] + near_recv[p, 1, 256:512].astype(F32)).astype(BF16)
        state["next_e"] = copy(next_send.at[p, 1], next_recv.at[p, 1], east)

    def next_own(p, state):
        value = product_t(p, 0, 512)
        state["near_e"].wait_recv()
        state["near_w"].wait_recv()
        keep[0:256] = value[:256] + near_recv[p, 0, 0:256].astype(F32)
        keep[256:512] = value[256:] + near_recv[p, 1, 0:256].astype(F32)

    def next_second(p, state):
        state["z_t"] = Batch(zrecv.at[p, pl.ds(1, NZ - 1)], z_peer(1))
        for part_at, arrival, offsets in ((1, "next_e", (4, 3, 5, 6)), (0, "next_w", (2, 1, 7))):
            state[arrival].wait_recv()
            rows = slice(part_at * 256, (part_at + 1) * 256)
            total = keep[rows] + next_recv[p, part_at].astype(F32)
            zsend[p, rows] = total.astype(BF16)
            for e in offsets:
                run = pl.ds(SLOT[e] * ROWS, ROWS)
                state["z_t"].start(zsend.at[p, run], zrecv.at[p, e], z_peer(e))
        keep[0:ROWS] = total[0:ROWS]

    def sums_last_t(p, state):
        total = keep[0:ROWS]
        state["z_t"].wait_recv()
        for e in range(1, NZ):
            total = total + zrecv[p, e].astype(F32)
        return total

    mask_copies = Batch(masks.at[pl.ds(0, NZ - 1)], z_peer(1))
    for e in range(1, NZ):
        mask_copies.start(masks.at[z], masks.at[z], z_peer(e))
    state = start_pass(0)
    prepare_block()
    mask_copies.wait_recv()
    mask_columns()
    make_block(3, 0)
    relay(0, 0, state)
    make_block(3, 1)
    forward(0, 1, state)
    make_block(1, 0)
    make_block(1, 1)
    forward_t(0, state)
    forward(0, 2, state)
    relay(0, 1, state)
    make_block(2, 0)
    make_block(2, 1)
    near_first(0, state)
    relay(0, 2, state)
    near_second(0)
    make_block(0, 0)
    make_block(0, 1)
    next_first(0, state)
    finish_gather(state)
    sums_first(0, state)
    next_own(0, state)
    product(0, 1)
    next_second(0, state)
    sums_second(0, state)
    sums = jnp.concatenate([sums_last(0, state), sums_last_t(0, state)], axis=1)

    for one in loads[3:]:
        one.wait()
    sums_high = sums.astype(BF16)
    sums_low = (sums - sums_high.astype(F32)).astype(BF16)
    scale = scale_col[...]
    presum = scale * (
        jnp.dot(sums_high, weight[...], preferred_element_type=F32)
        + jnp.dot(sums_low, weight[...], preferred_element_type=F32)
    )
    sigma = jax.nn.sigmoid(presum)
    layer_out[...] = (presum * sigma).astype(BF16)
    deriv = sigma * (1.0 + presum * (1.0 - sigma))
    error = (scale * cot[...].astype(F32) * deriv).astype(BF16)
    gath[1, 0, 0:ROWS] = error[:, :HALF]
    gath_t[1, 0, 0:ROWS] = error[:, HALF:]

    earlier = list(started)

    state = start_pass(1)
    dims = (((0,), (0,)), ((), ()))
    part[...] = lax.dot_general(
        sums_high, error, dims, preferred_element_type=F32
    ) + lax.dot_general(sums_low, error, dims, preferred_element_type=F32)
    theirs = pl.multiple_of((1 - c) * 128, 128)
    mine = pl.multiple_of(c * 128, 128)
    first = copy(part.at[pl.ds(theirs, 128)], a1r, sibling)
    for one in earlier:
        one.wait_send()
    relay(1, 0, state)
    forward(1, 1, state)

    first.wait_recv()
    half[...] = part[pl.ds(mine, 128), :] + a1r[...]
    a2s[...] = half[...].astype(BF16)
    second = Batch(a2r.at[pl.ds(1, NY - 1)], y_peer(1))
    for e in range(1, NY):
        at = pl.multiple_of(((y + e) % NY) * 16, 16)
        second.start(a2s.at[pl.ds(at, 16)], a2r.at[e], y_peer(e))

    forward_t(1, state)
    forward(1, 2, state)
    relay(1, 1, state)
    near_first(1, state)

    piece = half[pl.ds(pl.multiple_of(y * 16, 16), 16), :]
    second.wait_recv()
    for e in range(1, NY):
        piece = piece + a2r[e].astype(F32)
    a3r[z] = piece.astype(BF16)
    third = Batch(a3r.at[pl.ds(0, NZ - 1)], z_peer(1))
    for e in range(1, NZ):
        third.start(a3r.at[z], a3r.at[z], z_peer(e))

    relay(1, 2, state)
    near_second(1)
    next_first(1, state)
    finish_gather(state)
    sums_first(1, state)

    third.wait_recv()
    piece = a3r[0].astype(F32)
    for n in range(1, NZ):
        piece = piece + a3r[n].astype(F32)
    a4r[x] = piece
    fourth = Batch(a4r.at[pl.ds(0, NX - 1)], x_peer(1))
    for e in range(1, NX):
        fourth.start(a4r.at[x], a4r.at[x], x_peer(e))

    next_own(1, state)
    product(1, 1)
    next_second(1, state)

    fourth.wait_recv()
    piece = (a4r[0] + a4r[1]) + (a4r[2] + a4r[3])
    at = pl.multiple_of(c * 128 + y * 16, 16)
    wbuf[pl.ds(at, 16), :] = piece.astype(BF16)
    fifth = Batch(wbuf.at[pl.ds(0, 16 * (NY - 1))], y_peer(1))
    for e in range(1, NY):
        fifth.start(wbuf.at[pl.ds(at, 16)], wbuf.at[pl.ds(at, 16)], y_peer(e))
    sums_second(1, state)
    fifth.wait_recv()
    sixth = copy(wbuf.at[pl.ds(mine, 128)], wbuf.at[pl.ds(mine, 128)], sibling)
    back = jnp.concatenate([sums_last(1, state), sums_last_t(1, state)], axis=1)
    vgrad = (scale * back).astype(BF16)
    grad_feats[...] = lax.dot_general(
        vgrad, weight[...], (((1,), (1,)), ((), ())), preferred_element_type=F32
    ).astype(BF16)
    sixth.wait_recv()
    grad_weight[...] = wbuf[...].astype(F32)
    for one in started[len(earlier):]:
        one.wait_send()


def deliver(*refs):
    sems = refs[-1]
    copies = [pltpu.make_async_copy(refs[n], refs[n + 3], sems.at[n]) for n in range(3)]
    for one in copies:
        one.start()
    for one in copies:
        one.wait()


def local(node_feats, weight, node_scale, tile_mask, cotangent, coef):
    hidden = weight.shape[0]
    hbm = pl.BlockSpec(memory_space=pltpu.HBM)
    vmem = pl.BlockSpec(memory_space=pltpu.VMEM)
    shapes = (((ROWS, hidden), BF16), ((ROWS, hidden), BF16), ((hidden, hidden), F32))
    args = (node_feats, weight, node_scale.reshape(1, ROWS), tile_mask, cotangent)
    made = pl.pallas_call(
        functools.partial(kernel, coef),
        out_shape=tuple(pltpu.VMEM(*shape) for shape in shapes),
        in_specs=[hbm] * 5,
        out_specs=(vmem,) * 3,
        scratch_shapes=[
            pltpu.VMEM((ROWS, hidden), BF16),
            pltpu.VMEM((hidden, hidden), BF16),
            pltpu.VMEM((1, ROWS), BF16),
            pltpu.VMEM(tile_mask.shape, jnp.int32),
            pltpu.VMEM((ROWS, hidden), BF16),
            pltpu.SemaphoreType.DMA((5,)),
            pltpu.VMEM((1024, 2048), BF16),
            pltpu.VMEM((16, 2048), F32),
            pltpu.VMEM((2, NX, NZ * ROWS, HALF), BF16),
            pltpu.VMEM((2, 2, NY * ROWS, HALF), BF16),
            pltpu.VMEM((NZ, 8, HALF), F32),
            pltpu.VMEM((2, 512, HALF), BF16),
            pltpu.VMEM((2, 512, HALF), BF16),
            pltpu.VMEM((512, HALF), F32),
            pltpu.VMEM((2, 512, HALF), BF16),
            pltpu.VMEM((2, NY, ROWS, HALF), BF16),
            pltpu.VMEM((2, 2, 512, HALF), BF16),
            pltpu.VMEM((2, 2, 512, HALF), BF16),
            pltpu.VMEM((512, HALF), F32),
            pltpu.VMEM((2, 256, HALF), F32),
            pltpu.VMEM((2, 2, 256, HALF), BF16),
            pltpu.VMEM((2, 2, 256, HALF), BF16),
            pltpu.VMEM((2, 512, HALF), BF16),
            pltpu.VMEM((2, NZ, ROWS, HALF), BF16),
            pltpu.VMEM((8, 16, 512), F32),
            pltpu.VMEM((NX, 2, 8, 512), F32),
            pltpu.VMEM((256, 256), F32),
            pltpu.VMEM((128, 256), F32),
            pltpu.VMEM((128, 256), F32),
            pltpu.VMEM((128, 256), BF16),
            pltpu.VMEM((NY, 16, 256), BF16),
            pltpu.VMEM((NZ, 16, 256), BF16),
            pltpu.VMEM((NX, 16, 256), F32),
            pltpu.VMEM((256, 256), BF16),
            pltpu.VMEM((ROWS, 256), F32),
            pltpu.SemaphoreType.DMA((COPIES,)),
            pltpu.SemaphoreType.DMA((COPIES,)),
        ],
        compiler_params=pltpu.CompilerParams(
            collective_id=0, has_side_effects=True, vmem_limit_bytes=40 * 1024 * 1024
        ),
    )(*(pltpu.with_memory_space_constraint(arg, pltpu.HBM) for arg in args))
    return pl.pallas_call(
        deliver,
        out_shape=tuple(jax.ShapeDtypeStruct(*shape) for shape in shapes),
        in_specs=[vmem] * 3,
        out_specs=(hbm,) * 3,
        scratch_shapes=[pltpu.SemaphoreType.DMA((3,))],
        compiler_params=pltpu.CompilerParams(vmem_limit_bytes=8 * 1024 * 1024),
    )(*(pltpu.with_memory_space_constraint(one, pltpu.VMEM) for one in made))


def solution(mesh):
    in_specs = (
        P(("section", "rep"), None),
        P(),
        P(("section", "rep")),
        P("section", None),
        P(("section", "rep"), None),
    )
    out_specs = (P(("section", "rep"), None), P(("section", "rep"), None), P())
    coef = 4.0 / math.sqrt(128 * 256)
    return jax.shard_map(
        functools.partial(local, coef=coef), mesh=mesh, in_specs=in_specs, out_specs=out_specs,
        check_vma=False,
    )
```

```python
import functools
import math

import jax
import jax.numpy as jnp
from jax import lax
from jax.experimental import pallas as pl
from jax.experimental.pallas import tpu as pltpu
from jax.sharding import PartitionSpec as P


MESH = pl.DeviceIdType.MESH
NZ, NY, NX = 8, 8, 4
ROWS = 64
HALF = 128
MODULUS = 65521
OFFSET = (0, 1, 7, 2, 6, 3, 5, 4)
SLOT = {off: k for k, off in enumerate(OFFSET)}
GROUPS = ((0, 1), (1, 5), (5, 8))
COPIES = 80
BF16 = jnp.bfloat16
F32 = jnp.float32


def fold(v):
    return (v & 0xFFFF) + 15 * (v >> 16)


def reduce_once(v):
    return jnp.where(v >= MODULUS, v - MODULUS, v)


SCALE = 2.0 / MODULUS
WRAP = 1.0 - 0.5 * SCALE


def add_wrapped(u, step):
    total = u + step
    return jnp.where(total >= WRAP, total - 2.0, total)


def kernel(
    coef,
    feats_hbm, weight_hbm, scale_hbm, mask_hbm, cot_hbm,
    layer_out, grad_feats, grad_weight,
    feats, weight, scale_row, mask, cot, load_sems,
    adj, cm, gath, gath_t, masks, csend, crecv, acc, ysend, yrecv,
    near_send, near_recv, keep, keep_near, next_send, next_recv, zsend, zrecv,
    starts, steps, part, a1r, half, a2s, a2r, a3r, a4r, wbuf, scale_col,
    send_sems, recv_sems,
):
    sec = lax.axis_index("section")
    x = lax.axis_index("rep")
    c = sec % 2
    y = (sec // 2) % NY
    z = sec // (2 * NY)
    x_one = x + 1 - 2 * (x % 2)
    x_two = 3 - x
    x_opp = (x + 2) % NX

    def device(zz, yy, cc, xx):
        return ((zz * NY + yy) * 2 + cc, xx)

    sibling = device(z, y, 1 - c, x)
    east, west = device(z, y, c, x_one), device(z, y, c, x_two)

    def z_peer(e):
        return device((z + e) % NZ, y, c, x)

    def y_peer(e):
        return device(z, (y + e) % NY, c, x)

    def x_peer(e):
        return device(z, y, c, (x + e) % NX)

    loads = [
        pltpu.make_async_copy(src, dst, load_sems.at[n])
        for n, (src, dst) in enumerate((
            (feats_hbm, feats), (scale_hbm, scale_row), (mask_hbm, mask),
            (weight_hbm, weight), (cot_hbm, cot),
        ))
    ]
    for one in loads:
        one.start()

    barrier = pltpu.get_barrier_semaphore()
    peers = [z_peer(e) for e in range(1, NZ)] + [y_peer(e) for e in range(1, NY)]
    peers += [x_peer(e) for e in range(1, NX)] + [sibling]
    for peer in peers:
        pl.semaphore_signal(barrier, inc=1, device_id=peer, device_id_type=MESH)

    started = []
    numbers = iter(range(COPIES))

    class Batch:
        def __init__(self, view, target):
            number = next(numbers)
            self.send_sem, self.recv_sem = send_sems.at[number], recv_sems.at[number]
            self.whole = self.describe(view, view, target)
            started.append(self.whole)

        def describe(self, src, dst, target):
            return pltpu.make_async_remote_copy(
                src_ref=src, dst_ref=dst, send_sem=self.send_sem, recv_sem=self.recv_sem,
                device_id=target, device_id_type=MESH,
            )

        def start(self, src, dst, target):
            self.describe(src, dst, target).start()

        def wait_recv(self):
            self.whole.wait_recv()

    def copy(src, dst, target):
        one = Batch(dst, target)
        one.start(src, dst, target)
        return one

    col_j = lax.broadcasted_iota(jnp.int32, (16, 512), 1)
    row_i = lax.broadcasted_iota(jnp.int32, (16, 512), 0)
    col_slot = col_j >> 6
    col_off = jnp.where((col_slot & 1) == 1, (col_slot + 1) >> 1, (8 - (col_slot >> 1)) & 7)
    columns_x = (x, x_one, x_two, x_opp)

    def side_core(side):
        return 1 - c if side == 0 else c

    def mask_columns():
        which = lax.broadcasted_iota(jnp.int32, (16, HALF), 0)
        lane = lax.broadcasted_iota(jnp.int32, (16, HALF), 1)
        core_of = jnp.where(which < 8, 1 - c, c)
        tile = ((z * NY + (which & 7)) * 2 + core_of) * 2 + x // 2
        every = masks[...].reshape(64, HALF)
        dims = (((1,), (1,)), ((), ()))
        low = lax.dot_general((tile == lane).astype(F32), every, dims, preferred_element_type=F32)
        high = lax.dot_general(
            (tile == lane + HALF).astype(F32), every, dims, preferred_element_type=F32
        )
        entry = lax.broadcasted_iota(jnp.int32, (64, 512), 0)
        slot = lax.broadcasted_iota(jnp.int32, (64, 512), 1) >> 6
        off = jnp.where((slot & 1) == 1, (slot + 1) >> 1, (8 - (slot >> 1)) & 7)
        same = (entry >> 3) == ((z + off) & 7)
        for n, xx in enumerate(columns_x):
            pick_low = jnp.where(same & ((entry & 7) == xx // 2), 1.0, 0.0).astype(F32)
            pick_high = jnp.where(same & ((entry & 7) == xx // 2 + 2), 1.0, 0.0).astype(F32)
            chosen = jnp.dot(low, pick_low, preferred_element_type=F32) + jnp.dot(
                high, pick_high, preferred_element_type=F32
            )
            cm[:, n * 512:(n + 1) * 512] = jnp.where(chosen > 0.5, coef, 0.0)

    def column_ids(n):
        return ((((z + col_off) & 7) * NY + y) * 2 + c) * 256 + columns_x[n] * ROWS + (col_j & 63)

    def prepare(unit, a, b):
        first = fold(fold(a * b))
        hashed = reduce_once(fold(fold(first * 20011 + (a + b) * 7919)))
        starts[unit] = hashed.astype(F32) * SCALE - 1.0

    def prepare_steps(number, b, stride):
        step = reduce_once(fold(fold(b[0:8] * 20011 + 7919)))
        steps[number, 0] = reduce_once(fold(step * 16)).astype(F32) * SCALE
        steps[number, 1] = reduce_once(fold(step * stride)).astype(F32) * SCALE

    def prepare_block():
        for n in range(NX):
            b = column_ids(n)
            prepare_steps(n, b, 512)
            for side in range(2):
                a = ((z * NY) * 2 + side_core(side)) * 256 + x * ROWS + row_i
                prepare(n * 2 + side, a, b)

    def make_block(n, side):
        lanes = slice(n * 512, (n + 1) * 512)
        step16 = jnp.concatenate([steps[n, 0]] * 2, axis=0)
        leap = jnp.concatenate([steps[n, 1]] * 2, axis=0)

        def run(yy, u0):
            off = (yy - y + NY) % NY
            late = off // 5
            slot = (off + 7) // 8 * ((1 - late) * (2 * off - 1) + late * (16 - 2 * off))
            coefs = cm[pl.ds(side * 8 + yy, 1), lanes]
            u = u0
            for s in range(4):
                at = pl.multiple_of(side * 512 + slot * ROWS + s * 16, 16)
                adj[pl.ds(at, 16), lanes] = (u * coefs).astype(BF16)
                if s < 3:
                    u = add_wrapped(u, step16)
            return add_wrapped(u0, leap)

        lax.fori_loop(0, 8, run, starts[n * 2 + side])

    for one in loads[:3]:
        one.wait()
    row = scale_row[...].astype(F32)
    pick = lax.broadcasted_iota(jnp.int32, (ROWS, ROWS), 0) == lax.broadcasted_iota(
        jnp.int32, (ROWS, ROWS), 1
    )
    column = jnp.sum(jnp.where(pick, jnp.broadcast_to(row, (ROWS, ROWS)), 0.0), axis=1, keepdims=True)
    scale_col[...] = jnp.broadcast_to(column, (ROWS, 256))
    scaled = (scale_col[...] * feats[...].astype(F32)).astype(BF16)
    gath[0, 0, 0:ROWS] = scaled[:, :HALF]
    gath_t[0, 0, 0:ROWS] = scaled[:, HALF:]
    masks[z] = jnp.zeros((8, HALF), F32)
    masks[z, 0:2, :] = mask[:, 0:HALF].astype(F32)
    masks[z, 2:4, :] = mask[:, HALF:].astype(F32)

    pl.semaphore_wait(barrier, len(peers))

    def start_pass(p):
        own = gath.at[p, 0, pl.ds(0, ROWS)]
        own_t = gath_t.at[p, 0, pl.ds(0, ROWS)]
        state = {"z": {}, "one": {}, "two": {}, "opp": [], "y_t": {}, "core_t": []}
        for g, (lo, hi) in enumerate(GROUPS[1:], 1):
            run = pl.ds(lo * ROWS, (hi - lo) * ROWS)
            state["z"][g] = Batch(gath.at[p, 0, run], z_peer(1))
            state["y_t"][g] = Batch(gath_t.at[p, 0, run], y_peer(1))
        for k in range(1, 5):
            e = (NZ - OFFSET[k]) % NZ
            run = pl.ds(k * ROWS, ROWS)
            state["z"][1].start(own, gath.at[p, 0, run], z_peer(e))
            state["y_t"][1].start(own_t, gath_t.at[p, 0, run], y_peer(e))
            if k == 2:
                forward(p, 0, state)
        return state

    def spread(blocks, batch, peer):
        def rows(slot, lo, hi):
            return blocks.at[pl.ds(slot * ROWS + lo, hi - lo)]

        cut = ROWS // 2
        batch.start(rows(3, 0, ROWS), rows(5, 0, ROWS), peer(7))
        batch.start(rows(4, 0, ROWS), rows(6, 0, ROWS), peer(1))
        batch.start(rows(3, 0, cut), rows(7, 0, cut), peer(6))
        batch.start(rows(4, cut, ROWS), rows(7, cut, ROWS), peer(2))

    def spread_t(p, state):
        state["y_t"][1].wait_recv()
        spread(gath_t.at[p, 0], state["y_t"][2], y_peer)

    def forward_t(p, state):
        state["y_t"][2].wait_recv()
        state["core_t"].append(copy(gath_t.at[p, 0], gath_t.at[p, 1], sibling))

    def forward(p, g, state):
        lo, hi = GROUPS[g]
        if g:
            state["z"][g].wait_recv()
        if g == 1:
            spread(gath.at[p, 0], state["z"][2], z_peer)
        run = pl.ds(lo * ROWS, (hi - lo) * ROWS)
        state["one"][g] = copy(gath.at[p, 0, run], gath.at[p, 1, run], east)
        state["two"][g] = copy(gath.at[p, 0, run], gath.at[p, 2, run], west)

    def relay(p, g, state):
        lo, hi = GROUPS[g]
        size = (hi - lo) * ROWS // 2
        run = pl.ds(lo * ROWS, size)
        state["two"][g].wait_recv()
        state["opp"].append(copy(gath.at[p, 2, run], gath.at[p, 3, run], east))
        run = pl.ds(lo * ROWS + size, size)
        state["one"][g].wait_recv()
        state["opp"].append(copy(gath.at[p, 1, run], gath.at[p, 3, run], west))

    def finish_gather(state):
        for one in state["opp"]:
            one.wait_recv()

    def product(p, side):
        right = gath[p].reshape(NX * NZ * ROWS, HALF)
        value = jnp.dot(adj[side * 512:(side + 1) * 512, :], right, preferred_element_type=F32)
        if side == 0:
            csend[p] = value.astype(BF16)
        else:
            acc[...] = value

    def sums_first(p, state):
        product(p, 0)
        state["core"] = copy(csend.at[p], crecv.at[p], sibling)

    def sums_second(p, state):
        state["core"].wait_recv()
        total = acc[...] + crecv[p].astype(F32)
        acc[...] = total
        ysend[p] = total.astype(BF16)
        state["y"] = Batch(yrecv.at[p, pl.ds(1, NY - 1)], y_peer(1))
        for e in (4, 3, 5, 2, 6, 1, 7):
            run = pl.ds(SLOT[e] * ROWS, ROWS)
            state["y"].start(ysend.at[p, run], yrecv.at[p, e], y_peer(e))

    def sums_last(p, state):
        total = acc[0:ROWS]
        state["y"].wait_recv()
        for e in range(1, NY):
            total = total + yrecv[p, e].astype(F32)
        return total

    def product_t(p, lo, hi):
        dims = (((0,), (0,)), ((), ()))
        turned = lax.dot_general(
            gath_t[p, 1], adj[0:512, lo:hi], dims, preferred_element_type=F32
        ) + lax.dot_general(
            gath_t[p, 0], adj[512:1024, lo:hi], dims, preferred_element_type=F32
        )
        return turned.T

    def near_first(p, state):
        for one in state["core_t"]:
            one.wait_recv()
        opposite = product_t(p, 1536, 2048)
        near_send[p, 0, 256:512] = opposite[:256].astype(BF16)
        near_send[p, 1, 256:512] = opposite[256:].astype(BF16)
        far, close = pl.ds(256, 256), pl.ds(0, 256)
        state["far_e"] = copy(near_send.at[p, 0, far], near_recv.at[p, 0, far], east)
        state["far_w"] = copy(near_send.at[p, 1, far], near_recv.at[p, 1, far], west)
        near_send[p, 0, 0:256] = product_t(p, 512, 768).astype(BF16)
        state["near_e"] = copy(near_send.at[p, 0, close], near_recv.at[p, 0, close], east)
        near_send[p, 1, 0:256] = product_t(p, 1280, 1536).astype(BF16)
        state["near_w"] = copy(near_send.at[p, 1, close], near_recv.at[p, 1, close], west)

    def near_second(p):
        keep_near[0] = product_t(p, 1024, 1280)
        keep_near[1] = product_t(p, 768, 1024)

    def next_first(p, state):
        state["far_e"].wait_recv()
        next_send[p, 0] = (keep_near[0] + near_recv[p, 0, 256:512].astype(F32)).astype(BF16)
        state["next_w"] = copy(next_send.at[p, 0], next_recv.at[p, 0], west)
        state["far_w"].wait_recv()
        next_send[p, 1] = (keep_near[1] + near_recv[p, 1, 256:512].astype(F32)).astype(BF16)
        state["next_e"] = copy(next_send.at[p, 1], next_recv.at[p, 1], east)

    def next_own(p, state):
        value = product_t(p, 0, 512)
        state["near_e"].wait_recv()
        state["near_w"].wait_recv()
        keep[0:256] = value[:256] + near_recv[p, 0, 0:256].astype(F32)
        keep[256:512] = value[256:] + near_recv[p, 1, 0:256].astype(F32)

    def next_second(p, state):
        state["z_t"] = Batch(zrecv.at[p, pl.ds(1, NZ - 1)], z_peer(1))
        for part_at, arrival, offsets in ((1, "next_e", (4, 3, 5, 6)), (0, "next_w", (2, 1, 7))):
            state[arrival].wait_recv()
            rows = slice(part_at * 256, (part_at + 1) * 256)
            total = keep[rows] + next_recv[p, part_at].astype(F32)
            zsend[p, rows] = total.astype(BF16)
            for e in offsets:
                run = pl.ds(SLOT[e] * ROWS, ROWS)
                state["z_t"].start(zsend.at[p, run], zrecv.at[p, e], z_peer(e))
        keep[0:ROWS] = total[0:ROWS]

    def sums_last_t(p, state):
        total = keep[0:ROWS]
        state["z_t"].wait_recv()
        for e in range(1, NZ):
            total = total + zrecv[p, e].astype(F32)
        return total

    mask_copies = Batch(masks.at[pl.ds(0, NZ - 1)], z_peer(1))
    for e in range(1, NZ):
        mask_copies.start(masks.at[z], masks.at[z], z_peer(e))
    state = start_pass(0)
    prepare_block()
    mask_copies.wait_recv()
    forward(0, 1, state)
    spread_t(0, state)
    relay(0, 0, state)
    mask_columns()
    make_block(3, 0)
    make_block(3, 1)
    make_block(1, 0)
    make_block(1, 1)
    forward_t(0, state)
    forward(0, 2, state)
    relay(0, 1, state)
    make_block(2, 0)
    make_block(2, 1)
    near_first(0, state)
    relay(0, 2, state)
    near_second(0)
    make_block(0, 0)
    make_block(0, 1)
    next_first(0, state)
    finish_gather(state)
    sums_first(0, state)
    next_own(0, state)
    product(0, 1)
    next_second(0, state)
    sums_second(0, state)
    sums = jnp.concatenate([sums_last(0, state), sums_last_t(0, state)], axis=1)

    for one in loads[3:]:
        one.wait()
    sums_high = sums.astype(BF16)
    sums_low = (sums - sums_high.astype(F32)).astype(BF16)
    scale = scale_col[...]
    presum = scale * (
        jnp.dot(sums_high, weight[...], preferred_element_type=F32)
        + jnp.dot(sums_low, weight[...], preferred_element_type=F32)
    )
    sigma = jax.nn.sigmoid(presum)
    layer_out[...] = (presum * sigma).astype(BF16)
    deriv = sigma * (1.0 + presum * (1.0 - sigma))
    error = (scale * cot[...].astype(F32) * deriv).astype(BF16)
    gath[1, 0, 0:ROWS] = error[:, :HALF]
    gath_t[1, 0, 0:ROWS] = error[:, HALF:]

    earlier = list(started)

    state = start_pass(1)
    dims = (((0,), (0,)), ((), ()))
    part[...] = lax.dot_general(
        sums_high, error, dims, preferred_element_type=F32
    ) + lax.dot_general(sums_low, error, dims, preferred_element_type=F32)
    theirs = pl.multiple_of((1 - c) * 128, 128)
    mine = pl.multiple_of(c * 128, 128)
    first = copy(part.at[pl.ds(theirs, 128)], a1r, sibling)
    forward(1, 1, state)
    spread_t(1, state)
    relay(1, 0, state)
    for one in earlier:
        one.wait_send()

    first.wait_recv()
    half[...] = part[pl.ds(mine, 128), :] + a1r[...]
    a2s[...] = half[...].astype(BF16)
    second = Batch(a2r.at[pl.ds(1, NY - 1)], y_peer(1))
    for e in range(1, NY):
        at = pl.multiple_of(((y + e) % NY) * 16, 16)
        second.start(a2s.at[pl.ds(at, 16)], a2r.at[e], y_peer(e))

    forward_t(1, state)
    forward(1, 2, state)
    relay(1, 1, state)
    near_first(1, state)

    piece = half[pl.ds(pl.multiple_of(y * 16, 16), 16), :]
    second.wait_recv()
    for e in range(1, NY):
        piece = piece + a2r[e].astype(F32)
    a3r[z] = piece.astype(BF16)
    third = Batch(a3r.at[pl.ds(0, NZ - 1)], z_peer(1))
    for e in range(1, NZ):
        third.start(a3r.at[z], a3r.at[z], z_peer(e))

    relay(1, 2, state)
    near_second(1)
    next_first(1, state)
    finish_gather(state)
    sums_first(1, state)

    third.wait_recv()
    piece = a3r[0].astype(F32)
    for n in range(1, NZ):
        piece = piece + a3r[n].astype(F32)
    a4r[x] = piece
    fourth = Batch(a4r.at[pl.ds(0, NX - 1)], x_peer(1))
    for e in range(1, NX):
        fourth.start(a4r.at[x], a4r.at[x], x_peer(e))

    next_own(1, state)
    product(1, 1)
    next_second(1, state)

    fourth.wait_recv()
    piece = (a4r[0] + a4r[1]) + (a4r[2] + a4r[3])
    at = pl.multiple_of(c * 128 + y * 16, 16)
    wbuf[pl.ds(at, 16), :] = piece.astype(BF16)
    fifth = Batch(wbuf.at[pl.ds(0, 16 * (NY - 1))], y_peer(1))
    for e in range(1, NY):
        fifth.start(wbuf.at[pl.ds(at, 16)], wbuf.at[pl.ds(at, 16)], y_peer(e))
    sums_second(1, state)
    fifth.wait_recv()
    sixth = copy(wbuf.at[pl.ds(mine, 128)], wbuf.at[pl.ds(mine, 128)], sibling)
    back = jnp.concatenate([sums_last(1, state), sums_last_t(1, state)], axis=1)
    vgrad = (scale * back).astype(BF16)
    grad_feats[...] = lax.dot_general(
        vgrad, weight[...], (((1,), (1,)), ((), ())), preferred_element_type=F32
    ).astype(BF16)
    sixth.wait_recv()
    grad_weight[...] = wbuf[...].astype(F32)
    for one in started[len(earlier):]:
        one.wait_send()


def deliver(*refs):
    sems = refs[-1]
    copies = [pltpu.make_async_copy(refs[n], refs[n + 3], sems.at[n]) for n in range(3)]
    for one in copies:
        one.start()
    for one in copies:
        one.wait()


def local(node_feats, weight, node_scale, tile_mask, cotangent, coef):
    hidden = weight.shape[0]
    hbm = pl.BlockSpec(memory_space=pltpu.HBM)
    vmem = pl.BlockSpec(memory_space=pltpu.VMEM)
    shapes = (((ROWS, hidden), BF16), ((ROWS, hidden), BF16), ((hidden, hidden), F32))
    args = (node_feats, weight, node_scale.reshape(1, ROWS), tile_mask, cotangent)
    made = pl.pallas_call(
        functools.partial(kernel, coef),
        out_shape=tuple(pltpu.VMEM(*shape) for shape in shapes),
        in_specs=[hbm] * 5,
        out_specs=(vmem,) * 3,
        scratch_shapes=[
            pltpu.VMEM((ROWS, hidden), BF16),
            pltpu.VMEM((hidden, hidden), BF16),
            pltpu.VMEM((1, ROWS), BF16),
            pltpu.VMEM(tile_mask.shape, jnp.int32),
            pltpu.VMEM((ROWS, hidden), BF16),
            pltpu.SemaphoreType.DMA((5,)),
            pltpu.VMEM((1024, 2048), BF16),
            pltpu.VMEM((16, 2048), F32),
            pltpu.VMEM((2, NX, NZ * ROWS, HALF), BF16),
            pltpu.VMEM((2, 2, NY * ROWS, HALF), BF16),
            pltpu.VMEM((NZ, 8, HALF), F32),
            pltpu.VMEM((2, 512, HALF), BF16),
            pltpu.VMEM((2, 512, HALF), BF16),
            pltpu.VMEM((512, HALF), F32),
            pltpu.VMEM((2, 512, HALF), BF16),
            pltpu.VMEM((2, NY, ROWS, HALF), BF16),
            pltpu.VMEM((2, 2, 512, HALF), BF16),
            pltpu.VMEM((2, 2, 512, HALF), BF16),
            pltpu.VMEM((512, HALF), F32),
            pltpu.VMEM((2, 256, HALF), F32),
            pltpu.VMEM((2, 2, 256, HALF), BF16),
            pltpu.VMEM((2, 2, 256, HALF), BF16),
            pltpu.VMEM((2, 512, HALF), BF16),
            pltpu.VMEM((2, NZ, ROWS, HALF), BF16),
            pltpu.VMEM((8, 16, 512), F32),
            pltpu.VMEM((NX, 2, 8, 512), F32),
            pltpu.VMEM((256, 256), F32),
            pltpu.VMEM((128, 256), F32),
            pltpu.VMEM((128, 256), F32),
            pltpu.VMEM((128, 256), BF16),
            pltpu.VMEM((NY, 16, 256), BF16),
            pltpu.VMEM((NZ, 16, 256), BF16),
            pltpu.VMEM((NX, 16, 256), F32),
            pltpu.VMEM((256, 256), BF16),
            pltpu.VMEM((ROWS, 256), F32),
            pltpu.SemaphoreType.DMA((COPIES,)),
            pltpu.SemaphoreType.DMA((COPIES,)),
        ],
        compiler_params=pltpu.CompilerParams(
            collective_id=0, has_side_effects=True, vmem_limit_bytes=40 * 1024 * 1024
        ),
    )(*(pltpu.with_memory_space_constraint(arg, pltpu.HBM) for arg in args))
    return pl.pallas_call(
        deliver,
        out_shape=tuple(jax.ShapeDtypeStruct(*shape) for shape in shapes),
        in_specs=[vmem] * 3,
        out_specs=(hbm,) * 3,
        scratch_shapes=[pltpu.SemaphoreType.DMA((3,))],
        compiler_params=pltpu.CompilerParams(vmem_limit_bytes=8 * 1024 * 1024),
    )(*(pltpu.with_memory_space_constraint(one, pltpu.VMEM) for one in made))


def solution(mesh):
    in_specs = (
        P(("section", "rep"), None),
        P(),
        P(("section", "rep")),
        P("section", None),
        P(("section", "rep"), None),
    )
    out_specs = (P(("section", "rep"), None), P(("section", "rep"), None), P())
    coef = 4.0 / math.sqrt(128 * 256)
    return jax.shard_map(
        functools.partial(local, coef=coef), mesh=mesh, in_specs=in_specs, out_specs=out_specs,
        check_vma=False,
    )
```

```python
import functools
import math

import jax
import jax.numpy as jnp
from jax import lax
from jax.experimental import pallas as pl
from jax.experimental.pallas import tpu as pltpu
from jax.sharding import PartitionSpec as P


MESH = pl.DeviceIdType.MESH
NZ, NY, NX = 8, 8, 4
ROWS = 64
HALF = 128
MODULUS = 65521
OFFSET = (0, 1, 7, 2, 6, 3, 5, 4)
SLOT = {off: k for k, off in enumerate(OFFSET)}
GROUPS = ((0, 1), (1, 5), (5, 8))
COPIES = 80
BOARD = tuple((d, e) for d in range(2) for e in range(NX) if d or e)
BF16 = jnp.bfloat16
F32 = jnp.float32


def fold(v):
    return (v & 0xFFFF) + 15 * (v >> 16)


def reduce_once(v):
    return jnp.where(v >= MODULUS, v - MODULUS, v)


SCALE = 2.0 / MODULUS
WRAP = 1.0 - 0.5 * SCALE


def add_wrapped(u, step):
    total = u + step
    return jnp.where(total >= WRAP, total - 2.0, total)


def kernel(
    coef,
    feats_hbm, weight_hbm, scale_hbm, mask_hbm, cot_hbm,
    layer_out, grad_feats, grad_weight,
    feats, weight, scale_row, mask, cot, load_sems,
    adj, cm, gath, gath_t, masks, csend, crecv, acc, ysend, yrecv,
    near_send, near_recv, keep, keep_near, next_send, next_recv, zsend, zrecv,
    starts, steps, part, part_low, board_in, tiles, tiles_in, ring, whole, wbuf, scale_col,
    send_sems, recv_sems,
):
    sec = lax.axis_index("section")
    x = lax.axis_index("rep")
    c = sec % 2
    y = (sec // 2) % NY
    z = sec // (2 * NY)
    x_one = x + 1 - 2 * (x % 2)
    x_two = 3 - x
    x_opp = (x + 2) % NX

    def device(zz, yy, cc, xx):
        return ((zz * NY + yy) * 2 + cc, xx)

    sibling = device(z, y, 1 - c, x)
    east, west = device(z, y, c, x_one), device(z, y, c, x_two)

    def z_peer(e):
        return device((z + e) % NZ, y, c, x)

    def y_peer(e):
        return device(z, (y + e) % NY, c, x)

    def board_index(d, e):
        return (c + d) % 2 * NX + (x + e) % NX

    def board_peer(d, e):
        return device(z, y, (c + d) % 2, (x + e) % NX)

    loads = [
        pltpu.make_async_copy(src, dst, load_sems.at[n])
        for n, (src, dst) in enumerate((
            (feats_hbm, feats), (scale_hbm, scale_row), (mask_hbm, mask),
            (weight_hbm, weight), (cot_hbm, cot),
        ))
    ]
    for one in loads:
        one.start()

    barrier = pltpu.get_barrier_semaphore()
    peers = [z_peer(e) for e in range(1, NZ)] + [y_peer(e) for e in range(1, NY)]
    peers += [board_peer(d, e) for d, e in BOARD]
    for peer in peers:
        pl.semaphore_signal(barrier, inc=1, device_id=peer, device_id_type=MESH)

    started = []
    numbers = iter(range(COPIES))

    class Batch:
        def __init__(self, view, target):
            number = next(numbers)
            self.send_sem, self.recv_sem = send_sems.at[number], recv_sems.at[number]
            self.whole = self.describe(view, view, target)
            started.append(self.whole)

        def describe(self, src, dst, target):
            return pltpu.make_async_remote_copy(
                src_ref=src, dst_ref=dst, send_sem=self.send_sem, recv_sem=self.recv_sem,
                device_id=target, device_id_type=MESH,
            )

        def start(self, src, dst, target):
            self.describe(src, dst, target).start()

        def wait_recv(self):
            self.whole.wait_recv()

    def copy(src, dst, target):
        one = Batch(dst, target)
        one.start(src, dst, target)
        return one

    col_j = lax.broadcasted_iota(jnp.int32, (16, 512), 1)
    row_i = lax.broadcasted_iota(jnp.int32, (16, 512), 0)
    col_slot = col_j >> 6
    col_off = jnp.where((col_slot & 1) == 1, (col_slot + 1) >> 1, (8 - (col_slot >> 1)) & 7)
    columns_x = (x, x_one, x_two, x_opp)

    def side_core(side):
        return 1 - c if side == 0 else c

    def mask_columns():
        which = lax.broadcasted_iota(jnp.int32, (16, HALF), 0)
        lane = lax.broadcasted_iota(jnp.int32, (16, HALF), 1)
        core_of = jnp.where(which < 8, 1 - c, c)
        tile = ((z * NY + (which & 7)) * 2 + core_of) * 2 + x // 2
        every = masks[...].reshape(64, HALF)
        dims = (((1,), (1,)), ((), ()))
        low = lax.dot_general((tile == lane).astype(F32), every, dims, preferred_element_type=F32)
        high = lax.dot_general(
            (tile == lane + HALF).astype(F32), every, dims, preferred_element_type=F32
        )
        entry = lax.broadcasted_iota(jnp.int32, (64, 512), 0)
        slot = lax.broadcasted_iota(jnp.int32, (64, 512), 1) >> 6
        off = jnp.where((slot & 1) == 1, (slot + 1) >> 1, (8 - (slot >> 1)) & 7)
        same = (entry >> 3) == ((z + off) & 7)
        for n, xx in enumerate(columns_x):
            pick_low = jnp.where(same & ((entry & 7) == xx // 2), 1.0, 0.0).astype(F32)
            pick_high = jnp.where(same & ((entry & 7) == xx // 2 + 2), 1.0, 0.0).astype(F32)
            chosen = jnp.dot(low, pick_low, preferred_element_type=F32) + jnp.dot(
                high, pick_high, preferred_element_type=F32
            )
            cm[:, n * 512:(n + 1) * 512] = jnp.where(chosen > 0.5, coef, 0.0)

    def column_ids(n):
        return ((((z + col_off) & 7) * NY + y) * 2 + c) * 256 + columns_x[n] * ROWS + (col_j & 63)

    def prepare(unit, a, b):
        first = fold(fold(a * b))
        hashed = reduce_once(fold(fold(first * 20011 + (a + b) * 7919)))
        starts[unit] = hashed.astype(F32) * SCALE - 1.0

    def prepare_steps(number, b, stride):
        step = reduce_once(fold(fold(b[0:8] * 20011 + 7919)))
        steps[number, 0] = reduce_once(fold(step * 16)).astype(F32) * SCALE
        steps[number, 1] = reduce_once(fold(step * stride)).astype(F32) * SCALE

    def prepare_block():
        for n in range(NX):
            b = column_ids(n)
            prepare_steps(n, b, 512)
            for side in range(2):
                a = ((z * NY) * 2 + side_core(side)) * 256 + x * ROWS + row_i
                prepare(n * 2 + side, a, b)

    def make_block(n, side):
        lanes = slice(n * 512, (n + 1) * 512)
        step16 = jnp.concatenate([steps[n, 0]] * 2, axis=0)
        leap = jnp.concatenate([steps[n, 1]] * 2, axis=0)

        def run(yy, u0):
            off = (yy - y + NY) % NY
            late = off // 5
            slot = (off + 7) // 8 * ((1 - late) * (2 * off - 1) + late * (16 - 2 * off))
            coefs = cm[pl.ds(side * 8 + yy, 1), lanes]
            u = u0
            for s in range(4):
                at = pl.multiple_of(side * 512 + slot * ROWS + s * 16, 16)
                adj[pl.ds(at, 16), lanes] = (u * coefs).astype(BF16)
                if s < 3:
                    u = add_wrapped(u, step16)
            return add_wrapped(u0, leap)

        lax.fori_loop(0, 8, run, starts[n * 2 + side])

    for one in loads[:3]:
        one.wait()
    row = scale_row[...].astype(F32)
    pick = lax.broadcasted_iota(jnp.int32, (ROWS, ROWS), 0) == lax.broadcasted_iota(
        jnp.int32, (ROWS, ROWS), 1
    )
    column = jnp.sum(jnp.where(pick, jnp.broadcast_to(row, (ROWS, ROWS)), 0.0), axis=1, keepdims=True)
    scale_col[...] = jnp.broadcast_to(column, (ROWS, 256))
    scaled = (scale_col[...] * feats[...].astype(F32)).astype(BF16)
    gath[0, 0, 0:ROWS] = scaled[:, :HALF]
    gath_t[0, 0, 0:ROWS] = scaled[:, HALF:]
    masks[z] = jnp.zeros((8, HALF), F32)
    masks[z, 0:2, :] = mask[:, 0:HALF].astype(F32)
    masks[z, 2:4, :] = mask[:, HALF:].astype(F32)

    pl.semaphore_wait(barrier, len(peers))

    def start_pass(p):
        own = gath.at[p, 0, pl.ds(0, ROWS)]
        own_t = gath_t.at[p, 0, pl.ds(0, ROWS)]
        state = {"z": {}, "one": {}, "two": {}, "opp": [], "y_t": {}, "core_t": []}
        for g, (lo, hi) in enumerate(GROUPS[1:], 1):
            state["z"][g] = Batch(gath.at[p, 0, pl.ds(lo * ROWS, (hi - lo) * ROWS)], z_peer(1))
        state["y_t"] = Batch(gath_t.at[p, 0, pl.ds(ROWS, (NY - 1) * ROWS)], y_peer(1))
        for k in range(1, NZ):
            e = (NZ - OFFSET[k]) % NZ
            g = 1 if k < GROUPS[1][1] else 2
            state["z"][g].start(own, gath.at[p, 0, pl.ds(k * ROWS, ROWS)], z_peer(e))
            far = NY - k
            e = (NY - OFFSET[far]) % NY
            state["y_t"].start(own_t, gath_t.at[p, 0, pl.ds(far * ROWS, ROWS)], y_peer(e))
            if k == 2:
                forward(p, 0, state)
        return state

    def forward_t(p, state):
        state["y_t"].wait_recv()
        state["core_t"].append(copy(gath_t.at[p, 0], gath_t.at[p, 1], sibling))

    def forward(p, g, state):
        lo, hi = GROUPS[g]
        if g:
            state["z"][g].wait_recv()
        run = pl.ds(lo * ROWS, (hi - lo) * ROWS)
        state["one"][g] = copy(gath.at[p, 0, run], gath.at[p, 1, run], east)
        state["two"][g] = copy(gath.at[p, 0, run], gath.at[p, 2, run], west)

    def relay(p, g, state):
        lo, hi = GROUPS[g]
        size = (hi - lo) * ROWS // 2
        run = pl.ds(lo * ROWS, size)
        state["two"][g].wait_recv()
        state["opp"].append(copy(gath.at[p, 2, run], gath.at[p, 3, run], east))
        run = pl.ds(lo * ROWS + size, size)
        state["one"][g].wait_recv()
        state["opp"].append(copy(gath.at[p, 1, run], gath.at[p, 3, run], west))

    def finish_gather(state):
        for one in state["opp"]:
            one.wait_recv()

    def product(p, side):
        right = gath[p].reshape(NX * NZ * ROWS, HALF)
        value = jnp.dot(adj[side * 512:(side + 1) * 512, :], right, preferred_element_type=F32)
        if side == 0:
            csend[p] = value.astype(BF16)
        else:
            acc[...] = value

    def sums_first(p, state):
        product(p, 0)
        state["core"] = copy(csend.at[p], crecv.at[p], sibling)

    def sums_second(p, state):
        state["core"].wait_recv()
        total = acc[...] + crecv[p].astype(F32)
        acc[...] = total
        ysend[p] = total.astype(BF16)
        state["y"] = Batch(yrecv.at[p, pl.ds(1, NY - 1)], y_peer(1))
        for e in (4, 3, 5, 2, 6, 1, 7):
            run = pl.ds(SLOT[e] * ROWS, ROWS)
            state["y"].start(ysend.at[p, run], yrecv.at[p, e], y_peer(e))

    def sums_last(p, state):
        total = acc[0:ROWS]
        state["y"].wait_recv()
        for e in range(1, NY):
            total = total + yrecv[p, e].astype(F32)
        return total

    def product_t(p, lo, hi):
        dims = (((0,), (0,)), ((), ()))
        turned = lax.dot_general(
            gath_t[p, 1], adj[0:512, lo:hi], dims, preferred_element_type=F32
        ) + lax.dot_general(
            gath_t[p, 0], adj[512:1024, lo:hi], dims, preferred_element_type=F32
        )
        return turned.T

    def near_first(p, state):
        for one in state["core_t"]:
            one.wait_recv()
        opposite = product_t(p, 1536, 2048)
        near_send[p, 0, 256:512] = opposite[:256].astype(BF16)
        near_send[p, 1, 256:512] = opposite[256:].astype(BF16)
        far, close = pl.ds(256, 256), pl.ds(0, 256)
        state["far_e"] = copy(near_send.at[p, 0, far], near_recv.at[p, 0, far], east)
        state["far_w"] = copy(near_send.at[p, 1, far], near_recv.at[p, 1, far], west)
        near_send[p, 0, 0:256] = product_t(p, 512, 768).astype(BF16)
        state["near_e"] = copy(near_send.at[p, 0, close], near_recv.at[p, 0, close], east)
        near_send[p, 1, 0:256] = product_t(p, 1280, 1536).astype(BF16)
        state["near_w"] = copy(near_send.at[p, 1, close], near_recv.at[p, 1, close], west)

    def near_second(p):
        keep_near[0] = product_t(p, 1024, 1280)
        keep_near[1] = product_t(p, 768, 1024)

    def next_first(p, state):
        state["far_e"].wait_recv()
        next_send[p, 0] = (keep_near[0] + near_recv[p, 0, 256:512].astype(F32)).astype(BF16)
        state["next_w"] = copy(next_send.at[p, 0], next_recv.at[p, 0], west)
        state["far_w"].wait_recv()
        next_send[p, 1] = (keep_near[1] + near_recv[p, 1, 256:512].astype(F32)).astype(BF16)
        state["next_e"] = copy(next_send.at[p, 1], next_recv.at[p, 1], east)

    def next_own(p, state):
        value = product_t(p, 0, 512)
        state["near_e"].wait_recv()
        state["near_w"].wait_recv()
        keep[0:256] = value[:256] + near_recv[p, 0, 0:256].astype(F32)
        keep[256:512] = value[256:] + near_recv[p, 1, 0:256].astype(F32)

    def next_second(p, state):
        state["z_t"] = Batch(zrecv.at[p, pl.ds(1, NZ - 1)], z_peer(1))
        for part_at, arrival, offsets in ((1, "next_e", (4, 3, 5, 6)), (0, "next_w", (2, 1, 7))):
            state[arrival].wait_recv()
            rows = slice(part_at * 256, (part_at + 1) * 256)
            total = keep[rows] + next_recv[p, part_at].astype(F32)
            zsend[p, rows] = total.astype(BF16)
            for e in offsets:
                run = pl.ds(SLOT[e] * ROWS, ROWS)
                state["z_t"].start(zsend.at[p, run], zrecv.at[p, e], z_peer(e))
        keep[0:ROWS] = total[0:ROWS]

    def sums_last_t(p, state):
        total = keep[0:ROWS]
        state["z_t"].wait_recv()
        for e in range(1, NZ):
            total = total + zrecv[p, e].astype(F32)
        return total

    mask_copies = Batch(masks.at[pl.ds(0, NZ - 1)], z_peer(1))
    for e in range(1, NZ):
        mask_copies.start(masks.at[z], masks.at[z], z_peer(e))
    state = start_pass(0)
    prepare_block()
    mask_copies.wait_recv()
    mask_columns()
    make_block(3, 0)
    relay(0, 0, state)
    make_block(3, 1)
    forward(0, 1, state)
    make_block(1, 0)
    make_block(1, 1)
    forward_t(0, state)
    forward(0, 2, state)
    relay(0, 1, state)
    make_block(2, 0)
    make_block(2, 1)
    near_first(0, state)
    relay(0, 2, state)
    near_second(0)
    make_block(0, 0)
    make_block(0, 1)
    next_first(0, state)
    finish_gather(state)
    sums_first(0, state)
    next_own(0, state)
    product(0, 1)
    next_second(0, state)
    sums_second(0, state)
    sums = jnp.concatenate([sums_last(0, state), sums_last_t(0, state)], axis=1)

    for one in loads[3:]:
        one.wait()
    sums_high = sums.astype(BF16)
    sums_low = (sums - sums_high.astype(F32)).astype(BF16)
    scale = scale_col[...]
    presum = scale * (
        jnp.dot(sums_high, weight[...], preferred_element_type=F32)
        + jnp.dot(sums_low, weight[...], preferred_element_type=F32)
    )
    sigma = jax.nn.sigmoid(presum)
    layer_out[...] = (presum * sigma).astype(BF16)
    deriv = sigma * (1.0 + presum * (1.0 - sigma))
    error = (scale * cot[...].astype(F32) * deriv).astype(BF16)
    gath[1, 0, 0:ROWS] = error[:, :HALF]
    gath_t[1, 0, 0:ROWS] = error[:, HALF:]

    earlier = list(started)

    state = start_pass(1)
    dims = (((0,), (0,)), ((), ()))
    part[...] = lax.dot_general(
        sums_high, error, dims, preferred_element_type=F32
    ) + lax.dot_general(sums_low, error, dims, preferred_element_type=F32)
    part_low[...] = part[...].astype(BF16)
    board = c * NX + x
    first = Batch(board_in.at[pl.ds(0, 7)], board_peer(0, 1))
    for d, e in BOARD:
        at = pl.multiple_of(board_index(d, e) * 32, 32)
        first.start(part_low.at[pl.ds(at, 32)], board_in.at[d * NX + e], board_peer(d, e))
    for one in earlier:
        one.wait_send()
    relay(1, 0, state)
    forward(1, 1, state)

    forward_t(1, state)
    forward(1, 2, state)
    relay(1, 1, state)

    first.wait_recv()
    piece = part[pl.ds(pl.multiple_of(board * 32, 32), 32), :]
    for d, e in BOARD:
        piece = piece + board_in[d * NX + e].astype(F32)
    for n in range(NY):
        tiles[n] = piece[n // 2 * 8:n // 2 * 8 + 8, n % 2 * HALF:(n % 2 + 1) * HALF]
    second = Batch(tiles_in.at[pl.ds(1, NY - 1)], y_peer(1))
    for e in range(1, NY):
        second.start(tiles.at[(y + e) % NY], tiles_in.at[e], y_peer(e))

    near_first(1, state)
    relay(1, 2, state)
    near_second(1)

    second.wait_recv()
    tile = tiles[y]
    for e in range(1, NY):
        tile = tile + tiles_in[e]
    ring[z] = tile
    third = Batch(ring.at[pl.ds(0, NZ - 1)], z_peer(1))
    for e in range(1, NZ):
        third.start(ring.at[z], ring.at[z], z_peer(e))

    next_first(1, state)
    finish_gather(state)
    sums_first(1, state)

    third.wait_recv()
    tile = ring[0]
    for n in range(1, NZ):
        tile = tile + ring[n]
    whole[y] = tile
    fourth = Batch(whole.at[pl.ds(0, NY - 1)], y_peer(1))
    for e in range(1, NY):
        fourth.start(whole.at[y], whole.at[y], y_peer(e))

    next_own(1, state)
    product(1, 1)
    sums_second(1, state)
    next_second(1, state)

    fourth.wait_recv()
    rows = [jnp.concatenate([whole[2 * n], whole[2 * n + 1]], axis=1) for n in range(4)]
    run = pl.ds(pl.multiple_of(board * 32, 32), 32)
    wbuf[run, :] = jnp.concatenate(rows, axis=0).astype(BF16)
    fifth = Batch(wbuf.at[pl.ds(0, 7 * 32)], board_peer(0, 1))
    for d, e in BOARD:
        fifth.start(wbuf.at[run], wbuf.at[run], board_peer(d, e))
    back = jnp.concatenate([sums_last(1, state), sums_last_t(1, state)], axis=1)
    vgrad = (scale * back).astype(BF16)
    grad_feats[...] = lax.dot_general(
        vgrad, weight[...], (((1,), (1,)), ((), ())), preferred_element_type=F32
    ).astype(BF16)
    fifth.wait_recv()
    grad_weight[...] = wbuf[...].astype(F32)
    for one in started[len(earlier):]:
        one.wait_send()


def deliver(*refs):
    sems = refs[-1]
    copies = [pltpu.make_async_copy(refs[n], refs[n + 3], sems.at[n]) for n in range(3)]
    for one in copies:
        one.start()
    for one in copies:
        one.wait()


def local(node_feats, weight, node_scale, tile_mask, cotangent, coef):
    hidden = weight.shape[0]
    hbm = pl.BlockSpec(memory_space=pltpu.HBM)
    vmem = pl.BlockSpec(memory_space=pltpu.VMEM)
    shapes = (((ROWS, hidden), BF16), ((ROWS, hidden), BF16), ((hidden, hidden), F32))
    args = (node_feats, weight, node_scale.reshape(1, ROWS), tile_mask, cotangent)
    made = pl.pallas_call(
        functools.partial(kernel, coef),
        out_shape=tuple(pltpu.VMEM(*shape) for shape in shapes),
        in_specs=[hbm] * 5,
        out_specs=(vmem,) * 3,
        scratch_shapes=[
            pltpu.VMEM((ROWS, hidden), BF16),
            pltpu.VMEM((hidden, hidden), BF16),
            pltpu.VMEM((1, ROWS), BF16),
            pltpu.VMEM(tile_mask.shape, jnp.int32),
            pltpu.VMEM((ROWS, hidden), BF16),
            pltpu.SemaphoreType.DMA((5,)),
            pltpu.VMEM((1024, 2048), BF16),
            pltpu.VMEM((16, 2048), F32),
            pltpu.VMEM((2, NX, NZ * ROWS, HALF), BF16),
            pltpu.VMEM((2, 2, NY * ROWS, HALF), BF16),
            pltpu.VMEM((NZ, 8, HALF), F32),
            pltpu.VMEM((2, 512, HALF), BF16),
            pltpu.VMEM((2, 512, HALF), BF16),
            pltpu.VMEM((512, HALF), F32),
            pltpu.VMEM((2, 512, HALF), BF16),
            pltpu.VMEM((2, NY, ROWS, HALF), BF16),
            pltpu.VMEM((2, 2, 512, HALF), BF16),
            pltpu.VMEM((2, 2, 512, HALF), BF16),
            pltpu.VMEM((512, HALF), F32),
            pltpu.VMEM((2, 256, HALF), F32),
            pltpu.VMEM((2, 2, 256, HALF), BF16),
            pltpu.VMEM((2, 2, 256, HALF), BF16),
            pltpu.VMEM((2, 512, HALF), BF16),
            pltpu.VMEM((2, NZ, ROWS, HALF), BF16),
            pltpu.VMEM((8, 16, 512), F32),
            pltpu.VMEM((NX, 2, 8, 512), F32),
            pltpu.VMEM((256, 256), F32),
            pltpu.VMEM((256, 256), BF16),
            pltpu.VMEM((2 * NX, 32, 256), BF16),
            pltpu.VMEM((NY, 8, HALF), F32),
            pltpu.VMEM((NY, 8, HALF), F32),
            pltpu.VMEM((NZ, 8, HALF), F32),
            pltpu.VMEM((NY, 8, HALF), F32),
            pltpu.VMEM((256, 256), BF16),
            pltpu.VMEM((ROWS, 256), F32),
            pltpu.SemaphoreType.DMA((COPIES,)),
            pltpu.SemaphoreType.DMA((COPIES,)),
        ],
        compiler_params=pltpu.CompilerParams(
            collective_id=0, has_side_effects=True, vmem_limit_bytes=40 * 1024 * 1024
        ),
    )(*(pltpu.with_memory_space_constraint(arg, pltpu.HBM) for arg in args))
    return pl.pallas_call(
        deliver,
        out_shape=tuple(jax.ShapeDtypeStruct(*shape) for shape in shapes),
        in_specs=[vmem] * 3,
        out_specs=(hbm,) * 3,
        scratch_shapes=[pltpu.SemaphoreType.DMA((3,))],
        compiler_params=pltpu.CompilerParams(vmem_limit_bytes=8 * 1024 * 1024),
    )(*(pltpu.with_memory_space_constraint(one, pltpu.VMEM) for one in made))


def solution(mesh):
    in_specs = (
        P(("section", "rep"), None),
        P(),
        P(("section", "rep")),
        P("section", None),
        P(("section", "rep"), None),
    )
    out_specs = (P(("section", "rep"), None), P(("section", "rep"), None), P())
    coef = 4.0 / math.sqrt(128 * 256)
    return jax.shard_map(
        functools.partial(local, coef=coef), mesh=mesh, in_specs=in_specs, out_specs=out_specs,
        check_vma=False,
    )
```

```python
import functools
import math

import jax
import jax.numpy as jnp
from jax import lax
from jax.experimental import pallas as pl
from jax.experimental.pallas import tpu as pltpu
from jax.sharding import PartitionSpec as P


MESH = pl.DeviceIdType.MESH
NZ, NY, NX = 8, 8, 4
ROWS = 64
HALF = 128
MODULUS = 65521
OFFSET = (0, 1, 7, 2, 6, 3, 5, 4)
SLOT = {off: k for k, off in enumerate(OFFSET)}
GROUPS = ((0, 1), (1, 5), (5, 8))
COPIES = 80
BF16 = jnp.bfloat16
F32 = jnp.float32


def fold(v):
    return (v & 0xFFFF) + 15 * (v >> 16)


def reduce_once(v):
    return jnp.where(v >= MODULUS, v - MODULUS, v)


SCALE = 2.0 / MODULUS
WRAP = 1.0 - 0.5 * SCALE


def add_wrapped(u, step):
    total = u + step
    return jnp.where(total >= WRAP, total - 2.0, total)


def kernel(
    coef,
    feats_hbm, weight_hbm, scale_hbm, mask_hbm, cot_hbm,
    layer_out, grad_feats, grad_weight,
    feats, weight, scale_row, mask, cot, load_sems,
    adj, cm, gath, gath_t, masks, csend, crecv, acc, ysend, yrecv,
    near_send, near_recv, keep, keep_near, next_send, next_recv, zsend, zrecv,
    begun, begun_t, starts, steps, part, a1r, half, a2s, a2r, a3r, a4r, wbuf, scale_col,
    send_sems, recv_sems,
):
    sec = lax.axis_index("section")
    x = lax.axis_index("rep")
    c = sec % 2
    y = (sec // 2) % NY
    z = sec // (2 * NY)
    x_one = x + 1 - 2 * (x % 2)
    x_two = 3 - x
    x_opp = (x + 2) % NX

    def device(zz, yy, cc, xx):
        return ((zz * NY + yy) * 2 + cc, xx)

    sibling = device(z, y, 1 - c, x)
    east, west = device(z, y, c, x_one), device(z, y, c, x_two)

    def z_peer(e):
        return device((z + e) % NZ, y, c, x)

    def y_peer(e):
        return device(z, (y + e) % NY, c, x)

    def x_peer(e):
        return device(z, y, c, (x + e) % NX)

    loads = [
        pltpu.make_async_copy(src, dst, load_sems.at[n])
        for n, (src, dst) in enumerate((
            (feats_hbm, feats), (scale_hbm, scale_row), (mask_hbm, mask),
            (weight_hbm, weight), (cot_hbm, cot),
        ))
    ]
    for one in loads:
        one.start()

    barrier = pltpu.get_barrier_semaphore()
    peers = [z_peer(e) for e in range(1, NZ)] + [y_peer(e) for e in range(1, NY)]
    peers += [x_peer(e) for e in range(1, NX)] + [sibling]
    for peer in peers:
        pl.semaphore_signal(barrier, inc=1, device_id=peer, device_id_type=MESH)

    started = []
    numbers = iter(range(COPIES))

    class Batch:
        def __init__(self, view, target):
            number = next(numbers)
            self.send_sem, self.recv_sem = send_sems.at[number], recv_sems.at[number]
            self.whole = self.describe(view, view, target)
            started.append(self.whole)

        def describe(self, src, dst, target):
            return pltpu.make_async_remote_copy(
                src_ref=src, dst_ref=dst, send_sem=self.send_sem, recv_sem=self.recv_sem,
                device_id=target, device_id_type=MESH,
            )

        def start(self, src, dst, target):
            self.describe(src, dst, target).start()

        def wait_recv(self):
            self.whole.wait_recv()

    def copy(src, dst, target):
        one = Batch(dst, target)
        one.start(src, dst, target)
        return one

    col_j = lax.broadcasted_iota(jnp.int32, (16, 512), 1)
    row_i = lax.broadcasted_iota(jnp.int32, (16, 512), 0)
    col_slot = col_j >> 6
    col_off = jnp.where((col_slot & 1) == 1, (col_slot + 1) >> 1, (8 - (col_slot >> 1)) & 7)
    columns_x = (x, x_one, x_two, x_opp)

    def side_core(side):
        return 1 - c if side == 0 else c

    def mask_columns():
        which = lax.broadcasted_iota(jnp.int32, (16, HALF), 0)
        lane = lax.broadcasted_iota(jnp.int32, (16, HALF), 1)
        core_of = jnp.where(which < 8, 1 - c, c)
        tile = ((z * NY + (which & 7)) * 2 + core_of) * 2 + x // 2
        every = masks[...].reshape(64, HALF)
        dims = (((1,), (1,)), ((), ()))
        low = lax.dot_general((tile == lane).astype(F32), every, dims, preferred_element_type=F32)
        high = lax.dot_general(
            (tile == lane + HALF).astype(F32), every, dims, preferred_element_type=F32
        )
        entry = lax.broadcasted_iota(jnp.int32, (64, 512), 0)
        slot = lax.broadcasted_iota(jnp.int32, (64, 512), 1) >> 6
        off = jnp.where((slot & 1) == 1, (slot + 1) >> 1, (8 - (slot >> 1)) & 7)
        same = (entry >> 3) == ((z + off) & 7)
        for n, xx in enumerate(columns_x):
            pick_low = jnp.where(same & ((entry & 7) == xx // 2), 1.0, 0.0).astype(F32)
            pick_high = jnp.where(same & ((entry & 7) == xx // 2 + 2), 1.0, 0.0).astype(F32)
            chosen = jnp.dot(low, pick_low, preferred_element_type=F32) + jnp.dot(
                high, pick_high, preferred_element_type=F32
            )
            cm[:, n * 512:(n + 1) * 512] = jnp.where(chosen > 0.5, coef, 0.0)

    def column_ids(n):
        return ((((z + col_off) & 7) * NY + y) * 2 + c) * 256 + columns_x[n] * ROWS + (col_j & 63)

    def prepare(unit, a, b):
        first = fold(fold(a * b))
        hashed = reduce_once(fold(fold(first * 20011 + (a + b) * 7919)))
        starts[unit] = hashed.astype(F32) * SCALE - 1.0

    def prepare_steps(number, b, stride):
        step = reduce_once(fold(fold(b[0:8] * 20011 + 7919)))
        steps[number, 0] = reduce_once(fold(step * 16)).astype(F32) * SCALE
        steps[number, 1] = reduce_once(fold(step * stride)).astype(F32) * SCALE

    def prepare_block():
        for n in range(NX):
            b = column_ids(n)
            prepare_steps(n, b, 512)
            for side in range(2):
                a = ((z * NY) * 2 + side_core(side)) * 256 + x * ROWS + row_i
                prepare(n * 2 + side, a, b)

    def make_block(n, side):
        lanes = slice(n * 512, (n + 1) * 512)
        step16 = jnp.concatenate([steps[n, 0]] * 2, axis=0)
        leap = jnp.concatenate([steps[n, 1]] * 2, axis=0)

        def run(yy, u0):
            off = (yy - y + NY) % NY
            late = off // 5
            slot = (off + 7) // 8 * ((1 - late) * (2 * off - 1) + late * (16 - 2 * off))
            coefs = cm[pl.ds(side * 8 + yy, 1), lanes]
            u = u0
            for s in range(4):
                at = pl.multiple_of(side * 512 + slot * ROWS + s * 16, 16)
                adj[pl.ds(at, 16), lanes] = (u * coefs).astype(BF16)
                if s < 3:
                    u = add_wrapped(u, step16)
            return add_wrapped(u0, leap)

        lax.fori_loop(0, 8, run, starts[n * 2 + side])

    for one in loads[:3]:
        one.wait()
    row = scale_row[...].astype(F32)
    pick = lax.broadcasted_iota(jnp.int32, (ROWS, ROWS), 0) == lax.broadcasted_iota(
        jnp.int32, (ROWS, ROWS), 1
    )
    column = jnp.sum(jnp.where(pick, jnp.broadcast_to(row, (ROWS, ROWS)), 0.0), axis=1, keepdims=True)
    scale_col[...] = jnp.broadcast_to(column, (ROWS, 256))
    scaled = (scale_col[...] * feats[...].astype(F32)).astype(BF16)
    gath[0, 0, 0:ROWS] = scaled[:, :HALF]
    gath_t[0, 0, 0:ROWS] = scaled[:, HALF:]
    masks[z] = jnp.zeros((8, HALF), F32)
    masks[z, 0:2, :] = mask[:, 0:HALF].astype(F32)
    masks[z, 2:4, :] = mask[:, HALF:].astype(F32)

    pl.semaphore_wait(barrier, len(peers))

    def start_pass(p):
        own = gath.at[p, 0, pl.ds(0, ROWS)]
        own_t = gath_t.at[p, 0, pl.ds(0, ROWS)]
        state = {"z": {}, "one": {}, "two": {}, "opp": [], "y_t": {}, "core_t": []}
        for g, (lo, hi) in enumerate(GROUPS[1:], 1):
            state["z"][g] = Batch(gath.at[p, 0, pl.ds(lo * ROWS, (hi - lo) * ROWS)], z_peer(1))
        state["y_t"] = Batch(gath_t.at[p, 0, pl.ds(ROWS, (NY - 1) * ROWS)], y_peer(1))
        for k in range(1, NZ):
            e = (NZ - OFFSET[k]) % NZ
            g = 1 if k < GROUPS[1][1] else 2
            state["z"][g].start(own, gath.at[p, 0, pl.ds(k * ROWS, ROWS)], z_peer(e))
            far = NY - k
            e = (NY - OFFSET[far]) % NY
            state["y_t"].start(own_t, gath_t.at[p, 0, pl.ds(far * ROWS, ROWS)], y_peer(e))
            if k == 2:
                forward(p, 0, state)
        return state

    def forward_t(p, state):
        state["y_t"].wait_recv()
        state["core_t"].append(copy(gath_t.at[p, 0], gath_t.at[p, 1], sibling))

    def forward(p, g, state):
        lo, hi = GROUPS[g]
        if g:
            state["z"][g].wait_recv()
        run = pl.ds(lo * ROWS, (hi - lo) * ROWS)
        state["one"][g] = copy(gath.at[p, 0, run], gath.at[p, 1, run], east)
        state["two"][g] = copy(gath.at[p, 0, run], gath.at[p, 2, run], west)

    def relay(p, g, state):
        lo, hi = GROUPS[g]
        size = (hi - lo) * ROWS // 2
        run = pl.ds(lo * ROWS, size)
        state["two"][g].wait_recv()
        state["opp"].append(copy(gath.at[p, 2, run], gath.at[p, 3, run], east))
        run = pl.ds(lo * ROWS + size, size)
        state["one"][g].wait_recv()
        state["opp"].append(copy(gath.at[p, 1, run], gath.at[p, 3, run], west))

    def finish_gather(state):
        for one in state["opp"]:
            one.wait_recv()

    def early(p):
        right = gath[p, 0:3].reshape(3 * NZ * ROWS, HALF)
        begun[...] = jnp.dot(adj[0:512, 0:1536], right, preferred_element_type=F32)

    def sums_first(p, state):
        rest = jnp.dot(adj[0:512, 1536:2048], gath[p, 3], preferred_element_type=F32)
        csend[p] = (begun[...] + rest).astype(BF16)
        state["core"] = copy(csend.at[p], crecv.at[p], sibling)

    def product(p):
        right = gath[p].reshape(NX * NZ * ROWS, HALF)
        acc[...] = jnp.dot(adj[512:1024, :], right, preferred_element_type=F32)

    def sums_second(p, state):
        state["core"].wait_recv()
        total = acc[...] + crecv[p].astype(F32)
        acc[...] = total
        ysend[p] = total.astype(BF16)
        state["y"] = Batch(yrecv.at[p, pl.ds(1, NY - 1)], y_peer(1))
        for e in (4, 3, 5, 2, 6, 1, 7):
            run = pl.ds(SLOT[e] * ROWS, ROWS)
            state["y"].start(ysend.at[p, run], yrecv.at[p, e], y_peer(e))

    def sums_last(p, state):
        total = acc[0:ROWS]
        state["y"].wait_recv()
        for e in range(1, NY):
            total = total + yrecv[p, e].astype(F32)
        return total

    def early_t(p):
        for n in range(NX):
            lanes = slice(n * 512, (n + 1) * 512)
            begun_t[:, lanes] = lax.dot_general(
                gath_t[p, 0], adj[512:1024, lanes], (((0,), (0,)), ((), ())),
                preferred_element_type=F32,
            )

    def product_t(p, lo, hi):
        rest = lax.dot_general(
            gath_t[p, 1], adj[0:512, lo:hi], (((0,), (0,)), ((), ())), preferred_element_type=F32
        )
        return (begun_t[:, lo:hi] + rest).T

    def near_first(p, state):
        for one in state["core_t"]:
            one.wait_recv()
        opposite = product_t(p, 1536, 2048)
        near_send[p, 0, 256:512] = opposite[:256].astype(BF16)
        near_send[p, 1, 256:512] = opposite[256:].astype(BF16)
        far, close = pl.ds(256, 256), pl.ds(0, 256)
        state["far_e"] = copy(near_send.at[p, 0, far], near_recv.at[p, 0, far], east)
        state["far_w"] = copy(near_send.at[p, 1, far], near_recv.at[p, 1, far], west)
        near_send[p, 0, 0:256] = product_t(p, 512, 768).astype(BF16)
        state["near_e"] = copy(near_send.at[p, 0, close], near_recv.at[p, 0, close], east)
        near_send[p, 1, 0:256] = product_t(p, 1280, 1536).astype(BF16)
        state["near_w"] = copy(near_send.at[p, 1, close], near_recv.at[p, 1, close], west)

    def near_second(p):
        keep_near[0] = product_t(p, 1024, 1280)
        keep_near[1] = product_t(p, 768, 1024)

    def next_first(p, state):
        state["far_e"].wait_recv()
        next_send[p, 0] = (keep_near[0] + near_recv[p, 0, 256:512].astype(F32)).astype(BF16)
        state["next_w"] = copy(next_send.at[p, 0], next_recv.at[p, 0], west)
        state["far_w"].wait_recv()
        next_send[p, 1] = (keep_near[1] + near_recv[p, 1, 256:512].astype(F32)).astype(BF16)
        state["next_e"] = copy(next_send.at[p, 1], next_recv.at[p, 1], east)

    def next_own(p, state):
        value = product_t(p, 0, 512)
        state["near_e"].wait_recv()
        state["near_w"].wait_recv()
        keep[0:256] = value[:256] + near_recv[p, 0, 0:256].astype(F32)
        keep[256:512] = value[256:] + near_recv[p, 1, 0:256].astype(F32)

    def next_second(p, state):
        state["z_t"] = Batch(zrecv.at[p, pl.ds(1, NZ - 1)], z_peer(1))
        for part_at, arrival, offsets in ((1, "next_e", (4, 3, 5, 6)), (0, "next_w", (2, 1, 7))):
            state[arrival].wait_recv()
            rows = slice(part_at * 256, (part_at + 1) * 256)
            total = keep[rows] + next_recv[p, part_at].astype(F32)
            zsend[p, rows] = total.astype(BF16)
            for e in offsets:
                run = pl.ds(SLOT[e] * ROWS, ROWS)
                state["z_t"].start(zsend.at[p, run], zrecv.at[p, e], z_peer(e))
        keep[0:ROWS] = total[0:ROWS]

    def sums_last_t(p, state):
        total = keep[0:ROWS]
        state["z_t"].wait_recv()
        for e in range(1, NZ):
            total = total + zrecv[p, e].astype(F32)
        return total

    mask_copies = Batch(masks.at[pl.ds(0, NZ - 1)], z_peer(1))
    for e in range(1, NZ):
        mask_copies.start(masks.at[z], masks.at[z], z_peer(e))
    state = start_pass(0)
    prepare_block()
    mask_copies.wait_recv()
    mask_columns()
    make_block(3, 1)
    relay(0, 0, state)
    make_block(1, 1)
    forward(0, 1, state)
    make_block(2, 1)
    make_block(0, 1)
    forward_t(0, state)
    forward(0, 2, state)
    relay(0, 1, state)
    make_block(3, 0)
    early_t(0)
    make_block(1, 0)
    make_block(2, 0)
    near_first(0, state)
    relay(0, 2, state)
    near_second(0)
    make_block(0, 0)
    early(0)
    next_first(0, state)
    finish_gather(state)
    sums_first(0, state)
    next_own(0, state)
    product(0)
    next_second(0, state)
    sums_second(0, state)
    sums = jnp.concatenate([sums_last(0, state), sums_last_t(0, state)], axis=1)

    for one in loads[3:]:
        one.wait()
    sums_high = sums.astype(BF16)
    sums_low = (sums - sums_high.astype(F32)).astype(BF16)
    scale = scale_col[...]
    presum = scale * (
        jnp.dot(sums_high, weight[...], preferred_element_type=F32)
        + jnp.dot(sums_low, weight[...], preferred_element_type=F32)
    )
    sigma = jax.nn.sigmoid(presum)
    layer_out[...] = (presum * sigma).astype(BF16)
    deriv = sigma * (1.0 + presum * (1.0 - sigma))
    error = (scale * cot[...].astype(F32) * deriv).astype(BF16)
    gath[1, 0, 0:ROWS] = error[:, :HALF]
    gath_t[1, 0, 0:ROWS] = error[:, HALF:]

    earlier = list(started)

    state = start_pass(1)
    dims = (((0,), (0,)), ((), ()))
    part[...] = lax.dot_general(
        sums_high, error, dims, preferred_element_type=F32
    ) + lax.dot_general(sums_low, error, dims, preferred_element_type=F32)
    theirs = pl.multiple_of((1 - c) * 128, 128)
    mine = pl.multiple_of(c * 128, 128)
    first = copy(part.at[pl.ds(theirs, 128)], a1r, sibling)
    for one in earlier:
        one.wait_send()
    relay(1, 0, state)
    forward(1, 1, state)

    first.wait_recv()
    half[...] = part[pl.ds(mine, 128), :] + a1r[...]
    a2s[...] = half[...].astype(BF16)
    second = Batch(a2r.at[pl.ds(1, NY - 1)], y_peer(1))
    for e in range(1, NY):
        at = pl.multiple_of(((y + e) % NY) * 16, 16)
        second.start(a2s.at[pl.ds(at, 16)], a2r.at[e], y_peer(e))

    forward_t(1, state)
    forward(1, 2, state)
    relay(1, 1, state)
    early_t(1)
    near_first(1, state)

    piece = half[pl.ds(pl.multiple_of(y * 16, 16), 16), :]
    second.wait_recv()
    for e in range(1, NY):
        piece = piece + a2r[e].astype(F32)
    a3r[z] = piece.astype(BF16)
    third = Batch(a3r.at[pl.ds(0, NZ - 1)], z_peer(1))
    for e in range(1, NZ):
        third.start(a3r.at[z], a3r.at[z], z_peer(e))

    relay(1, 2, state)
    near_second(1)
    early(1)
    next_first(1, state)
    finish_gather(state)
    sums_first(1, state)

    third.wait_recv()
    piece = a3r[0].astype(F32)
    for n in range(1, NZ):
        piece = piece + a3r[n].astype(F32)
    a4r[x] = piece
    fourth = Batch(a4r.at[pl.ds(0, NX - 1)], x_peer(1))
    for e in range(1, NX):
        fourth.start(a4r.at[x], a4r.at[x], x_peer(e))

    next_own(1, state)
    product(1)
    next_second(1, state)

    fourth.wait_recv()
    piece = (a4r[0] + a4r[1]) + (a4r[2] + a4r[3])
    at = pl.multiple_of(c * 128 + y * 16, 16)
    wbuf[pl.ds(at, 16), :] = piece.astype(BF16)
    fifth = Batch(wbuf.at[pl.ds(0, 16 * (NY - 1))], y_peer(1))
    for e in range(1, NY):
        fifth.start(wbuf.at[pl.ds(at, 16)], wbuf.at[pl.ds(at, 16)], y_peer(e))
    sums_second(1, state)
    fifth.wait_recv()
    sixth = copy(wbuf.at[pl.ds(mine, 128)], wbuf.at[pl.ds(mine, 128)], sibling)
    back = jnp.concatenate([sums_last(1, state), sums_last_t(1, state)], axis=1)
    vgrad = (scale * back).astype(BF16)
    grad_feats[...] = lax.dot_general(
        vgrad, weight[...], (((1,), (1,)), ((), ())), preferred_element_type=F32
    ).astype(BF16)
    sixth.wait_recv()
    grad_weight[...] = wbuf[...].astype(F32)
    for one in started[len(earlier):]:
        one.wait_send()


def deliver(*refs):
    sems = refs[-1]
    copies = [pltpu.make_async_copy(refs[n], refs[n + 3], sems.at[n]) for n in range(3)]
    for one in copies:
        one.start()
    for one in copies:
        one.wait()


def local(node_feats, weight, node_scale, tile_mask, cotangent, coef):
    hidden = weight.shape[0]
    hbm = pl.BlockSpec(memory_space=pltpu.HBM)
    vmem = pl.BlockSpec(memory_space=pltpu.VMEM)
    shapes = (((ROWS, hidden), BF16), ((ROWS, hidden), BF16), ((hidden, hidden), F32))
    args = (node_feats, weight, node_scale.reshape(1, ROWS), tile_mask, cotangent)
    made = pl.pallas_call(
        functools.partial(kernel, coef),
        out_shape=tuple(pltpu.VMEM(*shape) for shape in shapes),
        in_specs=[hbm] * 5,
        out_specs=(vmem,) * 3,
        scratch_shapes=[
            pltpu.VMEM((ROWS, hidden), BF16),
            pltpu.VMEM((hidden, hidden), BF16),
            pltpu.VMEM((1, ROWS), BF16),
            pltpu.VMEM(tile_mask.shape, jnp.int32),
            pltpu.VMEM((ROWS, hidden), BF16),
            pltpu.SemaphoreType.DMA((5,)),
            pltpu.VMEM((1024, 2048), BF16),
            pltpu.VMEM((16, 2048), F32),
            pltpu.VMEM((2, NX, NZ * ROWS, HALF), BF16),
            pltpu.VMEM((2, 2, NY * ROWS, HALF), BF16),
            pltpu.VMEM((NZ, 8, HALF), F32),
            pltpu.VMEM((2, 512, HALF), BF16),
            pltpu.VMEM((2, 512, HALF), BF16),
            pltpu.VMEM((512, HALF), F32),
            pltpu.VMEM((2, 512, HALF), BF16),
            pltpu.VMEM((2, NY, ROWS, HALF), BF16),
            pltpu.VMEM((2, 2, 512, HALF), BF16),
            pltpu.VMEM((2, 2, 512, HALF), BF16),
            pltpu.VMEM((512, HALF), F32),
            pltpu.VMEM((2, 256, HALF), F32),
            pltpu.VMEM((2, 2, 256, HALF), BF16),
            pltpu.VMEM((2, 2, 256, HALF), BF16),
            pltpu.VMEM((2, 512, HALF), BF16),
            pltpu.VMEM((2, NZ, ROWS, HALF), BF16),
            pltpu.VMEM((512, HALF), F32),
            pltpu.VMEM((HALF, 2048), F32),
            pltpu.VMEM((8, 16, 512), F32),
            pltpu.VMEM((NX, 2, 8, 512), F32),
            pltpu.VMEM((256, 256), F32),
            pltpu.VMEM((128, 256), F32),
            pltpu.VMEM((128, 256), F32),
            pltpu.VMEM((128, 256), BF16),
            pltpu.VMEM((NY, 16, 256), BF16),
            pltpu.VMEM((NZ, 16, 256), BF16),
            pltpu.VMEM((NX, 16, 256), F32),
            pltpu.VMEM((256, 256), BF16),
            pltpu.VMEM((ROWS, 256), F32),
            pltpu.SemaphoreType.DMA((COPIES,)),
            pltpu.SemaphoreType.DMA((COPIES,)),
        ],
        compiler_params=pltpu.CompilerParams(
            collective_id=0, has_side_effects=True, vmem_limit_bytes=40 * 1024 * 1024
        ),
    )(*(pltpu.with_memory_space_constraint(arg, pltpu.HBM) for arg in args))
    return pl.pallas_call(
        deliver,
        out_shape=tuple(jax.ShapeDtypeStruct(*shape) for shape in shapes),
        in_specs=[vmem] * 3,
        out_specs=(hbm,) * 3,
        scratch_shapes=[pltpu.SemaphoreType.DMA((3,))],
        compiler_params=pltpu.CompilerParams(vmem_limit_bytes=8 * 1024 * 1024),
    )(*(pltpu.with_memory_space_constraint(one, pltpu.VMEM) for one in made))


def solution(mesh):
    in_specs = (
        P(("section", "rep"), None),
        P(),
        P(("section", "rep")),
        P("section", None),
        P(("section", "rep"), None),
    )
    out_specs = (P(("section", "rep"), None), P(("section", "rep"), None), P())
    coef = 4.0 / math.sqrt(128 * 256)
    return jax.shard_map(
        functools.partial(local, coef=coef), mesh=mesh, in_specs=in_specs, out_specs=out_specs,
        check_vma=False,
    )
```

```python
import functools
import math

import jax
import jax.numpy as jnp
from jax import lax
from jax.experimental import pallas as pl
from jax.experimental.pallas import tpu as pltpu
from jax.sharding import PartitionSpec as P


MESH = pl.DeviceIdType.MESH
NZ, NY, NX = 8, 8, 4
ROWS = 64
HALF = 128
MODULUS = 65521
OFFSET = (0, 1, 7, 2, 6, 3, 5, 4)
SLOT = {off: k for k, off in enumerate(OFFSET)}
GROUPS = ((0, 1), (1, 5), (5, 8))
COPIES = 80
BF16 = jnp.bfloat16
F32 = jnp.float32


def fold(v):
    return (v & 0xFFFF) + 15 * (v >> 16)


def reduce_once(v):
    return jnp.where(v >= MODULUS, v - MODULUS, v)


SCALE = 2.0 / MODULUS
WRAP = 1.0 - 0.5 * SCALE


def add_wrapped(u, step):
    total = u + step
    return jnp.where(total >= WRAP, total - 2.0, total)


def kernel(
    coef,
    feats_hbm, weight_hbm, scale_hbm, mask_hbm, cot_hbm,
    layer_out, grad_feats, grad_weight,
    feats, weight, scale_row, mask, cot, load_sems,
    adj, cm, gath, gath_t, masks, csend, crecv, acc, ysend, yrecv,
    near_send, near_recv, keep, keep_near, next_send, next_recv, zsend, zrecv,
    begun, begun_t, starts, steps, part, a1r, half, a2s, a2r, a3r, a4r, wbuf, scale_col,
    send_sems, recv_sems,
):
    sec = lax.axis_index("section")
    x = lax.axis_index("rep")
    c = sec % 2
    y = (sec // 2) % NY
    z = sec // (2 * NY)
    x_one = x + 1 - 2 * (x % 2)
    x_two = 3 - x
    x_opp = (x + 2) % NX

    def device(zz, yy, cc, xx):
        return ((zz * NY + yy) * 2 + cc, xx)

    sibling = device(z, y, 1 - c, x)
    east, west = device(z, y, c, x_one), device(z, y, c, x_two)

    def z_peer(e):
        return device((z + e) % NZ, y, c, x)

    def y_peer(e):
        return device(z, (y + e) % NY, c, x)

    def x_peer(e):
        return device(z, y, c, (x + e) % NX)

    loads = [
        pltpu.make_async_copy(src, dst, load_sems.at[n])
        for n, (src, dst) in enumerate((
            (feats_hbm, feats), (scale_hbm, scale_row), (mask_hbm, mask),
            (weight_hbm, weight), (cot_hbm, cot),
        ))
    ]
    for one in loads:
        one.start()

    barrier = pltpu.get_barrier_semaphore()
    peers = [z_peer(e) for e in range(1, NZ)] + [y_peer(e) for e in range(1, NY)]
    peers += [x_peer(e) for e in range(1, NX)] + [sibling]
    for peer in peers:
        pl.semaphore_signal(barrier, inc=1, device_id=peer, device_id_type=MESH)

    started = []
    numbers = iter(range(COPIES))

    class Batch:
        def __init__(self, view, target):
            number = next(numbers)
            self.send_sem, self.recv_sem = send_sems.at[number], recv_sems.at[number]
            self.whole = self.describe(view, view, target)
            started.append(self.whole)

        def describe(self, src, dst, target):
            return pltpu.make_async_remote_copy(
                src_ref=src, dst_ref=dst, send_sem=self.send_sem, recv_sem=self.recv_sem,
                device_id=target, device_id_type=MESH,
            )

        def start(self, src, dst, target):
            self.describe(src, dst, target).start()

        def wait_recv(self):
            self.whole.wait_recv()

    def copy(src, dst, target):
        one = Batch(dst, target)
        one.start(src, dst, target)
        return one

    col_j = lax.broadcasted_iota(jnp.int32, (16, 512), 1)
    row_i = lax.broadcasted_iota(jnp.int32, (16, 512), 0)
    col_slot = col_j >> 6
    col_off = jnp.where((col_slot & 1) == 1, (col_slot + 1) >> 1, (8 - (col_slot >> 1)) & 7)
    columns_x = (x, x_one, x_two, x_opp)

    def side_core(side):
        return 1 - c if side == 0 else c

    def mask_columns():
        which = lax.broadcasted_iota(jnp.int32, (16, HALF), 0)
        lane = lax.broadcasted_iota(jnp.int32, (16, HALF), 1)
        core_of = jnp.where(which < 8, 1 - c, c)
        tile = ((z * NY + (which & 7)) * 2 + core_of) * 2 + x // 2
        every = masks[...].reshape(64, HALF)
        dims = (((1,), (1,)), ((), ()))
        low = lax.dot_general((tile == lane).astype(F32), every, dims, preferred_element_type=F32)
        high = lax.dot_general(
            (tile == lane + HALF).astype(F32), every, dims, preferred_element_type=F32
        )
        entry = lax.broadcasted_iota(jnp.int32, (64, 512), 0)
        slot = lax.broadcasted_iota(jnp.int32, (64, 512), 1) >> 6
        off = jnp.where((slot & 1) == 1, (slot + 1) >> 1, (8 - (slot >> 1)) & 7)
        same = (entry >> 3) == ((z + off) & 7)
        for n, xx in enumerate(columns_x):
            pick_low = jnp.where(same & ((entry & 7) == xx // 2), 1.0, 0.0).astype(F32)
            pick_high = jnp.where(same & ((entry & 7) == xx // 2 + 2), 1.0, 0.0).astype(F32)
            chosen = jnp.dot(low, pick_low, preferred_element_type=F32) + jnp.dot(
                high, pick_high, preferred_element_type=F32
            )
            cm[:, n * 512:(n + 1) * 512] = jnp.where(chosen > 0.5, coef, 0.0)

    def column_ids(n):
        return ((((z + col_off) & 7) * NY + y) * 2 + c) * 256 + columns_x[n] * ROWS + (col_j & 63)

    def prepare(unit, a, b):
        first = fold(fold(a * b))
        hashed = reduce_once(fold(fold(first * 20011 + (a + b) * 7919)))
        starts[unit] = hashed.astype(F32) * SCALE - 1.0

    def prepare_steps(number, b, stride):
        step = reduce_once(fold(fold(b[0:8] * 20011 + 7919)))
        steps[number, 0] = reduce_once(fold(step * 16)).astype(F32) * SCALE
        steps[number, 1] = reduce_once(fold(step * stride)).astype(F32) * SCALE

    def prepare_block():
        for n in range(NX):
            b = column_ids(n)
            prepare_steps(n, b, 512)
            for side in range(2):
                a = ((z * NY) * 2 + side_core(side)) * 256 + x * ROWS + row_i
                prepare(n * 2 + side, a, b)

    def make_block(n, side):
        lanes = slice(n * 512, (n + 1) * 512)
        step16 = jnp.concatenate([steps[n, 0]] * 2, axis=0)
        leap = jnp.concatenate([steps[n, 1]] * 2, axis=0)

        def run(yy, u0):
            off = (yy - y + NY) % NY
            late = off // 5
            slot = (off + 7) // 8 * ((1 - late) * (2 * off - 1) + late * (16 - 2 * off))
            coefs = cm[pl.ds(side * 8 + yy, 1), lanes]
            u = u0
            for s in range(4):
                at = pl.multiple_of(side * 512 + slot * ROWS + s * 16, 16)
                adj[pl.ds(at, 16), lanes] = (u * coefs).astype(BF16)
                if s < 3:
                    u = add_wrapped(u, step16)
            return add_wrapped(u0, leap)

        lax.fori_loop(0, 8, run, starts[n * 2 + side])

    for one in loads[:3]:
        one.wait()
    row = scale_row[...].astype(F32)
    pick = lax.broadcasted_iota(jnp.int32, (ROWS, ROWS), 0) == lax.broadcasted_iota(
        jnp.int32, (ROWS, ROWS), 1
    )
    column = jnp.sum(jnp.where(pick, jnp.broadcast_to(row, (ROWS, ROWS)), 0.0), axis=1, keepdims=True)
    scale_col[...] = jnp.broadcast_to(column, (ROWS, 256))
    scaled = (scale_col[...] * feats[...].astype(F32)).astype(BF16)
    gath[0, 0, 0:ROWS] = scaled[:, :HALF]
    gath_t[0, 0, 0:ROWS] = scaled[:, HALF:]
    masks[z] = jnp.zeros((8, HALF), F32)
    masks[z, 0:2, :] = mask[:, 0:HALF].astype(F32)
    masks[z, 2:4, :] = mask[:, HALF:].astype(F32)

    pl.semaphore_wait(barrier, len(peers))

    def start_pass(p):
        own = gath.at[p, 0, pl.ds(0, ROWS)]
        own_t = gath_t.at[p, 0, pl.ds(0, ROWS)]
        state = {"z": {}, "one": {}, "two": {}, "opp": [], "y_t": {}, "core_t": []}
        for g, (lo, hi) in enumerate(GROUPS[1:], 1):
            state["z"][g] = Batch(gath.at[p, 0, pl.ds(lo * ROWS, (hi - lo) * ROWS)], z_peer(1))
        state["y_t"] = Batch(gath_t.at[p, 0, pl.ds(ROWS, (NY - 1) * ROWS)], y_peer(1))
        for k in range(1, NZ):
            e = (NZ - OFFSET[k]) % NZ
            g = 1 if k < GROUPS[1][1] else 2
            state["z"][g].start(own, gath.at[p, 0, pl.ds(k * ROWS, ROWS)], z_peer(e))
            far = NY - k
            e = (NY - OFFSET[far]) % NY
            state["y_t"].start(own_t, gath_t.at[p, 0, pl.ds(far * ROWS, ROWS)], y_peer(e))
            if k == 2:
                forward(p, 0, state)
        return state

    def forward_t(p, state):
        state["y_t"].wait_recv()
        state["core_t"].append(copy(gath_t.at[p, 0], gath_t.at[p, 1], sibling))

    def forward(p, g, state):
        lo, hi = GROUPS[g]
        if g:
            state["z"][g].wait_recv()
        run = pl.ds(lo * ROWS, (hi - lo) * ROWS)
        state["one"][g] = copy(gath.at[p, 0, run], gath.at[p, 1, run], east)
        state["two"][g] = copy(gath.at[p, 0, run], gath.at[p, 2, run], west)

    def relay(p, g, state):
        lo, hi = GROUPS[g]
        size = (hi - lo) * ROWS // 2
        run = pl.ds(lo * ROWS, size)
        state["two"][g].wait_recv()
        state["opp"].append(copy(gath.at[p, 2, run], gath.at[p, 3, run], east))
        run = pl.ds(lo * ROWS + size, size)
        state["one"][g].wait_recv()
        state["opp"].append(copy(gath.at[p, 1, run], gath.at[p, 3, run], west))

    def finish_gather(state):
        for one in state["opp"]:
            one.wait_recv()

    def early(p):
        right = gath[p, 0:3].reshape(3 * NZ * ROWS, HALF)
        begun[...] = jnp.dot(adj[0:512, 0:1536], right, preferred_element_type=F32)

    def sums_first(p, state):
        rest = jnp.dot(adj[0:512, 1536:2048], gath[p, 3], preferred_element_type=F32)
        csend[p] = (begun[...] + rest).astype(BF16)
        state["core"] = copy(csend.at[p], crecv.at[p], sibling)

    def product(p):
        right = gath[p].reshape(NX * NZ * ROWS, HALF)
        acc[...] = jnp.dot(adj[512:1024, :], right, preferred_element_type=F32)

    def sums_second(p, state):
        state["core"].wait_recv()
        total = acc[...] + crecv[p].astype(F32)
        acc[...] = total
        ysend[p] = total.astype(BF16)
        state["y"] = Batch(yrecv.at[p, pl.ds(1, NY - 1)], y_peer(1))
        for e in (4, 3, 5, 2, 6, 1, 7):
            run = pl.ds(SLOT[e] * ROWS, ROWS)
            state["y"].start(ysend.at[p, run], yrecv.at[p, e], y_peer(e))

    def sums_last(p, state):
        total = acc[0:ROWS]
        state["y"].wait_recv()
        for e in range(1, NY):
            total = total + yrecv[p, e].astype(F32)
        return total

    def early_t(p):
        for n in range(NX):
            lanes = slice(n * 512, (n + 1) * 512)
            begun_t[:, lanes] = lax.dot_general(
                gath_t[p, 0], adj[512:1024, lanes], (((0,), (0,)), ((), ())),
                preferred_element_type=F32,
            )

    def product_t(p, lo, hi):
        rest = lax.dot_general(
            gath_t[p, 1], adj[0:512, lo:hi], (((0,), (0,)), ((), ())), preferred_element_type=F32
        )
        return (begun_t[:, lo:hi] + rest).T

    def near_first(p, state):
        for one in state["core_t"]:
            one.wait_recv()
        opposite = product_t(p, 1536, 2048)
        near_send[p, 0, 256:512] = opposite[:256].astype(BF16)
        near_send[p, 1, 256:512] = opposite[256:].astype(BF16)
        far = pl.ds(256, 256)
        state["far_e"] = copy(near_send.at[p, 0, far], near_recv.at[p, 0, far], east)
        state["far_w"] = copy(near_send.at[p, 1, far], near_recv.at[p, 1, far], west)

    def near_close(p, state):
        close = pl.ds(0, 256)
        near_send[p, 0, 0:256] = product_t(p, 512, 768).astype(BF16)
        state["near_e"] = copy(near_send.at[p, 0, close], near_recv.at[p, 0, close], east)
        near_send[p, 1, 0:256] = product_t(p, 1280, 1536).astype(BF16)
        state["near_w"] = copy(near_send.at[p, 1, close], near_recv.at[p, 1, close], west)

    def near_second(p):
        keep_near[0] = product_t(p, 1024, 1280)
        keep_near[1] = product_t(p, 768, 1024)

    def next_first(p, state):
        state["far_e"].wait_recv()
        next_send[p, 0] = (keep_near[0] + near_recv[p, 0, 256:512].astype(F32)).astype(BF16)
        state["next_w"] = copy(next_send.at[p, 0], next_recv.at[p, 0], west)
        state["far_w"].wait_recv()
        next_send[p, 1] = (keep_near[1] + near_recv[p, 1, 256:512].astype(F32)).astype(BF16)
        state["next_e"] = copy(next_send.at[p, 1], next_recv.at[p, 1], east)

    def next_own(p, state):
        value = product_t(p, 0, 512)
        state["near_e"].wait_recv()
        state["near_w"].wait_recv()
        keep[0:256] = value[:256] + near_recv[p, 0, 0:256].astype(F32)
        keep[256:512] = value[256:] + near_recv[p, 1, 0:256].astype(F32)

    def next_second(p, state):
        state["z_t"] = Batch(zrecv.at[p, pl.ds(1, NZ - 1)], z_peer(1))
        for part_at, arrival, offsets in ((1, "next_e", (4, 3, 5, 6)), (0, "next_w", (2, 1, 7))):
            state[arrival].wait_recv()
            rows = slice(part_at * 256, (part_at + 1) * 256)
            total = keep[rows] + next_recv[p, part_at].astype(F32)
            zsend[p, rows] = total.astype(BF16)
            for e in offsets:
                run = pl.ds(SLOT[e] * ROWS, ROWS)
                state["z_t"].start(zsend.at[p, run], zrecv.at[p, e], z_peer(e))
        keep[0:ROWS] = total[0:ROWS]

    def sums_last_t(p, state):
        total = keep[0:ROWS]
        state["z_t"].wait_recv()
        for e in range(1, NZ):
            total = total + zrecv[p, e].astype(F32)
        return total

    mask_copies = Batch(masks.at[pl.ds(0, NZ - 1)], z_peer(1))
    for e in range(1, NZ):
        mask_copies.start(masks.at[z], masks.at[z], z_peer(e))
    state = start_pass(0)
    prepare_block()
    mask_copies.wait_recv()
    mask_columns()
    make_block(3, 1)
    relay(0, 0, state)
    make_block(1, 1)
    forward(0, 1, state)
    make_block(2, 1)
    make_block(0, 1)
    forward_t(0, state)
    forward(0, 2, state)
    relay(0, 1, state)
    make_block(3, 0)
    early_t(0)
    make_block(1, 0)
    make_block(2, 0)
    near_first(0, state)
    relay(0, 2, state)
    near_close(0, state)
    near_second(0)
    make_block(0, 0)
    early(0)
    next_first(0, state)
    finish_gather(state)
    sums_first(0, state)
    next_own(0, state)
    product(0)
    next_second(0, state)
    sums_second(0, state)
    sums = jnp.concatenate([sums_last(0, state), sums_last_t(0, state)], axis=1)

    for one in loads[3:]:
        one.wait()
    sums_high = sums.astype(BF16)
    sums_low = (sums - sums_high.astype(F32)).astype(BF16)
    scale = scale_col[...]
    presum = scale * (
        jnp.dot(sums_high, weight[...], preferred_element_type=F32)
        + jnp.dot(sums_low, weight[...], preferred_element_type=F32)
    )
    sigma = jax.nn.sigmoid(presum)
    layer_out[...] = (presum * sigma).astype(BF16)
    deriv = sigma * (1.0 + presum * (1.0 - sigma))
    error = (scale * cot[...].astype(F32) * deriv).astype(BF16)
    gath[1, 0, 0:ROWS] = error[:, :HALF]
    gath_t[1, 0, 0:ROWS] = error[:, HALF:]

    earlier = list(started)

    state = start_pass(1)
    dims = (((0,), (0,)), ((), ()))
    part[...] = lax.dot_general(
        sums_high, error, dims, preferred_element_type=F32
    ) + lax.dot_general(sums_low, error, dims, preferred_element_type=F32)
    theirs = pl.multiple_of((1 - c) * 128, 128)
    mine = pl.multiple_of(c * 128, 128)
    first = copy(part.at[pl.ds(theirs, 128)], a1r, sibling)
    for one in earlier:
        one.wait_send()
    relay(1, 0, state)
    forward(1, 1, state)

    first.wait_recv()
    half[...] = part[pl.ds(mine, 128), :] + a1r[...]
    a2s[...] = half[...].astype(BF16)
    second = Batch(a2r.at[pl.ds(1, NY - 1)], y_peer(1))
    for e in range(1, NY):
        at = pl.multiple_of(((y + e) % NY) * 16, 16)
        second.start(a2s.at[pl.ds(at, 16)], a2r.at[e], y_peer(e))

    forward_t(1, state)
    forward(1, 2, state)
    relay(1, 1, state)
    early_t(1)
    near_first(1, state)
    relay(1, 2, state)
    near_close(1, state)

    piece = half[pl.ds(pl.multiple_of(y * 16, 16), 16), :]
    second.wait_recv()
    for e in range(1, NY):
        piece = piece + a2r[e].astype(F32)
    a3r[z] = piece.astype(BF16)
    third = Batch(a3r.at[pl.ds(0, NZ - 1)], z_peer(1))
    for e in range(1, NZ):
        third.start(a3r.at[z], a3r.at[z], z_peer(e))

    near_second(1)
    early(1)
    next_first(1, state)
    finish_gather(state)
    sums_first(1, state)

    third.wait_recv()
    piece = a3r[0].astype(F32)
    for n in range(1, NZ):
        piece = piece + a3r[n].astype(F32)
    a4r[x] = piece
    fourth = Batch(a4r.at[pl.ds(0, NX - 1)], x_peer(1))
    for e in range(1, NX):
        fourth.start(a4r.at[x], a4r.at[x], x_peer(e))

    next_own(1, state)
    product(1)
    next_second(1, state)

    fourth.wait_recv()
    piece = (a4r[0] + a4r[1]) + (a4r[2] + a4r[3])
    at = pl.multiple_of(c * 128 + y * 16, 16)
    wbuf[pl.ds(at, 16), :] = piece.astype(BF16)
    fifth = Batch(wbuf.at[pl.ds(0, 16 * (NY - 1))], y_peer(1))
    for e in range(1, NY):
        fifth.start(wbuf.at[pl.ds(at, 16)], wbuf.at[pl.ds(at, 16)], y_peer(e))
    sums_second(1, state)
    fifth.wait_recv()
    sixth = copy(wbuf.at[pl.ds(mine, 128)], wbuf.at[pl.ds(mine, 128)], sibling)
    back = jnp.concatenate([sums_last(1, state), sums_last_t(1, state)], axis=1)
    vgrad = (scale * back).astype(BF16)
    grad_feats[...] = lax.dot_general(
        vgrad, weight[...], (((1,), (1,)), ((), ())), preferred_element_type=F32
    ).astype(BF16)
    sixth.wait_recv()
    grad_weight[...] = wbuf[...].astype(F32)
    for one in started[len(earlier):]:
        one.wait_send()


def deliver(*refs):
    sems = refs[-1]
    copies = [pltpu.make_async_copy(refs[n], refs[n + 3], sems.at[n]) for n in range(3)]
    for one in copies:
        one.start()
    for one in copies:
        one.wait()


def local(node_feats, weight, node_scale, tile_mask, cotangent, coef):
    hidden = weight.shape[0]
    hbm = pl.BlockSpec(memory_space=pltpu.HBM)
    vmem = pl.BlockSpec(memory_space=pltpu.VMEM)
    shapes = (((ROWS, hidden), BF16), ((ROWS, hidden), BF16), ((hidden, hidden), F32))
    args = (node_feats, weight, node_scale.reshape(1, ROWS), tile_mask, cotangent)
    made = pl.pallas_call(
        functools.partial(kernel, coef),
        out_shape=tuple(pltpu.VMEM(*shape) for shape in shapes),
        in_specs=[hbm] * 5,
        out_specs=(vmem,) * 3,
        scratch_shapes=[
            pltpu.VMEM((ROWS, hidden), BF16),
            pltpu.VMEM((hidden, hidden), BF16),
            pltpu.VMEM((1, ROWS), BF16),
            pltpu.VMEM(tile_mask.shape, jnp.int32),
            pltpu.VMEM((ROWS, hidden), BF16),
            pltpu.SemaphoreType.DMA((5,)),
            pltpu.VMEM((1024, 2048), BF16),
            pltpu.VMEM((16, 2048), F32),
            pltpu.VMEM((2, NX, NZ * ROWS, HALF), BF16),
            pltpu.VMEM((2, 2, NY * ROWS, HALF), BF16),
            pltpu.VMEM((NZ, 8, HALF), F32),
            pltpu.VMEM((2, 512, HALF), BF16),
            pltpu.VMEM((2, 512, HALF), BF16),
            pltpu.VMEM((512, HALF), F32),
            pltpu.VMEM((2, 512, HALF), BF16),
            pltpu.VMEM((2, NY, ROWS, HALF), BF16),
            pltpu.VMEM((2, 2, 512, HALF), BF16),
            pltpu.VMEM((2, 2, 512, HALF), BF16),
            pltpu.VMEM((512, HALF), F32),
            pltpu.VMEM((2, 256, HALF), F32),
            pltpu.VMEM((2, 2, 256, HALF), BF16),
            pltpu.VMEM((2, 2, 256, HALF), BF16),
            pltpu.VMEM((2, 512, HALF), BF16),
            pltpu.VMEM((2, NZ, ROWS, HALF), BF16),
            pltpu.VMEM((512, HALF), F32),
            pltpu.VMEM((HALF, 2048), F32),
            pltpu.VMEM((8, 16, 512), F32),
            pltpu.VMEM((NX, 2, 8, 512), F32),
            pltpu.VMEM((256, 256), F32),
            pltpu.VMEM((128, 256), F32),
            pltpu.VMEM((128, 256), F32),
            pltpu.VMEM((128, 256), BF16),
            pltpu.VMEM((NY, 16, 256), BF16),
            pltpu.VMEM((NZ, 16, 256), BF16),
            pltpu.VMEM((NX, 16, 256), F32),
            pltpu.VMEM((256, 256), BF16),
            pltpu.VMEM((ROWS, 256), F32),
            pltpu.SemaphoreType.DMA((COPIES,)),
            pltpu.SemaphoreType.DMA((COPIES,)),
        ],
        compiler_params=pltpu.CompilerParams(
            collective_id=0, has_side_effects=True, vmem_limit_bytes=40 * 1024 * 1024
        ),
    )(*(pltpu.with_memory_space_constraint(arg, pltpu.HBM) for arg in args))
    return pl.pallas_call(
        deliver,
        out_shape=tuple(jax.ShapeDtypeStruct(*shape) for shape in shapes),
        in_specs=[vmem] * 3,
        out_specs=(hbm,) * 3,
        scratch_shapes=[pltpu.SemaphoreType.DMA((3,))],
        compiler_params=pltpu.CompilerParams(vmem_limit_bytes=8 * 1024 * 1024),
    )(*(pltpu.with_memory_space_constraint(one, pltpu.VMEM) for one in made))


def solution(mesh):
    in_specs = (
        P(("section", "rep"), None),
        P(),
        P(("section", "rep")),
        P("section", None),
        P(("section", "rep"), None),
    )
    out_specs = (P(("section", "rep"), None), P(("section", "rep"), None), P())
    coef = 4.0 / math.sqrt(128 * 256)
    return jax.shard_map(
        functools.partial(local, coef=coef), mesh=mesh, in_specs=in_specs, out_specs=out_specs,
        check_vma=False,
    )
```

```python
import functools
import math

import jax
import jax.numpy as jnp
from jax import lax
from jax.experimental import pallas as pl
from jax.experimental.pallas import tpu as pltpu
from jax.sharding import PartitionSpec as P


MESH = pl.DeviceIdType.MESH
NZ, NY, NX = 8, 8, 4
ROWS = 64
HALF = 128
MODULUS = 65521
OFFSET = (0, 1, 7, 2, 6, 3, 5, 4)
SLOT = {off: k for k, off in enumerate(OFFSET)}
GROUPS = ((0, 1), (1, 5), (5, 8))
COPIES = 80
BF16 = jnp.bfloat16
F32 = jnp.float32


def fold(v):
    return (v & 0xFFFF) + 15 * (v >> 16)


def reduce_once(v):
    return jnp.where(v >= MODULUS, v - MODULUS, v)


SCALE = 2.0 / MODULUS
WRAP = 1.0 - 0.5 * SCALE


def add_wrapped(u, step):
    total = u + step
    return jnp.where(total >= WRAP, total - 2.0, total)


def kernel(
    coef,
    feats_hbm, weight_hbm, scale_hbm, mask_hbm, cot_hbm,
    layer_out, grad_feats, grad_weight,
    feats, weight, scale_row, mask, cot, load_sems,
    adj, cm, gath, gath_t, masks, csend, crecv, acc, ysend, yrecv,
    near_send, near_recv, keep, keep_near, next_send, next_recv, zsend, zrecv,
    begun, begun_t, starts, steps, part, a1r, half, a2s, a2r, a3r, a4r, wbuf, scale_col,
    send_sems, recv_sems,
):
    sec = lax.axis_index("section")
    x = lax.axis_index("rep")
    c = sec % 2
    y = (sec // 2) % NY
    z = sec // (2 * NY)
    x_one = x + 1 - 2 * (x % 2)
    x_two = 3 - x
    x_opp = (x + 2) % NX

    def device(zz, yy, cc, xx):
        return ((zz * NY + yy) * 2 + cc, xx)

    sibling = device(z, y, 1 - c, x)
    east, west = device(z, y, c, x_one), device(z, y, c, x_two)

    def z_peer(e):
        return device((z + e) % NZ, y, c, x)

    def y_peer(e):
        return device(z, (y + e) % NY, c, x)

    def x_peer(e):
        return device(z, y, c, (x + e) % NX)

    loads = [
        pltpu.make_async_copy(src, dst, load_sems.at[n])
        for n, (src, dst) in enumerate((
            (feats_hbm, feats), (scale_hbm, scale_row), (mask_hbm, mask),
            (weight_hbm, weight), (cot_hbm, cot),
        ))
    ]
    for one in loads:
        one.start()

    barrier = pltpu.get_barrier_semaphore()
    peers = [z_peer(e) for e in range(1, NZ)] + [y_peer(e) for e in range(1, NY)]
    peers += [x_peer(e) for e in range(1, NX)] + [sibling]
    for peer in peers:
        pl.semaphore_signal(barrier, inc=1, device_id=peer, device_id_type=MESH)

    started = []
    numbers = iter(range(COPIES))

    class Batch:
        def __init__(self, view, target):
            number = next(numbers)
            self.send_sem, self.recv_sem = send_sems.at[number], recv_sems.at[number]
            self.whole = self.describe(view, view, target)
            started.append(self.whole)

        def describe(self, src, dst, target):
            return pltpu.make_async_remote_copy(
                src_ref=src, dst_ref=dst, send_sem=self.send_sem, recv_sem=self.recv_sem,
                device_id=target, device_id_type=MESH,
            )

        def start(self, src, dst, target):
            self.describe(src, dst, target).start()

        def wait_recv(self):
            self.whole.wait_recv()

    def copy(src, dst, target):
        one = Batch(dst, target)
        one.start(src, dst, target)
        return one

    col_j = lax.broadcasted_iota(jnp.int32, (16, 512), 1)
    row_i = lax.broadcasted_iota(jnp.int32, (16, 512), 0)
    col_slot = col_j >> 6
    col_off = jnp.where((col_slot & 1) == 1, (col_slot + 1) >> 1, (8 - (col_slot >> 1)) & 7)
    columns_x = (x, x_one, x_two, x_opp)

    def side_core(side):
        return 1 - c if side == 0 else c

    def mask_columns():
        which = lax.broadcasted_iota(jnp.int32, (16, HALF), 0)
        lane = lax.broadcasted_iota(jnp.int32, (16, HALF), 1)
        core_of = jnp.where(which < 8, 1 - c, c)
        tile = ((z * NY + (which & 7)) * 2 + core_of) * 2 + x // 2
        every = masks[...].reshape(64, HALF)
        dims = (((1,), (1,)), ((), ()))
        low = lax.dot_general((tile == lane).astype(F32), every, dims, preferred_element_type=F32)
        high = lax.dot_general(
            (tile == lane + HALF).astype(F32), every, dims, preferred_element_type=F32
        )
        entry = lax.broadcasted_iota(jnp.int32, (64, 512), 0)
        slot = lax.broadcasted_iota(jnp.int32, (64, 512), 1) >> 6
        off = jnp.where((slot & 1) == 1, (slot + 1) >> 1, (8 - (slot >> 1)) & 7)
        same = (entry >> 3) == ((z + off) & 7)
        for n, xx in enumerate(columns_x):
            pick_low = jnp.where(same & ((entry & 7) == xx // 2), 1.0, 0.0).astype(F32)
            pick_high = jnp.where(same & ((entry & 7) == xx // 2 + 2), 1.0, 0.0).astype(F32)
            chosen = jnp.dot(low, pick_low, preferred_element_type=F32) + jnp.dot(
                high, pick_high, preferred_element_type=F32
            )
            cm[:, n * 512:(n + 1) * 512] = jnp.where(chosen > 0.5, coef, 0.0)

    def column_ids(n):
        return ((((z + col_off) & 7) * NY + y) * 2 + c) * 256 + columns_x[n] * ROWS + (col_j & 63)

    def prepare(unit, a, b):
        first = fold(fold(a * b))
        hashed = reduce_once(fold(fold(first * 20011 + (a + b) * 7919)))
        starts[unit] = hashed.astype(F32) * SCALE - 1.0

    def prepare_steps(number, b, stride):
        step = reduce_once(fold(fold(b[0:8] * 20011 + 7919)))
        steps[number, 0] = reduce_once(fold(step * 16)).astype(F32) * SCALE
        steps[number, 1] = reduce_once(fold(step * stride)).astype(F32) * SCALE

    def prepare_block():
        for n in range(NX):
            b = column_ids(n)
            prepare_steps(n, b, 512)
            for side in range(2):
                a = ((z * NY) * 2 + side_core(side)) * 256 + x * ROWS + row_i
                prepare(n * 2 + side, a, b)

    def make_block(n, side):
        lanes = slice(n * 512, (n + 1) * 512)
        step16 = jnp.concatenate([steps[n, 0]] * 2, axis=0)
        leap = jnp.concatenate([steps[n, 1]] * 2, axis=0)

        def run(yy, u0):
            off = (yy - y + NY) % NY
            late = off // 5
            slot = (off + 7) // 8 * ((1 - late) * (2 * off - 1) + late * (16 - 2 * off))
            coefs = cm[pl.ds(side * 8 + yy, 1), lanes]
            u = u0
            for s in range(4):
                at = pl.multiple_of(side * 512 + slot * ROWS + s * 16, 16)
                adj[pl.ds(at, 16), lanes] = (u * coefs).astype(BF16)
                if s < 3:
                    u = add_wrapped(u, step16)
            return add_wrapped(u0, leap)

        lax.fori_loop(0, 8, run, starts[n * 2 + side])

    for one in loads[:3]:
        one.wait()
    row = scale_row[...].astype(F32)
    pick = lax.broadcasted_iota(jnp.int32, (ROWS, ROWS), 0) == lax.broadcasted_iota(
        jnp.int32, (ROWS, ROWS), 1
    )
    column = jnp.sum(jnp.where(pick, jnp.broadcast_to(row, (ROWS, ROWS)), 0.0), axis=1, keepdims=True)
    scale_col[...] = jnp.broadcast_to(column, (ROWS, 256))
    scaled = (scale_col[...] * feats[...].astype(F32)).astype(BF16)
    gath[0, 0, 0:ROWS] = scaled[:, :HALF]
    gath_t[0, 0, 0:ROWS] = scaled[:, HALF:]
    masks[z] = jnp.zeros((8, HALF), F32)
    masks[z, 0:2, :] = mask[:, 0:HALF].astype(F32)
    masks[z, 2:4, :] = mask[:, HALF:].astype(F32)

    pl.semaphore_wait(barrier, len(peers))

    def start_pass(p):
        own = gath.at[p, 0, pl.ds(0, ROWS)]
        own_t = gath_t.at[p, 0, pl.ds(0, ROWS)]
        state = {"z": {}, "one": {}, "two": {}, "opp": [], "y_t": {}, "core_t": []}
        for g, (lo, hi) in enumerate(GROUPS[1:], 1):
            state["z"][g] = Batch(gath.at[p, 0, pl.ds(lo * ROWS, (hi - lo) * ROWS)], z_peer(1))
        state["y_t"] = Batch(gath_t.at[p, 0, pl.ds(ROWS, (NY - 1) * ROWS)], y_peer(1))
        for k in (7, 6, 5, 4, 3, 2, 1):
            e = (NY - OFFSET[k]) % NY
            state["y_t"].start(own_t, gath_t.at[p, 0, pl.ds(k * ROWS, ROWS)], y_peer(e))
        for k in range(1, NZ):
            e = (NZ - OFFSET[k]) % NZ
            g = 1 if k < GROUPS[1][1] else 2
            state["z"][g].start(own, gath.at[p, 0, pl.ds(k * ROWS, ROWS)], z_peer(e))
            if k == 4:
                forward(p, 0, state)
        return state

    def forward_t(p, state):
        state["y_t"].wait_recv()
        state["core_t"].append(copy(gath_t.at[p, 0], gath_t.at[p, 1], sibling))

    def forward(p, g, state):
        lo, hi = GROUPS[g]
        if g:
            state["z"][g].wait_recv()
        run = pl.ds(lo * ROWS, (hi - lo) * ROWS)
        state["one"][g] = copy(gath.at[p, 0, run], gath.at[p, 1, run], east)
        state["two"][g] = copy(gath.at[p, 0, run], gath.at[p, 2, run], west)

    def relay(p, g, state):
        lo, hi = GROUPS[g]
        size = (hi - lo) * ROWS // 2
        run = pl.ds(lo * ROWS, size)
        state["two"][g].wait_recv()
        state["opp"].append(copy(gath.at[p, 2, run], gath.at[p, 3, run], east))
        run = pl.ds(lo * ROWS + size, size)
        state["one"][g].wait_recv()
        state["opp"].append(copy(gath.at[p, 1, run], gath.at[p, 3, run], west))

    def finish_gather(state):
        for one in state["opp"]:
            one.wait_recv()

    def early(p):
        right = gath[p, 0:3].reshape(3 * NZ * ROWS, HALF)
        begun[...] = jnp.dot(adj[0:512, 0:1536], right, preferred_element_type=F32)

    def sums_first(p, state):
        rest = jnp.dot(adj[0:512, 1536:2048], gath[p, 3], preferred_element_type=F32)
        csend[p] = (begun[...] + rest).astype(BF16)
        state["core"] = copy(csend.at[p], crecv.at[p], sibling)

    def product(p):
        right = gath[p].reshape(NX * NZ * ROWS, HALF)
        acc[...] = jnp.dot(adj[512:1024, :], right, preferred_element_type=F32)

    def sums_second(p, state):
        state["core"].wait_recv()
        total = acc[...] + crecv[p].astype(F32)
        acc[...] = total
        ysend[p] = total.astype(BF16)
        state["y"] = Batch(yrecv.at[p, pl.ds(1, NY - 1)], y_peer(1))
        for e in (4, 3, 5, 2, 6, 1, 7):
            run = pl.ds(SLOT[e] * ROWS, ROWS)
            state["y"].start(ysend.at[p, run], yrecv.at[p, e], y_peer(e))

    def sums_last(p, state):
        total = acc[0:ROWS]
        state["y"].wait_recv()
        for e in range(1, NY):
            total = total + yrecv[p, e].astype(F32)
        return total

    def early_t(p):
        for n in range(NX):
            lanes = slice(n * 512, (n + 1) * 512)
            begun_t[:, lanes] = lax.dot_general(
                gath_t[p, 0], adj[512:1024, lanes], (((0,), (0,)), ((), ())),
                preferred_element_type=F32,
            )

    def product_t(p, lo, hi):
        rest = lax.dot_general(
            gath_t[p, 1], adj[0:512, lo:hi], (((0,), (0,)), ((), ())), preferred_element_type=F32
        )
        return (begun_t[:, lo:hi] + rest).T

    def near_first(p, state):
        for one in state["core_t"]:
            one.wait_recv()
        opposite = product_t(p, 1536, 2048)
        near_send[p, 0, 256:512] = opposite[:256].astype(BF16)
        near_send[p, 1, 256:512] = opposite[256:].astype(BF16)
        far, close = pl.ds(256, 256), pl.ds(0, 256)
        state["far_e"] = copy(near_send.at[p, 0, far], near_recv.at[p, 0, far], east)
        state["far_w"] = copy(near_send.at[p, 1, far], near_recv.at[p, 1, far], west)
        near_send[p, 0, 0:256] = product_t(p, 512, 768).astype(BF16)
        state["near_e"] = copy(near_send.at[p, 0, close], near_recv.at[p, 0, close], east)
        near_send[p, 1, 0:256] = product_t(p, 1280, 1536).astype(BF16)
        state["near_w"] = copy(near_send.at[p, 1, close], near_recv.at[p, 1, close], west)

    def near_second(p):
        keep_near[0] = product_t(p, 1024, 1280)
        keep_near[1] = product_t(p, 768, 1024)

    def next_first(p, state):
        state["far_e"].wait_recv()
        next_send[p, 0] = (keep_near[0] + near_recv[p, 0, 256:512].astype(F32)).astype(BF16)
        state["next_w"] = copy(next_send.at[p, 0], next_recv.at[p, 0], west)
        state["far_w"].wait_recv()
        next_send[p, 1] = (keep_near[1] + near_recv[p, 1, 256:512].astype(F32)).astype(BF16)
        state["next_e"] = copy(next_send.at[p, 1], next_recv.at[p, 1], east)

    def next_own(p, state):
        value = product_t(p, 0, 512)
        state["near_e"].wait_recv()
        state["near_w"].wait_recv()
        keep[0:256] = value[:256] + near_recv[p, 0, 0:256].astype(F32)
        keep[256:512] = value[256:] + near_recv[p, 1, 0:256].astype(F32)

    def next_second(p, state):
        state["z_t"] = Batch(zrecv.at[p, pl.ds(1, NZ - 1)], z_peer(1))
        for part_at, arrival, offsets in ((1, "next_e", (4, 3, 5, 6)), (0, "next_w", (2, 1, 7))):
            state[arrival].wait_recv()
            rows = slice(part_at * 256, (part_at + 1) * 256)
            total = keep[rows] + next_recv[p, part_at].astype(F32)
            zsend[p, rows] = total.astype(BF16)
            for e in offsets:
                run = pl.ds(SLOT[e] * ROWS, ROWS)
                state["z_t"].start(zsend.at[p, run], zrecv.at[p, e], z_peer(e))
        keep[0:ROWS] = total[0:ROWS]

    def sums_last_t(p, state):
        total = keep[0:ROWS]
        state["z_t"].wait_recv()
        for e in range(1, NZ):
            total = total + zrecv[p, e].astype(F32)
        return total

    mask_copies = Batch(masks.at[pl.ds(0, NZ - 1)], z_peer(1))
    for e in range(1, NZ):
        mask_copies.start(masks.at[z], masks.at[z], z_peer(e))
    state = start_pass(0)
    prepare_block()
    mask_copies.wait_recv()
    mask_columns()
    make_block(3, 1)
    relay(0, 0, state)
    make_block(1, 1)
    forward(0, 1, state)
    make_block(2, 1)
    make_block(0, 1)
    forward_t(0, state)
    forward(0, 2, state)
    relay(0, 1, state)
    make_block(3, 0)
    early_t(0)
    make_block(1, 0)
    make_block(2, 0)
    near_first(0, state)
    relay(0, 2, state)
    near_second(0)
    make_block(0, 0)
    early(0)
    next_first(0, state)
    finish_gather(state)
    sums_first(0, state)
    next_own(0, state)
    product(0)
    next_second(0, state)
    sums_second(0, state)
    sums = jnp.concatenate([sums_last(0, state), sums_last_t(0, state)], axis=1)

    for one in loads[3:]:
        one.wait()
    sums_high = sums.astype(BF16)
    sums_low = (sums - sums_high.astype(F32)).astype(BF16)
    scale = scale_col[...]
    presum = scale * (
        jnp.dot(sums_high, weight[...], preferred_element_type=F32)
        + jnp.dot(sums_low, weight[...], preferred_element_type=F32)
    )
    sigma = jax.nn.sigmoid(presum)
    layer_out[...] = (presum * sigma).astype(BF16)
    deriv = sigma * (1.0 + presum * (1.0 - sigma))
    error = (scale * cot[...].astype(F32) * deriv).astype(BF16)
    gath[1, 0, 0:ROWS] = error[:, :HALF]
    gath_t[1, 0, 0:ROWS] = error[:, HALF:]

    earlier = list(started)

    state = start_pass(1)
    dims = (((0,), (0,)), ((), ()))
    part[...] = lax.dot_general(
        sums_high, error, dims, preferred_element_type=F32
    ) + lax.dot_general(sums_low, error, dims, preferred_element_type=F32)
    theirs = pl.multiple_of((1 - c) * 128, 128)
    mine = pl.multiple_of(c * 128, 128)
    first = copy(part.at[pl.ds(theirs, 128)], a1r, sibling)
    for one in earlier:
        one.wait_send()
    relay(1, 0, state)
    forward(1, 1, state)

    first.wait_recv()
    half[...] = part[pl.ds(mine, 128), :] + a1r[...]
    a2s[...] = half[...].astype(BF16)
    second = Batch(a2r.at[pl.ds(1, NY - 1)], y_peer(1))
    for e in range(1, NY):
        at = pl.multiple_of(((y + e) % NY) * 16, 16)
        second.start(a2s.at[pl.ds(at, 16)], a2r.at[e], y_peer(e))

    forward_t(1, state)
    forward(1, 2, state)
    relay(1, 1, state)
    early_t(1)
    near_first(1, state)

    piece = half[pl.ds(pl.multiple_of(y * 16, 16), 16), :]
    second.wait_recv()
    for e in range(1, NY):
        piece = piece + a2r[e].astype(F32)
    a3r[z] = piece.astype(BF16)
    third = Batch(a3r.at[pl.ds(0, NZ - 1)], z_peer(1))
    for e in range(1, NZ):
        third.start(a3r.at[z], a3r.at[z], z_peer(e))

    relay(1, 2, state)
    near_second(1)
    early(1)
    next_first(1, state)
    finish_gather(state)
    sums_first(1, state)

    third.wait_recv()
    piece = a3r[0].astype(F32)
    for n in range(1, NZ):
        piece = piece + a3r[n].astype(F32)
    a4r[x] = piece
    fourth = Batch(a4r.at[pl.ds(0, NX - 1)], x_peer(1))
    for e in range(1, NX):
        fourth.start(a4r.at[x], a4r.at[x], x_peer(e))

    next_own(1, state)
    product(1)
    next_second(1, state)

    fourth.wait_recv()
    piece = (a4r[0] + a4r[1]) + (a4r[2] + a4r[3])
    at = pl.multiple_of(c * 128 + y * 16, 16)
    wbuf[pl.ds(at, 16), :] = piece.astype(BF16)
    fifth = Batch(wbuf.at[pl.ds(0, 16 * (NY - 1))], y_peer(1))
    for e in range(1, NY):
        fifth.start(wbuf.at[pl.ds(at, 16)], wbuf.at[pl.ds(at, 16)], y_peer(e))
    sums_second(1, state)
    fifth.wait_recv()
    sixth = copy(wbuf.at[pl.ds(mine, 128)], wbuf.at[pl.ds(mine, 128)], sibling)
    back = jnp.concatenate([sums_last(1, state), sums_last_t(1, state)], axis=1)
    vgrad = (scale * back).astype(BF16)
    grad_feats[...] = lax.dot_general(
        vgrad, weight[...], (((1,), (1,)), ((), ())), preferred_element_type=F32
    ).astype(BF16)
    sixth.wait_recv()
    grad_weight[...] = wbuf[...].astype(F32)
    for one in started[len(earlier):]:
        one.wait_send()


def deliver(*refs):
    sems = refs[-1]
    copies = [pltpu.make_async_copy(refs[n], refs[n + 3], sems.at[n]) for n in range(3)]
    for one in copies:
        one.start()
    for one in copies:
        one.wait()


def local(node_feats, weight, node_scale, tile_mask, cotangent, coef):
    hidden = weight.shape[0]
    hbm = pl.BlockSpec(memory_space=pltpu.HBM)
    vmem = pl.BlockSpec(memory_space=pltpu.VMEM)
    shapes = (((ROWS, hidden), BF16), ((ROWS, hidden), BF16), ((hidden, hidden), F32))
    args = (node_feats, weight, node_scale.reshape(1, ROWS), tile_mask, cotangent)
    made = pl.pallas_call(
        functools.partial(kernel, coef),
        out_shape=tuple(pltpu.VMEM(*shape) for shape in shapes),
        in_specs=[hbm] * 5,
        out_specs=(vmem,) * 3,
        scratch_shapes=[
            pltpu.VMEM((ROWS, hidden), BF16),
            pltpu.VMEM((hidden, hidden), BF16),
            pltpu.VMEM((1, ROWS), BF16),
            pltpu.VMEM(tile_mask.shape, jnp.int32),
            pltpu.VMEM((ROWS, hidden), BF16),
            pltpu.SemaphoreType.DMA((5,)),
            pltpu.VMEM((1024, 2048), BF16),
            pltpu.VMEM((16, 2048), F32),
            pltpu.VMEM((2, NX, NZ * ROWS, HALF), BF16),
            pltpu.VMEM((2, 2, NY * ROWS, HALF), BF16),
            pltpu.VMEM((NZ, 8, HALF), F32),
            pltpu.VMEM((2, 512, HALF), BF16),
            pltpu.VMEM((2, 512, HALF), BF16),
            pltpu.VMEM((512, HALF), F32),
            pltpu.VMEM((2, 512, HALF), BF16),
            pltpu.VMEM((2, NY, ROWS, HALF), BF16),
            pltpu.VMEM((2, 2, 512, HALF), BF16),
            pltpu.VMEM((2, 2, 512, HALF), BF16),
            pltpu.VMEM((512, HALF), F32),
            pltpu.VMEM((2, 256, HALF), F32),
            pltpu.VMEM((2, 2, 256, HALF), BF16),
            pltpu.VMEM((2, 2, 256, HALF), BF16),
            pltpu.VMEM((2, 512, HALF), BF16),
            pltpu.VMEM((2, NZ, ROWS, HALF), BF16),
            pltpu.VMEM((512, HALF), F32),
            pltpu.VMEM((HALF, 2048), F32),
            pltpu.VMEM((8, 16, 512), F32),
            pltpu.VMEM((NX, 2, 8, 512), F32),
            pltpu.VMEM((256, 256), F32),
            pltpu.VMEM((128, 256), F32),
            pltpu.VMEM((128, 256), F32),
            pltpu.VMEM((128, 256), BF16),
            pltpu.VMEM((NY, 16, 256), BF16),
            pltpu.VMEM((NZ, 16, 256), BF16),
            pltpu.VMEM((NX, 16, 256), F32),
            pltpu.VMEM((256, 256), BF16),
            pltpu.VMEM((ROWS, 256), F32),
            pltpu.SemaphoreType.DMA((COPIES,)),
            pltpu.SemaphoreType.DMA((COPIES,)),
        ],
        compiler_params=pltpu.CompilerParams(
            collective_id=0, has_side_effects=True, vmem_limit_bytes=40 * 1024 * 1024
        ),
    )(*(pltpu.with_memory_space_constraint(arg, pltpu.HBM) for arg in args))
    return pl.pallas_call(
        deliver,
        out_shape=tuple(jax.ShapeDtypeStruct(*shape) for shape in shapes),
        in_specs=[vmem] * 3,
        out_specs=(hbm,) * 3,
        scratch_shapes=[pltpu.SemaphoreType.DMA((3,))],
        compiler_params=pltpu.CompilerParams(vmem_limit_bytes=8 * 1024 * 1024),
    )(*(pltpu.with_memory_space_constraint(one, pltpu.VMEM) for one in made))


def solution(mesh):
    in_specs = (
        P(("section", "rep"), None),
        P(),
        P(("section", "rep")),
        P("section", None),
        P(("section", "rep"), None),
    )
    out_specs = (P(("section", "rep"), None), P(("section", "rep"), None), P())
    coef = 4.0 / math.sqrt(128 * 256)
    return jax.shard_map(
        functools.partial(local, coef=coef), mesh=mesh, in_specs=in_specs, out_specs=out_specs,
        check_vma=False,
    )
```

```python
import functools
import math

import jax
import jax.numpy as jnp
from jax import lax
from jax.experimental import pallas as pl
from jax.experimental.pallas import tpu as pltpu
from jax.sharding import PartitionSpec as P


MESH = pl.DeviceIdType.MESH
NZ, NY, NX = 8, 8, 4
ROWS = 64
HALF = 128
MODULUS = 65521
OFFSET = (0, 1, 7, 2, 6, 3, 5, 4)
SLOT = {off: k for k, off in enumerate(OFFSET)}
GROUPS = ((0, 1), (1, 5), (5, 8))
COPIES = 80
BF16 = jnp.bfloat16
F32 = jnp.float32


def fold(v):
    return (v & 0xFFFF) + 15 * (v >> 16)


def reduce_once(v):
    return jnp.where(v >= MODULUS, v - MODULUS, v)


SCALE = 2.0 / MODULUS
WRAP = 1.0 - 0.5 * SCALE


def add_wrapped(u, step):
    total = u + step
    return jnp.where(total >= WRAP, total - 2.0, total)


def kernel(
    coef,
    feats_hbm, weight_hbm, scale_hbm, mask_hbm, cot_hbm,
    layer_out, grad_feats, grad_weight,
    feats, weight, scale_row, mask, cot, load_sems,
    adj, cm, gath, gath_t, masks, csend, crecv, acc, ysend, yrecv,
    near_send, near_recv, keep, keep_near, next_send, next_recv, zsend, zrecv,
    begun, begun_t, starts, steps, part, a1r, half, a2s, a2r, a3r, a4r, wbuf, scale_col,
    send_sems, recv_sems,
):
    sec = lax.axis_index("section")
    x = lax.axis_index("rep")
    c = sec % 2
    y = (sec // 2) % NY
    z = sec // (2 * NY)
    x_one = x + 1 - 2 * (x % 2)
    x_two = 3 - x
    x_opp = (x + 2) % NX

    def device(zz, yy, cc, xx):
        return ((zz * NY + yy) * 2 + cc, xx)

    sibling = device(z, y, 1 - c, x)
    east, west = device(z, y, c, x_one), device(z, y, c, x_two)

    def z_peer(e):
        return device((z + e) % NZ, y, c, x)

    def y_peer(e):
        return device(z, (y + e) % NY, c, x)

    def x_peer(e):
        return device(z, y, c, (x + e) % NX)

    loads = [
        pltpu.make_async_copy(src, dst, load_sems.at[n])
        for n, (src, dst) in enumerate((
            (feats_hbm, feats), (scale_hbm, scale_row), (mask_hbm, mask),
            (weight_hbm, weight), (cot_hbm, cot),
        ))
    ]
    for one in loads:
        one.start()

    barrier = pltpu.get_barrier_semaphore()
    peers = [z_peer(e) for e in range(1, NZ)] + [y_peer(e) for e in range(1, NY)]
    peers += [x_peer(e) for e in range(1, NX)] + [sibling]
    for peer in peers:
        pl.semaphore_signal(barrier, inc=1, device_id=peer, device_id_type=MESH)

    started = []
    numbers = iter(range(COPIES))

    class Batch:
        def __init__(self, view, target):
            number = next(numbers)
            self.send_sem, self.recv_sem = send_sems.at[number], recv_sems.at[number]
            self.whole = self.describe(view, view, target)
            started.append(self.whole)

        def describe(self, src, dst, target):
            return pltpu.make_async_remote_copy(
                src_ref=src, dst_ref=dst, send_sem=self.send_sem, recv_sem=self.recv_sem,
                device_id=target, device_id_type=MESH,
            )

        def start(self, src, dst, target):
            self.describe(src, dst, target).start()

        def wait_recv(self):
            self.whole.wait_recv()

    def copy(src, dst, target):
        one = Batch(dst, target)
        one.start(src, dst, target)
        return one

    col_j = lax.broadcasted_iota(jnp.int32, (16, 512), 1)
    row_i = lax.broadcasted_iota(jnp.int32, (16, 512), 0)
    col_slot = col_j >> 6
    col_off = jnp.where((col_slot & 1) == 1, (col_slot + 1) >> 1, (8 - (col_slot >> 1)) & 7)
    columns_x = (x, x_one, x_two, x_opp)

    def side_core(side):
        return 1 - c if side == 0 else c

    def mask_columns():
        which = lax.broadcasted_iota(jnp.int32, (16, HALF), 0)
        lane = lax.broadcasted_iota(jnp.int32, (16, HALF), 1)
        core_of = jnp.where(which < 8, 1 - c, c)
        tile = ((z * NY + (which & 7)) * 2 + core_of) * 2 + x // 2
        every = masks[...].reshape(64, HALF)
        dims = (((1,), (1,)), ((), ()))
        low = lax.dot_general((tile == lane).astype(F32), every, dims, preferred_element_type=F32)
        high = lax.dot_general(
            (tile == lane + HALF).astype(F32), every, dims, preferred_element_type=F32
        )
        entry = lax.broadcasted_iota(jnp.int32, (64, 512), 0)
        slot = lax.broadcasted_iota(jnp.int32, (64, 512), 1) >> 6
        off = jnp.where((slot & 1) == 1, (slot + 1) >> 1, (8 - (slot >> 1)) & 7)
        same = (entry >> 3) == ((z + off) & 7)
        for n, xx in enumerate(columns_x):
            pick_low = jnp.where(same & ((entry & 7) == xx // 2), 1.0, 0.0).astype(F32)
            pick_high = jnp.where(same & ((entry & 7) == xx // 2 + 2), 1.0, 0.0).astype(F32)
            chosen = jnp.dot(low, pick_low, preferred_element_type=F32) + jnp.dot(
                high, pick_high, preferred_element_type=F32
            )
            cm[:, n * 512:(n + 1) * 512] = jnp.where(chosen > 0.5, coef, 0.0)

    def column_ids(n):
        return ((((z + col_off) & 7) * NY + y) * 2 + c) * 256 + columns_x[n] * ROWS + (col_j & 63)

    def prepare(unit, a, b):
        first = fold(fold(a * b))
        hashed = reduce_once(fold(fold(first * 20011 + (a + b) * 7919)))
        starts[unit] = hashed.astype(F32) * SCALE - 1.0

    def prepare_steps(number, b, stride):
        step = reduce_once(fold(fold(b[0:8] * 20011 + 7919)))
        steps[number, 0] = reduce_once(fold(step * 16)).astype(F32) * SCALE
        steps[number, 1] = reduce_once(fold(step * stride)).astype(F32) * SCALE

    def prepare_block():
        for n in range(NX):
            b = column_ids(n)
            prepare_steps(n, b, 512)
            for side in range(2):
                a = ((z * NY) * 2 + side_core(side)) * 256 + x * ROWS + row_i
                prepare(n * 2 + side, a, b)

    def make_block(n, side):
        lanes = slice(n * 512, (n + 1) * 512)
        step16 = jnp.concatenate([steps[n, 0]] * 2, axis=0)
        leap = jnp.concatenate([steps[n, 1]] * 2, axis=0)

        def run(yy, u0):
            off = (yy - y + NY) % NY
            late = off // 5
            slot = (off + 7) // 8 * ((1 - late) * (2 * off - 1) + late * (16 - 2 * off))
            coefs = cm[pl.ds(side * 8 + yy, 1), lanes]
            u = u0
            for s in range(4):
                at = pl.multiple_of(side * 512 + slot * ROWS + s * 16, 16)
                adj[pl.ds(at, 16), lanes] = (u * coefs).astype(BF16)
                if s < 3:
                    u = add_wrapped(u, step16)
            return add_wrapped(u0, leap)

        lax.fori_loop(0, 8, run, starts[n * 2 + side])

    for one in loads[:3]:
        one.wait()
    row = scale_row[...].astype(F32)
    pick = lax.broadcasted_iota(jnp.int32, (ROWS, ROWS), 0) == lax.broadcasted_iota(
        jnp.int32, (ROWS, ROWS), 1
    )
    column = jnp.sum(jnp.where(pick, jnp.broadcast_to(row, (ROWS, ROWS)), 0.0), axis=1, keepdims=True)
    scale_col[...] = jnp.broadcast_to(column, (ROWS, 256))
    scaled = (scale_col[...] * feats[...].astype(F32)).astype(BF16)
    gath[0, 0, 0:ROWS] = scaled[:, :HALF]
    gath_t[0, 0, 0:ROWS] = scaled[:, HALF:]
    masks[z] = jnp.zeros((8, HALF), F32)
    masks[z, 0:2, :] = mask[:, 0:HALF].astype(F32)
    masks[z, 2:4, :] = mask[:, HALF:].astype(F32)

    pl.semaphore_wait(barrier, len(peers))

    def start_pass(p, between):
        own = gath.at[p, 0, pl.ds(0, ROWS)]
        own_t = gath_t.at[p, 0, pl.ds(0, ROWS)]
        state = {"z": {}, "one": {}, "two": {}, "opp": [], "y_t": {}, "core_t": []}
        for g, (lo, hi) in enumerate(GROUPS[1:], 1):
            state["z"][g] = Batch(gath.at[p, 0, pl.ds(lo * ROWS, (hi - lo) * ROWS)], z_peer(1))
        state["y_t"] = Batch(gath_t.at[p, 0, pl.ds(ROWS, (NY - 1) * ROWS)], y_peer(1))
        for k in (7, 6, 5, 4, 3, 2, 1):
            e = (NY - OFFSET[k]) % NY
            state["y_t"].start(own_t, gath_t.at[p, 0, pl.ds(k * ROWS, ROWS)], y_peer(e))
        between()
        for k in range(1, NZ):
            e = (NZ - OFFSET[k]) % NZ
            g = 1 if k < GROUPS[1][1] else 2
            state["z"][g].start(own, gath.at[p, 0, pl.ds(k * ROWS, ROWS)], z_peer(e))
            if k == 4:
                forward(p, 0, state)
        return state

    def forward_t(p, state):
        state["y_t"].wait_recv()
        state["core_t"].append(copy(gath_t.at[p, 0], gath_t.at[p, 1], sibling))

    def forward(p, g, state):
        lo, hi = GROUPS[g]
        if g:
            state["z"][g].wait_recv()
        run = pl.ds(lo * ROWS, (hi - lo) * ROWS)
        state["one"][g] = copy(gath.at[p, 0, run], gath.at[p, 1, run], east)
        state["two"][g] = copy(gath.at[p, 0, run], gath.at[p, 2, run], west)

    def relay(p, g, state):
        lo, hi = GROUPS[g]
        size = (hi - lo) * ROWS // 2
        run = pl.ds(lo * ROWS, size)
        state["two"][g].wait_recv()
        state["opp"].append(copy(gath.at[p, 2, run], gath.at[p, 3, run], east))
        run = pl.ds(lo * ROWS + size, size)
        state["one"][g].wait_recv()
        state["opp"].append(copy(gath.at[p, 1, run], gath.at[p, 3, run], west))

    def finish_gather(state):
        for one in state["opp"]:
            one.wait_recv()

    def early(p):
        right = gath[p, 0:3].reshape(3 * NZ * ROWS, HALF)
        begun[...] = jnp.dot(adj[0:512, 0:1536], right, preferred_element_type=F32)

    def sums_first(p, state):
        rest = jnp.dot(adj[0:512, 1536:2048], gath[p, 3], preferred_element_type=F32)
        csend[p] = (begun[...] + rest).astype(BF16)
        state["core"] = copy(csend.at[p], crecv.at[p], sibling)

    def product(p):
        right = gath[p].reshape(NX * NZ * ROWS, HALF)
        acc[...] = jnp.dot(adj[512:1024, :], right, preferred_element_type=F32)

    def sums_second(p, state):
        state["core"].wait_recv()
        total = acc[...] + crecv[p].astype(F32)
        acc[...] = total
        ysend[p] = total.astype(BF16)
        state["y"] = Batch(yrecv.at[p, pl.ds(1, NY - 1)], y_peer(1))
        for e in (4, 3, 5, 2, 6, 1, 7):
            run = pl.ds(SLOT[e] * ROWS, ROWS)
            state["y"].start(ysend.at[p, run], yrecv.at[p, e], y_peer(e))

    def sums_last(p, state):
        total = acc[0:ROWS]
        state["y"].wait_recv()
        for e in range(1, NY):
            total = total + yrecv[p, e].astype(F32)
        return total

    def early_t(p):
        for n in range(NX):
            lanes = slice(n * 512, (n + 1) * 512)
            begun_t[:, lanes] = lax.dot_general(
                gath_t[p, 0], adj[512:1024, lanes], (((0,), (0,)), ((), ())),
                preferred_element_type=F32,
            )

    def product_t(p, lo, hi):
        rest = lax.dot_general(
            gath_t[p, 1], adj[0:512, lo:hi], (((0,), (0,)), ((), ())), preferred_element_type=F32
        )
        return (begun_t[:, lo:hi] + rest).T

    def near_first(p, state):
        for one in state["core_t"]:
            one.wait_recv()
        opposite = product_t(p, 1536, 2048)
        near_send[p, 0, 256:512] = opposite[:256].astype(BF16)
        near_send[p, 1, 256:512] = opposite[256:].astype(BF16)
        far, close = pl.ds(256, 256), pl.ds(0, 256)
        state["far_e"] = copy(near_send.at[p, 0, far], near_recv.at[p, 0, far], east)
        state["far_w"] = copy(near_send.at[p, 1, far], near_recv.at[p, 1, far], west)
        near_send[p, 0, 0:256] = product_t(p, 512, 768).astype(BF16)
        state["near_e"] = copy(near_send.at[p, 0, close], near_recv.at[p, 0, close], east)
        near_send[p, 1, 0:256] = product_t(p, 1280, 1536).astype(BF16)
        state["near_w"] = copy(near_send.at[p, 1, close], near_recv.at[p, 1, close], west)

    def near_second(p):
        keep_near[0] = product_t(p, 1024, 1280)
        keep_near[1] = product_t(p, 768, 1024)

    def next_first(p, state):
        state["far_e"].wait_recv()
        next_send[p, 0] = (keep_near[0] + near_recv[p, 0, 256:512].astype(F32)).astype(BF16)
        state["next_w"] = copy(next_send.at[p, 0], next_recv.at[p, 0], west)
        state["far_w"].wait_recv()
        next_send[p, 1] = (keep_near[1] + near_recv[p, 1, 256:512].astype(F32)).astype(BF16)
        state["next_e"] = copy(next_send.at[p, 1], next_recv.at[p, 1], east)

    def next_own(p, state):
        value = product_t(p, 0, 512)
        state["near_e"].wait_recv()
        state["near_w"].wait_recv()
        keep[0:256] = value[:256] + near_recv[p, 0, 0:256].astype(F32)
        keep[256:512] = value[256:] + near_recv[p, 1, 0:256].astype(F32)

    def next_second(p, state):
        state["z_t"] = Batch(zrecv.at[p, pl.ds(1, NZ - 1)], z_peer(1))
        for part_at, arrival, offsets in ((1, "next_e", (4, 3, 5, 6)), (0, "next_w", (2, 1, 7))):
            state[arrival].wait_recv()
            rows = slice(part_at * 256, (part_at + 1) * 256)
            total = keep[rows] + next_recv[p, part_at].astype(F32)
            zsend[p, rows] = total.astype(BF16)
            for e in offsets:
                run = pl.ds(SLOT[e] * ROWS, ROWS)
                state["z_t"].start(zsend.at[p, run], zrecv.at[p, e], z_peer(e))
        keep[0:ROWS] = total[0:ROWS]

    def sums_last_t(p, state):
        total = keep[0:ROWS]
        state["z_t"].wait_recv()
        for e in range(1, NZ):
            total = total + zrecv[p, e].astype(F32)
        return total

    mask_copies = Batch(masks.at[pl.ds(0, NZ - 1)], z_peer(1))

    def send_mask():
        for e in range(1, NZ):
            mask_copies.start(masks.at[z], masks.at[z], z_peer(e))

    state = start_pass(0, send_mask)
    prepare_block()
    mask_copies.wait_recv()
    mask_columns()
    make_block(3, 1)
    relay(0, 0, state)
    make_block(1, 1)
    forward(0, 1, state)
    make_block(2, 1)
    make_block(0, 1)
    forward_t(0, state)
    forward(0, 2, state)
    relay(0, 1, state)
    make_block(3, 0)
    early_t(0)
    make_block(1, 0)
    make_block(2, 0)
    near_first(0, state)
    relay(0, 2, state)
    near_second(0)
    make_block(0, 0)
    early(0)
    next_first(0, state)
    finish_gather(state)
    sums_first(0, state)
    next_own(0, state)
    product(0)
    next_second(0, state)
    sums_second(0, state)
    sums = jnp.concatenate([sums_last(0, state), sums_last_t(0, state)], axis=1)

    for one in loads[3:]:
        one.wait()
    sums_high = sums.astype(BF16)
    sums_low = (sums - sums_high.astype(F32)).astype(BF16)
    scale = scale_col[...]

    def error_half(f):
        lanes = slice(f * HALF, (f + 1) * HALF)
        presum = scale[:, lanes] * (
            jnp.dot(sums_high, weight[:, lanes], preferred_element_type=F32)
            + jnp.dot(sums_low, weight[:, lanes], preferred_element_type=F32)
        )
        sigma = jax.nn.sigmoid(presum)
        layer_out[:, lanes] = (presum * sigma).astype(BF16)
        deriv = sigma * (1.0 + presum * (1.0 - sigma))
        return (scale[:, lanes] * cot[:, lanes].astype(F32) * deriv).astype(BF16)

    gath_t[1, 0, 0:ROWS] = error_half(1)

    def first_half():
        gath[1, 0, 0:ROWS] = error_half(0)

    earlier = list(started)

    state = start_pass(1, first_half)
    error = jnp.concatenate([gath[1, 0, 0:ROWS], gath_t[1, 0, 0:ROWS]], axis=1)
    dims = (((0,), (0,)), ((), ()))
    part[...] = lax.dot_general(
        sums_high, error, dims, preferred_element_type=F32
    ) + lax.dot_general(sums_low, error, dims, preferred_element_type=F32)
    theirs = pl.multiple_of((1 - c) * 128, 128)
    mine = pl.multiple_of(c * 128, 128)
    first = copy(part.at[pl.ds(theirs, 128)], a1r, sibling)
    for one in earlier:
        one.wait_send()
    relay(1, 0, state)
    forward(1, 1, state)

    first.wait_recv()
    half[...] = part[pl.ds(mine, 128), :] + a1r[...]
    a2s[...] = half[...].astype(BF16)
    second = Batch(a2r.at[pl.ds(1, NY - 1)], y_peer(1))
    for e in range(1, NY):
        at = pl.multiple_of(((y + e) % NY) * 16, 16)
        second.start(a2s.at[pl.ds(at, 16)], a2r.at[e], y_peer(e))

    forward_t(1, state)
    forward(1, 2, state)
    relay(1, 1, state)
    early_t(1)
    near_first(1, state)

    piece = half[pl.ds(pl.multiple_of(y * 16, 16), 16), :]
    second.wait_recv()
    for e in range(1, NY):
        piece = piece + a2r[e].astype(F32)
    a3r[z] = piece.astype(BF16)
    third = Batch(a3r.at[pl.ds(0, NZ - 1)], z_peer(1))
    for e in range(1, NZ):
        third.start(a3r.at[z], a3r.at[z], z_peer(e))

    relay(1, 2, state)
    near_second(1)
    early(1)
    next_first(1, state)
    finish_gather(state)
    sums_first(1, state)

    third.wait_recv()
    piece = a3r[0].astype(F32)
    for n in range(1, NZ):
        piece = piece + a3r[n].astype(F32)
    a4r[x] = piece
    fourth = Batch(a4r.at[pl.ds(0, NX - 1)], x_peer(1))
    for e in range(1, NX):
        fourth.start(a4r.at[x], a4r.at[x], x_peer(e))

    next_own(1, state)
    product(1)
    next_second(1, state)

    fourth.wait_recv()
    piece = (a4r[0] + a4r[1]) + (a4r[2] + a4r[3])
    at = pl.multiple_of(c * 128 + y * 16, 16)
    wbuf[pl.ds(at, 16), :] = piece.astype(BF16)
    fifth = Batch(wbuf.at[pl.ds(0, 16 * (NY - 1))], y_peer(1))
    for e in range(1, NY):
        fifth.start(wbuf.at[pl.ds(at, 16)], wbuf.at[pl.ds(at, 16)], y_peer(e))
    sums_second(1, state)
    fifth.wait_recv()
    sixth = copy(wbuf.at[pl.ds(mine, 128)], wbuf.at[pl.ds(mine, 128)], sibling)
    back = jnp.concatenate([sums_last(1, state), sums_last_t(1, state)], axis=1)
    vgrad = (scale * back).astype(BF16)
    grad_feats[...] = lax.dot_general(
        vgrad, weight[...], (((1,), (1,)), ((), ())), preferred_element_type=F32
    ).astype(BF16)
    sixth.wait_recv()
    grad_weight[...] = wbuf[...].astype(F32)
    for one in started[len(earlier):]:
        one.wait_send()


def deliver(*refs):
    sems = refs[-1]
    copies = [pltpu.make_async_copy(refs[n], refs[n + 3], sems.at[n]) for n in range(3)]
    for one in copies:
        one.start()
    for one in copies:
        one.wait()


def local(node_feats, weight, node_scale, tile_mask, cotangent, coef):
    hidden = weight.shape[0]
    hbm = pl.BlockSpec(memory_space=pltpu.HBM)
    vmem = pl.BlockSpec(memory_space=pltpu.VMEM)
    shapes = (((ROWS, hidden), BF16), ((ROWS, hidden), BF16), ((hidden, hidden), F32))
    args = (node_feats, weight, node_scale.reshape(1, ROWS), tile_mask, cotangent)
    made = pl.pallas_call(
        functools.partial(kernel, coef),
        out_shape=tuple(pltpu.VMEM(*shape) for shape in shapes),
        in_specs=[hbm] * 5,
        out_specs=(vmem,) * 3,
        scratch_shapes=[
            pltpu.VMEM((ROWS, hidden), BF16),
            pltpu.VMEM((hidden, hidden), BF16),
            pltpu.VMEM((1, ROWS), BF16),
            pltpu.VMEM(tile_mask.shape, jnp.int32),
            pltpu.VMEM((ROWS, hidden), BF16),
            pltpu.SemaphoreType.DMA((5,)),
            pltpu.VMEM((1024, 2048), BF16),
            pltpu.VMEM((16, 2048), F32),
            pltpu.VMEM((2, NX, NZ * ROWS, HALF), BF16),
            pltpu.VMEM((2, 2, NY * ROWS, HALF), BF16),
            pltpu.VMEM((NZ, 8, HALF), F32),
            pltpu.VMEM((2, 512, HALF), BF16),
            pltpu.VMEM((2, 512, HALF), BF16),
            pltpu.VMEM((512, HALF), F32),
            pltpu.VMEM((2, 512, HALF), BF16),
            pltpu.VMEM((2, NY, ROWS, HALF), BF16),
            pltpu.VMEM((2, 2, 512, HALF), BF16),
            pltpu.VMEM((2, 2, 512, HALF), BF16),
            pltpu.VMEM((512, HALF), F32),
            pltpu.VMEM((2, 256, HALF), F32),
            pltpu.VMEM((2, 2, 256, HALF), BF16),
            pltpu.VMEM((2, 2, 256, HALF), BF16),
            pltpu.VMEM((2, 512, HALF), BF16),
            pltpu.VMEM((2, NZ, ROWS, HALF), BF16),
            pltpu.VMEM((512, HALF), F32),
            pltpu.VMEM((HALF, 2048), F32),
            pltpu.VMEM((8, 16, 512), F32),
            pltpu.VMEM((NX, 2, 8, 512), F32),
            pltpu.VMEM((256, 256), F32),
            pltpu.VMEM((128, 256), F32),
            pltpu.VMEM((128, 256), F32),
            pltpu.VMEM((128, 256), BF16),
            pltpu.VMEM((NY, 16, 256), BF16),
            pltpu.VMEM((NZ, 16, 256), BF16),
            pltpu.VMEM((NX, 16, 256), F32),
            pltpu.VMEM((256, 256), BF16),
            pltpu.VMEM((ROWS, 256), F32),
            pltpu.SemaphoreType.DMA((COPIES,)),
            pltpu.SemaphoreType.DMA((COPIES,)),
        ],
        compiler_params=pltpu.CompilerParams(
            collective_id=0, has_side_effects=True, vmem_limit_bytes=40 * 1024 * 1024
        ),
    )(*(pltpu.with_memory_space_constraint(arg, pltpu.HBM) for arg in args))
    return pl.pallas_call(
        deliver,
        out_shape=tuple(jax.ShapeDtypeStruct(*shape) for shape in shapes),
        in_specs=[vmem] * 3,
        out_specs=(hbm,) * 3,
        scratch_shapes=[pltpu.SemaphoreType.DMA((3,))],
        compiler_params=pltpu.CompilerParams(vmem_limit_bytes=8 * 1024 * 1024),
    )(*(pltpu.with_memory_space_constraint(one, pltpu.VMEM) for one in made))


def solution(mesh):
    in_specs = (
        P(("section", "rep"), None),
        P(),
        P(("section", "rep")),
        P("section", None),
        P(("section", "rep"), None),
    )
    out_specs = (P(("section", "rep"), None), P(("section", "rep"), None), P())
    coef = 4.0 / math.sqrt(128 * 256)
    return jax.shard_map(
        functools.partial(local, coef=coef), mesh=mesh, in_specs=in_specs, out_specs=out_specs,
        check_vma=False,
    )
```

```python
import functools
import math

import jax
import jax.numpy as jnp
from jax import lax
from jax.experimental import pallas as pl
from jax.experimental.pallas import tpu as pltpu
from jax.sharding import PartitionSpec as P


MESH = pl.DeviceIdType.MESH
NZ, NY, NX = 8, 8, 4
ROWS = 64
HALF = 128
MODULUS = 65521
OFFSET = (0, 1, 7, 2, 6, 3, 5, 4)
SLOT = {off: k for k, off in enumerate(OFFSET)}
GROUPS = ((0, 1), (1, 5), (5, 8))
COPIES = 80
BF16 = jnp.bfloat16
F32 = jnp.float32


def fold(v):
    return (v & 0xFFFF) + 15 * (v >> 16)


def reduce_once(v):
    return jnp.where(v >= MODULUS, v - MODULUS, v)


SCALE = 2.0 / MODULUS
WRAP = 1.0 - 0.5 * SCALE


def add_wrapped(u, step):
    total = u + step
    return jnp.where(total >= WRAP, total - 2.0, total)


def kernel(
    coef,
    feats_hbm, weight_hbm, scale_hbm, mask_hbm, cot_hbm,
    layer_out, grad_feats, grad_weight,
    feats, weight, scale_row, mask, cot, load_sems,
    adj, cm, gath, gath_t, masks, csend, crecv, acc, ysend, yrecv,
    near_send, near_recv, keep, keep_near, next_send, next_recv, zsend, zrecv,
    begun, begun_t, starts, steps, part, a1r, half, a2s, a2r, a3r, a4r, wbuf, scale_col,
    send_sems, recv_sems,
):
    sec = lax.axis_index("section")
    x = lax.axis_index("rep")
    c = sec % 2
    y = (sec // 2) % NY
    z = sec // (2 * NY)
    x_one = x + 1 - 2 * (x % 2)
    x_two = 3 - x
    x_opp = (x + 2) % NX

    def device(zz, yy, cc, xx):
        return ((zz * NY + yy) * 2 + cc, xx)

    sibling = device(z, y, 1 - c, x)
    east, west = device(z, y, c, x_one), device(z, y, c, x_two)

    def z_peer(e):
        return device((z + e) % NZ, y, c, x)

    def y_peer(e):
        return device(z, (y + e) % NY, c, x)

    def x_peer(e):
        return device(z, y, c, (x + e) % NX)

    loads = [
        pltpu.make_async_copy(src, dst, load_sems.at[n])
        for n, (src, dst) in enumerate((
            (feats_hbm, feats), (scale_hbm, scale_row), (mask_hbm, mask),
            (weight_hbm, weight), (cot_hbm, cot),
        ))
    ]
    for one in loads:
        one.start()

    barrier = pltpu.get_barrier_semaphore()
    peers = [z_peer(e) for e in range(1, NZ)] + [y_peer(e) for e in range(1, NY)]
    peers += [x_peer(e) for e in range(1, NX)] + [sibling]
    for peer in peers:
        pl.semaphore_signal(barrier, inc=1, device_id=peer, device_id_type=MESH)

    started = []
    numbers = iter(range(COPIES))

    class Batch:
        def __init__(self, view, target):
            number = next(numbers)
            self.send_sem, self.recv_sem = send_sems.at[number], recv_sems.at[number]
            self.whole = self.describe(view, view, target)
            started.append(self.whole)

        def describe(self, src, dst, target):
            return pltpu.make_async_remote_copy(
                src_ref=src, dst_ref=dst, send_sem=self.send_sem, recv_sem=self.recv_sem,
                device_id=target, device_id_type=MESH,
            )

        def start(self, src, dst, target):
            self.describe(src, dst, target).start()

        def wait_recv(self):
            self.whole.wait_recv()

    def copy(src, dst, target):
        one = Batch(dst, target)
        one.start(src, dst, target)
        return one

    col_j = lax.broadcasted_iota(jnp.int32, (16, 512), 1)
    row_i = lax.broadcasted_iota(jnp.int32, (16, 512), 0)
    col_slot = col_j >> 6
    col_off = jnp.where((col_slot & 1) == 1, (col_slot + 1) >> 1, (8 - (col_slot >> 1)) & 7)
    columns_x = (x, x_one, x_two, x_opp)

    def side_core(side):
        return 1 - c if side == 0 else c

    def mask_columns():
        which = lax.broadcasted_iota(jnp.int32, (16, HALF), 0)
        lane = lax.broadcasted_iota(jnp.int32, (16, HALF), 1)
        core_of = jnp.where(which < 8, 1 - c, c)
        tile = ((z * NY + (which & 7)) * 2 + core_of) * 2 + x // 2
        every = masks[...].reshape(64, HALF)
        dims = (((1,), (1,)), ((), ()))
        low = lax.dot_general((tile == lane).astype(F32), every, dims, preferred_element_type=F32)
        high = lax.dot_general(
            (tile == lane + HALF).astype(F32), every, dims, preferred_element_type=F32
        )
        entry = lax.broadcasted_iota(jnp.int32, (64, 512), 0)
        slot = lax.broadcasted_iota(jnp.int32, (64, 512), 1) >> 6
        off = jnp.where((slot & 1) == 1, (slot + 1) >> 1, (8 - (slot >> 1)) & 7)
        same = (entry >> 3) == ((z + off) & 7)
        for n, xx in enumerate(columns_x):
            pick_low = jnp.where(same & ((entry & 7) == xx // 2), 1.0, 0.0).astype(F32)
            pick_high = jnp.where(same & ((entry & 7) == xx // 2 + 2), 1.0, 0.0).astype(F32)
            chosen = jnp.dot(low, pick_low, preferred_element_type=F32) + jnp.dot(
                high, pick_high, preferred_element_type=F32
            )
            cm[:, n * 512:(n + 1) * 512] = jnp.where(chosen > 0.5, coef, 0.0)

    def column_ids(n):
        return ((((z + col_off) & 7) * NY + y) * 2 + c) * 256 + columns_x[n] * ROWS + (col_j & 63)

    def prepare(unit, a, b):
        first = fold(fold(a * b))
        hashed = reduce_once(fold(fold(first * 20011 + (a + b) * 7919)))
        starts[unit] = hashed.astype(F32) * SCALE - 1.0

    def prepare_steps(number, b, stride):
        step = reduce_once(fold(fold(b[0:8] * 20011 + 7919)))
        steps[number, 0] = reduce_once(fold(step * 16)).astype(F32) * SCALE
        steps[number, 1] = reduce_once(fold(step * stride)).astype(F32) * SCALE

    def prepare_block():
        for n in range(NX):
            b = column_ids(n)
            prepare_steps(n, b, 512)
            for side in range(2):
                a = ((z * NY) * 2 + side_core(side)) * 256 + x * ROWS + row_i
                prepare(n * 2 + side, a, b)

    def make_block(n, side):
        lanes = slice(n * 512, (n + 1) * 512)
        step16 = jnp.concatenate([steps[n, 0]] * 2, axis=0)
        leap = jnp.concatenate([steps[n, 1]] * 2, axis=0)

        def run(yy, u0):
            off = (yy - y + NY) % NY
            late = off // 5
            slot = (off + 7) // 8 * ((1 - late) * (2 * off - 1) + late * (16 - 2 * off))
            coefs = cm[pl.ds(side * 8 + yy, 1), lanes]
            u = u0
            for s in range(4):
                at = pl.multiple_of(side * 512 + slot * ROWS + s * 16, 16)
                adj[pl.ds(at, 16), lanes] = (u * coefs).astype(BF16)
                if s < 3:
                    u = add_wrapped(u, step16)
            return add_wrapped(u0, leap)

        lax.fori_loop(0, 8, run, starts[n * 2 + side])

    for one in loads[:3]:
        one.wait()
    row = scale_row[...].astype(F32)
    pick = lax.broadcasted_iota(jnp.int32, (ROWS, ROWS), 0) == lax.broadcasted_iota(
        jnp.int32, (ROWS, ROWS), 1
    )
    column = jnp.sum(jnp.where(pick, jnp.broadcast_to(row, (ROWS, ROWS)), 0.0), axis=1, keepdims=True)
    scale_col[...] = jnp.broadcast_to(column, (ROWS, 256))
    scaled = (scale_col[...] * feats[...].astype(F32)).astype(BF16)
    gath[0, 0, 0:ROWS] = scaled[:, :HALF]
    gath_t[0, 0, 0:ROWS] = scaled[:, HALF:]
    masks[z] = jnp.zeros((8, HALF), F32)
    masks[z, 0:2, :] = mask[:, 0:HALF].astype(F32)
    masks[z, 2:4, :] = mask[:, HALF:].astype(F32)

    pl.semaphore_wait(barrier, len(peers))

    def start_pass(p):
        own = gath.at[p, 0, pl.ds(0, ROWS)]
        own_t = gath_t.at[p, 0, pl.ds(0, ROWS)]
        state = {"z": {}, "one": {}, "two": {}, "opp": [], "y_t": {}, "core_t": []}
        for g, (lo, hi) in enumerate(GROUPS[1:], 1):
            state["z"][g] = Batch(gath.at[p, 0, pl.ds(lo * ROWS, (hi - lo) * ROWS)], z_peer(1))
        state["y_t"] = Batch(gath_t.at[p, 0, pl.ds(ROWS, (NY - 1) * ROWS)], y_peer(1))
        for k in (7, 6, 5, 4, 3, 2, 1):
            e = (NY - OFFSET[k]) % NY
            state["y_t"].start(own_t, gath_t.at[p, 0, pl.ds(k * ROWS, ROWS)], y_peer(e))
        for k in range(1, NZ):
            e = (NZ - OFFSET[k]) % NZ
            g = 1 if k < GROUPS[1][1] else 2
            state["z"][g].start(own, gath.at[p, 0, pl.ds(k * ROWS, ROWS)], z_peer(e))
            if k == 4:
                forward(p, 0, state)
        return state

    def forward_t(p, state):
        state["y_t"].wait_recv()
        state["core_t"].append(copy(gath_t.at[p, 0], gath_t.at[p, 1], sibling))

    def forward(p, g, state):
        lo, hi = GROUPS[g]
        if g:
            state["z"][g].wait_recv()
        run = pl.ds(lo * ROWS, (hi - lo) * ROWS)
        state["one"][g] = copy(gath.at[p, 0, run], gath.at[p, 1, run], east)
        state["two"][g] = copy(gath.at[p, 0, run], gath.at[p, 2, run], west)

    def relay(p, g, state):
        lo, hi = GROUPS[g]
        size = (hi - lo) * ROWS // 2
        run = pl.ds(lo * ROWS, size)
        state["two"][g].wait_recv()
        state["opp"].append(copy(gath.at[p, 2, run], gath.at[p, 3, run], east))
        run = pl.ds(lo * ROWS + size, size)
        state["one"][g].wait_recv()
        state["opp"].append(copy(gath.at[p, 1, run], gath.at[p, 3, run], west))

    def finish_gather(state):
        for one in state["opp"]:
            one.wait_recv()

    def early(p):
        right = gath[p, 0:3].reshape(3 * NZ * ROWS, HALF)
        begun[...] = jnp.dot(adj[0:512, 0:1536], right, preferred_element_type=F32)

    def sums_first(p, state):
        rest = jnp.dot(adj[0:512, 1536:2048], gath[p, 3], preferred_element_type=F32)
        csend[p] = (begun[...] + rest).astype(BF16)
        state["core"] = copy(csend.at[p], crecv.at[p], sibling)

    def product(p):
        right = gath[p].reshape(NX * NZ * ROWS, HALF)
        acc[...] = jnp.dot(adj[512:1024, :], right, preferred_element_type=F32)

    def sums_second(p, state):
        state["core"].wait_recv()
        total = acc[...] + crecv[p].astype(F32)
        acc[...] = total
        ysend[p] = total.astype(BF16)
        state["y"] = Batch(yrecv.at[p, pl.ds(1, NY - 1)], y_peer(1))
        for e in (4, 3, 5, 2, 6, 1, 7):
            run = pl.ds(SLOT[e] * ROWS, ROWS)
            state["y"].start(ysend.at[p, run], yrecv.at[p, e], y_peer(e))

    def sums_last(p, state):
        total = acc[0:ROWS]
        state["y"].wait_recv()
        for e in range(1, NY):
            total = total + yrecv[p, e].astype(F32)
        return total

    def early_t(p):
        for n in range(NX):
            lanes = slice(n * 512, (n + 1) * 512)
            begun_t[:, lanes] = lax.dot_general(
                gath_t[p, 0], adj[512:1024, lanes], (((0,), (0,)), ((), ())),
                preferred_element_type=F32,
            )

    def product_t(p, lo, hi):
        rest = lax.dot_general(
            gath_t[p, 1], adj[0:512, lo:hi], (((0,), (0,)), ((), ())), preferred_element_type=F32
        )
        return (begun_t[:, lo:hi] + rest).T

    def near_first(p, state):
        for one in state["core_t"]:
            one.wait_recv()
        opposite = product_t(p, 1536, 2048)
        near_send[p, 0, 256:512] = opposite[:256].astype(BF16)
        near_send[p, 1, 256:512] = opposite[256:].astype(BF16)
        far, close = pl.ds(256, 256), pl.ds(0, 256)
        state["far_e"] = copy(near_send.at[p, 0, far], near_recv.at[p, 0, far], east)
        state["far_w"] = copy(near_send.at[p, 1, far], near_recv.at[p, 1, far], west)
        near_send[p, 0, 0:256] = product_t(p, 512, 768).astype(BF16)
        state["near_e"] = copy(near_send.at[p, 0, close], near_recv.at[p, 0, close], east)
        near_send[p, 1, 0:256] = product_t(p, 1280, 1536).astype(BF16)
        state["near_w"] = copy(near_send.at[p, 1, close], near_recv.at[p, 1, close], west)

    def near_second(p):
        keep_near[0] = product_t(p, 1024, 1280)
        keep_near[1] = product_t(p, 768, 1024)

    def next_first(p, state):
        state["far_e"].wait_recv()
        next_send[p, 0] = (keep_near[0] + near_recv[p, 0, 256:512].astype(F32)).astype(BF16)
        state["next_w"] = copy(next_send.at[p, 0], next_recv.at[p, 0], west)
        state["far_w"].wait_recv()
        next_send[p, 1] = (keep_near[1] + near_recv[p, 1, 256:512].astype(F32)).astype(BF16)
        state["next_e"] = copy(next_send.at[p, 1], next_recv.at[p, 1], east)

    def next_own(p, state):
        value = product_t(p, 0, 512)
        state["near_e"].wait_recv()
        state["near_w"].wait_recv()
        keep[0:256] = value[:256] + near_recv[p, 0, 0:256].astype(F32)
        keep[256:512] = value[256:] + near_recv[p, 1, 0:256].astype(F32)

    def next_second(p, state):
        state["z_t"] = Batch(zrecv.at[p, pl.ds(1, NZ - 1)], z_peer(1))
        for part_at, arrival, offsets in ((1, "next_e", (4, 3, 5, 6)), (0, "next_w", (2, 1, 7))):
            state[arrival].wait_recv()
            rows = slice(part_at * 256, (part_at + 1) * 256)
            total = keep[rows] + next_recv[p, part_at].astype(F32)
            zsend[p, rows] = total.astype(BF16)
            for e in offsets:
                run = pl.ds(SLOT[e] * ROWS, ROWS)
                state["z_t"].start(zsend.at[p, run], zrecv.at[p, e], z_peer(e))
        keep[0:ROWS] = total[0:ROWS]

    def sums_last_t(p, state):
        total = keep[0:ROWS]
        state["z_t"].wait_recv()
        for e in range(1, NZ):
            total = total + zrecv[p, e].astype(F32)
        return total

    mask_copies = Batch(masks.at[pl.ds(0, NZ - 1)], z_peer(1))
    for e in range(1, NZ):
        mask_copies.start(masks.at[z], masks.at[z], z_peer(e))
    state = start_pass(0)
    prepare_block()
    mask_copies.wait_recv()
    mask_columns()
    make_block(3, 1)
    relay(0, 0, state)
    make_block(1, 1)
    forward(0, 1, state)
    make_block(2, 1)
    make_block(0, 1)
    forward_t(0, state)
    forward(0, 2, state)
    relay(0, 1, state)
    make_block(3, 0)
    early_t(0)
    make_block(1, 0)
    make_block(2, 0)
    near_first(0, state)
    relay(0, 2, state)
    near_second(0)
    make_block(0, 0)
    early(0)
    next_first(0, state)
    finish_gather(state)
    sums_first(0, state)
    next_own(0, state)
    product(0)
    next_second(0, state)
    sums_second(0, state)
    sums = jnp.concatenate([sums_last(0, state), sums_last_t(0, state)], axis=1)

    for one in loads[3:]:
        one.wait()
    sums_high = sums.astype(BF16)
    sums_low = (sums - sums_high.astype(F32)).astype(BF16)
    scale = scale_col[...]
    presum = scale * (
        jnp.dot(sums_high, weight[...], preferred_element_type=F32)
        + jnp.dot(sums_low, weight[...], preferred_element_type=F32)
    )
    sigma = jax.nn.sigmoid(presum)
    layer_out[...] = (presum * sigma).astype(BF16)
    deriv = sigma * (1.0 + presum * (1.0 - sigma))
    error = (scale * cot[...].astype(F32) * deriv).astype(BF16)
    gath[1, 0, 0:ROWS] = error[:, :HALF]
    gath_t[1, 0, 0:ROWS] = error[:, HALF:]

    earlier = list(started)

    state = start_pass(1)
    dims = (((0,), (0,)), ((), ()))
    part[...] = lax.dot_general(
        sums_high, error, dims, preferred_element_type=F32
    ) + lax.dot_general(sums_low, error, dims, preferred_element_type=F32)
    theirs = pl.multiple_of((1 - c) * 128, 128)
    mine = pl.multiple_of(c * 128, 128)
    first = copy(part.at[pl.ds(theirs, 128)], a1r, sibling)
    for one in earlier:
        one.wait_send()
    relay(1, 0, state)
    forward(1, 1, state)

    first.wait_recv()
    half[...] = part[pl.ds(mine, 128), :] + a1r[...]
    a2s[...] = half[...].astype(BF16)
    second = Batch(a2r.at[pl.ds(1, NY - 1)], y_peer(1))
    for e in range(1, NY):
        at = pl.multiple_of(((y + e) % NY) * 16, 16)
        second.start(a2s.at[pl.ds(at, 16)], a2r.at[e], y_peer(e))

    forward_t(1, state)
    forward(1, 2, state)
    relay(1, 1, state)
    early_t(1)
    near_first(1, state)

    piece = half[pl.ds(pl.multiple_of(y * 16, 16), 16), :]
    second.wait_recv()
    for e in range(1, NY):
        piece = piece + a2r[e].astype(F32)
    a3r[z] = piece.astype(BF16)
    third = Batch(a3r.at[pl.ds(0, NZ - 1)], z_peer(1))
    for e in range(1, NZ):
        third.start(a3r.at[z], a3r.at[z], z_peer(e))

    relay(1, 2, state)
    near_second(1)
    early(1)
    next_first(1, state)
    finish_gather(state)
    sums_first(1, state)

    third.wait_recv()
    piece = a3r[0].astype(F32)
    for n in range(1, NZ):
        piece = piece + a3r[n].astype(F32)
    a4r[x] = piece
    fourth = Batch(a4r.at[pl.ds(0, NX - 1)], x_peer(1))
    for e in range(1, NX):
        fourth.start(a4r.at[x], a4r.at[x], x_peer(e))

    next_own(1, state)
    product(1)
    next_second(1, state)
    sums_second(1, state)

    fourth.wait_recv()
    piece = (a4r[0] + a4r[1]) + (a4r[2] + a4r[3])
    at = pl.multiple_of(c * 128 + y * 16, 16)
    wbuf[pl.ds(at, 16), :] = piece.astype(BF16)
    fifth = Batch(wbuf.at[pl.ds(0, 16 * (NY - 1))], y_peer(1))
    for e in range(1, NY):
        fifth.start(wbuf.at[pl.ds(at, 16)], wbuf.at[pl.ds(at, 16)], y_peer(e))
    fifth.wait_recv()
    sixth = copy(wbuf.at[pl.ds(mine, 128)], wbuf.at[pl.ds(mine, 128)], sibling)
    back = jnp.concatenate([sums_last(1, state), sums_last_t(1, state)], axis=1)
    vgrad = (scale * back).astype(BF16)
    grad_feats[...] = lax.dot_general(
        vgrad, weight[...], (((1,), (1,)), ((), ())), preferred_element_type=F32
    ).astype(BF16)
    sixth.wait_recv()
    grad_weight[...] = wbuf[...].astype(F32)
    for one in started[len(earlier):]:
        one.wait_send()


def deliver(*refs):
    sems = refs[-1]
    copies = [pltpu.make_async_copy(refs[n], refs[n + 3], sems.at[n]) for n in range(3)]
    for one in copies:
        one.start()
    for one in copies:
        one.wait()


def local(node_feats, weight, node_scale, tile_mask, cotangent, coef):
    hidden = weight.shape[0]
    hbm = pl.BlockSpec(memory_space=pltpu.HBM)
    vmem = pl.BlockSpec(memory_space=pltpu.VMEM)
    shapes = (((ROWS, hidden), BF16), ((ROWS, hidden), BF16), ((hidden, hidden), F32))
    args = (node_feats, weight, node_scale.reshape(1, ROWS), tile_mask, cotangent)
    made = pl.pallas_call(
        functools.partial(kernel, coef),
        out_shape=tuple(pltpu.VMEM(*shape) for shape in shapes),
        in_specs=[hbm] * 5,
        out_specs=(vmem,) * 3,
        scratch_shapes=[
            pltpu.VMEM((ROWS, hidden), BF16),
            pltpu.VMEM((hidden, hidden), BF16),
            pltpu.VMEM((1, ROWS), BF16),
            pltpu.VMEM(tile_mask.shape, jnp.int32),
            pltpu.VMEM((ROWS, hidden), BF16),
            pltpu.SemaphoreType.DMA((5,)),
            pltpu.VMEM((1024, 2048), BF16),
            pltpu.VMEM((16, 2048), F32),
            pltpu.VMEM((2, NX, NZ * ROWS, HALF), BF16),
            pltpu.VMEM((2, 2, NY * ROWS, HALF), BF16),
            pltpu.VMEM((NZ, 8, HALF), F32),
            pltpu.VMEM((2, 512, HALF), BF16),
            pltpu.VMEM((2, 512, HALF), BF16),
            pltpu.VMEM((512, HALF), F32),
            pltpu.VMEM((2, 512, HALF), BF16),
            pltpu.VMEM((2, NY, ROWS, HALF), BF16),
            pltpu.VMEM((2, 2, 512, HALF), BF16),
            pltpu.VMEM((2, 2, 512, HALF), BF16),
            pltpu.VMEM((512, HALF), F32),
            pltpu.VMEM((2, 256, HALF), F32),
            pltpu.VMEM((2, 2, 256, HALF), BF16),
            pltpu.VMEM((2, 2, 256, HALF), BF16),
            pltpu.VMEM((2, 512, HALF), BF16),
            pltpu.VMEM((2, NZ, ROWS, HALF), BF16),
            pltpu.VMEM((512, HALF), F32),
            pltpu.VMEM((HALF, 2048), F32),
            pltpu.VMEM((8, 16, 512), F32),
            pltpu.VMEM((NX, 2, 8, 512), F32),
            pltpu.VMEM((256, 256), F32),
            pltpu.VMEM((128, 256), F32),
            pltpu.VMEM((128, 256), F32),
            pltpu.VMEM((128, 256), BF16),
            pltpu.VMEM((NY, 16, 256), BF16),
            pltpu.VMEM((NZ, 16, 256), BF16),
            pltpu.VMEM((NX, 16, 256), F32),
            pltpu.VMEM((256, 256), BF16),
            pltpu.VMEM((ROWS, 256), F32),
            pltpu.SemaphoreType.DMA((COPIES,)),
            pltpu.SemaphoreType.DMA((COPIES,)),
        ],
        compiler_params=pltpu.CompilerParams(
            collective_id=0, has_side_effects=True, vmem_limit_bytes=40 * 1024 * 1024
        ),
    )(*(pltpu.with_memory_space_constraint(arg, pltpu.HBM) for arg in args))
    return pl.pallas_call(
        deliver,
        out_shape=tuple(jax.ShapeDtypeStruct(*shape) for shape in shapes),
        in_specs=[vmem] * 3,
        out_specs=(hbm,) * 3,
        scratch_shapes=[pltpu.SemaphoreType.DMA((3,))],
        compiler_params=pltpu.CompilerParams(vmem_limit_bytes=8 * 1024 * 1024),
    )(*(pltpu.with_memory_space_constraint(one, pltpu.VMEM) for one in made))


def solution(mesh):
    in_specs = (
        P(("section", "rep"), None),
        P(),
        P(("section", "rep")),
        P("section", None),
        P(("section", "rep"), None),
    )
    out_specs = (P(("section", "rep"), None), P(("section", "rep"), None), P())
    coef = 4.0 / math.sqrt(128 * 256)
    return jax.shard_map(
        functools.partial(local, coef=coef), mesh=mesh, in_specs=in_specs, out_specs=out_specs,
        check_vma=False,
    )
```
